32 devices in a mesh: seq: 16 (over z, y, core), fsdp: 2 (over x).
Axes of the slice: x: 2, y: 2, z: 4, core: 2. Of those that a mesh axis runs over, the one named last changes fastest.
Arguments:
- tokens: bfloat16 [2, 2048, 2048], P('fsdp', 'seq'), may hold values from -6 to 6
- segment_ids: int32 [2, 2048], P('fsdp'), may hold values from 0 to 3, as said below
- routes: int32 [2, 2048, 6], P('fsdp', 'seq'), may hold values from 0 to 15, all different within a row; in each aligned block of 128 rows (0 to 127, 128 to 255, ..., all dimensions but the last counted through in order) at most 96 rows name the same one
- gate_weights: float32 [2, 2048, 6], P('fsdp', 'seq'), may hold values from 0.2 to 0.5
- out_grad: bfloat16 [2, 2048, 2048], P('fsdp', 'seq'), may hold values from -6 to 6
- attn_gain: float32 [2048], P('fsdp'), may hold values from 0.5 to 1.5
- q_weight: float32 [2048, 3072], P('fsdp'), may hold values from -0.1875 to 0.1875
- latent_weight: float32 [2048, 576], P('fsdp'), may hold values from -0.125 to 0.125
- latent_gain: float32 [512], P('fsdp'), may hold values from 0.5 to 1.5
- kv_weight: float32 [512, 4096], P('fsdp'), may hold values from -0.25 to 0.25
- out_weight: float32 [2048, 2048], P('fsdp'), may hold values from -2 to 2
- ffn_gain: float32 [2048], P('fsdp'), may hold values from 0.5 to 1.5
- shared_gate: float32 [2048, 2816], P('fsdp'), may hold values from -0.125 to 0.125
- shared_up: float32 [2048, 2816], P('fsdp'), may hold values from -0.125 to 0.125
- shared_down: float32 [2816, 2048], P('fsdp'), may hold values from -0.109375 to 0.109375
- expert_gate: float32 [16, 2048, 1408], P('seq', 'fsdp'), may hold values from -0.125 to 0.125
- expert_up: float32 [16, 2048, 1408], P('seq', 'fsdp'), may hold values from -0.125 to 0.125
- expert_down: float32 [16, 1408, 2048], P('seq', 'fsdp'), may hold values from -0.15625 to 0.15625
Outputs:
- output: bfloat16 [2, 2048, 2048], P('fsdp', 'seq')
- input_grad: float32 [2, 2048, 2048], P('fsdp', 'seq')
- attn_gain_grad: float32 [2048], P('fsdp')
- q_weight_grad: float32 [2048, 3072], P('fsdp')
- latent_weight_grad: float32 [2048, 576], P('fsdp')
- latent_gain_grad: float32 [512], P('fsdp')
- kv_weight_grad: float32 [512, 4096], P('fsdp')
- out_weight_grad: float32 [2048, 2048], P('fsdp')
- ffn_gain_grad: float32 [2048], P('fsdp')
- shared_gate_grad: float32 [2048, 2816], P('fsdp')
- shared_up_grad: float32 [2048, 2816], P('fsdp')
- shared_down_grad: float32 [2816, 2048], P('fsdp')
- expert_gate_grad: float32 [16, 2048, 1408], P('seq', 'fsdp')
- expert_up_grad: float32 [16, 2048, 1408], P('seq', 'fsdp')
- expert_down_grad: float32 [16, 1408, 2048], P('seq', 'fsdp')
The draws below stay inside these ranges and needn't reach their ends.
Inputs may be any that keep to these rules, and one draw needn't show every extreme that they name: `routes`: each token names 6 different experts; in each aligned block of 128 positions of a sequence, no expert is named by more than 96 tokens, a bound that some block reaches. `segment_ids`: each sequence holds four documents, ids never falling along it; the k-th boundary lies within 256 positions of k * 512.
All inputs are finite; a program needn't handle non-finite values.
Results may differ from the reference program's by a relative error of at most 0.024.
The reference program's roundings to bfloat16 on the way count: a program that leaves them out, or rounds other values in their place, can miss the bound.
Values may be sent and summed in bfloat16 or wider, within the bound.
A program may use at most 448 MiB of HBM per device.

```python
import math
import jax
import jax.numpy as jnp
import numpy as np
from jax import lax

MODEL_DIMENSION = 2048
HEADS = 16
NOPE = 128
ROPE = 64
KV_RANK = 512
V_DIM = 128
FF = 1408
SH_FF = 2816
TOP = 6
SEQUENCE_TOKENS = 2048
SEQS = 2
BLOCK = 128
EXPERTS = 16
MOST = 96


def draw_segment_ids(key, part):
    jitter = jax.random.randint(key, (SEQS, 3), -(SEQUENCE_TOKENS // 8), SEQUENCE_TOKENS // 8, dtype=jnp.int32)
    quarters = jnp.arange(1, 4, dtype=jnp.int32) * (SEQUENCE_TOKENS // 4)
    cuts = quarters[None, :] + jitter
    places = jnp.arange(SEQUENCE_TOKENS, dtype=jnp.int32)
    return jnp.sum((places[None, :, None] >= cuts[:, None, :]).astype(jnp.int32), axis=-1).astype(jnp.int32)


def level_of(key, dims, cuts, smallest, top_value):
    factor_of = 1.0
    for axis_at, parts in cuts:
        steps = jax.random.uniform(jax.random.fold_in(jax.random.fold_in(key, 6), axis_at), (parts,), jnp.float32, smallest / len(cuts), top_value / len(cuts))
        factor_of = factor_of * jnp.repeat(jnp.exp(steps), dims[axis_at] // parts).reshape((-1,) + (1,) * (len(dims) - 1 - axis_at))
    return factor_of


def assign_block(stream_key, own, number, rows, number_of, top, reach, lean):
    ranking = jax.random.permutation(stream_key, number_of)
    heavy_load, ordinary = portions_of(number_of, rows * top, reach, lean, True), portions_of(number_of, rows * top, reach, lean, False)
    places = jnp.arange(number_of)

    def named(lengths, turn):
        used = int((lengths > 0).sum())
        fixed = max(1, used // 4)
        shifted = fixed + (places - fixed + turn * (used - fixed)) % max(1, number_of - fixed)
        return jnp.zeros((number_of,), jnp.int32).at[ranking[jnp.where(places < fixed, places, shifted)]].set(jnp.asarray(lengths, jnp.int32))

    lengths = jnp.where(number % 4 == 0, named(heavy_load, number // 4), named(ordinary, number - number // 4 - 1))
    mixed = jax.random.permutation(jax.random.fold_in(own, 3), number_of)
    source_of, receiver = mixed[0:number_of // 2 * 2:2], mixed[1:number_of // 2 * 2:2]
    margin = jnp.minimum(lengths[source_of] - 1, reach - lengths[receiver]) // 2
    margin = jnp.where((source_of == ranking[0]) | (receiver == ranking[0]) | (lengths[receiver] == 0), 0, jnp.maximum(margin, 0))
    shifted = jax.random.randint(jax.random.fold_in(own, 4), (number_of // 2,), 0, 1 << 20) % (margin + 1)
    lengths = lengths.at[source_of].add(-shifted).at[receiver].add(shifted)
    labels = jnp.searchsorted(jnp.cumsum(lengths), jnp.arange(rows * top), side="right").astype(jnp.int32)
    grid = labels.reshape(top, rows).T
    grid = grid[jax.random.permutation(jax.random.fold_in(own, 1), rows)]
    turn = jax.random.randint(jax.random.fold_in(own, 2), (rows, 1), 0, top)
    return jnp.take_along_axis(grid, (jnp.arange(top)[None, :] + turn) % top, axis=1)


def portions_of(amount, total, reach, skew, full):
    weights = [(1 << 20) // math.isqrt(standing ** skew) + 1 for standing in range(1, amount + 1)]
    largest = reach if full else min(reach, max(-(-total // amount), total * weights[0] // sum(weights)))
    least = 1 if total - largest >= amount - 1 else 0
    given, spare = [largest] + [least] * (amount - 1), total - largest - least * (amount - 1)
    while spare > 0:
        free = [i for i in range(1, amount) if given[i] < largest] or [i for i in range(1, amount) if given[i] < reach]
        whole, remaining = sum([weights[i] for i in free]), spare
        for i in free:
            addition = min(reach - given[i], max(1, remaining * weights[i] // whole), spare)
            given[i] = given[i] + addition
            spare = spare - addition
    return np.array(given)


def normal_values(own_key, shape, width, limit, shards=(), held_as=jnp.bfloat16):
    entries = jax.random.normal(own_key, shape, jnp.float32) * width
    if len(shards) > 0:
        entries = level_of(own_key, shape, shards, -0.22, 0.18) * entries
    return jnp.clip(entries, min=-limit, max=limit).astype(held_as)


def setup_inputs(seed: int = 0) -> dict:
    streams_of = jax.random.split(jax.random.key(seed), 19)
    tokens = normal_values(streams_of[0], (SEQS, SEQUENCE_TOKENS, MODEL_DIMENSION), 1.0, 6.0, ((0, 2), (1, 16)))
    segment_ids = draw_segment_ids(jax.random.fold_in(streams_of[18], 71), 0)
    routes_keys = jax.random.split(jax.random.fold_in(streams_of[2], 1), SEQS * SEQUENCE_TOKENS // BLOCK)
    routes_turns = jax.random.permutation(jax.random.fold_in(streams_of[2], 3), SEQS * SEQUENCE_TOKENS // BLOCK)
    routes = jax.vmap(lambda own, number: assign_block(jax.random.fold_in(streams_of[2], 2), own, number, BLOCK, EXPERTS, TOP, MOST, 1))(routes_keys, routes_turns).reshape((SEQS, SEQUENCE_TOKENS, TOP))
    gate_weights = jnp.clip(0.2 + 0.3 * jax.random.uniform(streams_of[3], (SEQS, SEQUENCE_TOKENS, TOP), jnp.float32) ** level_of(streams_of[3], (SEQS, SEQUENCE_TOKENS, TOP), ((0, 2), (1, 16)), -0.2, 0.2), 0.2, 0.5)
    out_grad = normal_values(streams_of[4], (SEQS, SEQUENCE_TOKENS, MODEL_DIMENSION), 1.0, 6.0, ((0, 2), (1, 16)))
    attn_gain = jnp.clip(1.0 + 0.1 * jax.random.normal(streams_of[5], (MODEL_DIMENSION,), jnp.float32), 0.5, 1.5)
    q_weight = normal_values(streams_of[6], (MODEL_DIMENSION, HEADS * (NOPE + ROPE)), (MODEL_DIMENSION // 2) ** -0.5, 0.1875, ((0, 2),), jnp.float32)
    latent_weight = normal_values(streams_of[7], (MODEL_DIMENSION, KV_RANK + ROPE), MODEL_DIMENSION ** -0.5, 0.125, ((0, 2),), jnp.float32)
    latent_gain = jnp.clip(1.0 + 0.1 * jax.random.normal(streams_of[8], (KV_RANK,), jnp.float32), 0.5, 1.5)
    kv_weight = normal_values(streams_of[9], (KV_RANK, HEADS * (NOPE + V_DIM)), KV_RANK ** -0.5, 0.25, ((0, 2),), jnp.float32)
    out_weight = normal_values(streams_of[10], (HEADS * V_DIM, MODEL_DIMENSION), (max(8, HEADS * V_DIM // 256)) ** -0.5, 2.0, ((0, 2),), jnp.float32)
    ffn_gain = jnp.clip(1.0 + 0.1 * jax.random.normal(streams_of[11], (MODEL_DIMENSION,), jnp.float32), 0.5, 1.5)
    shared_gate = normal_values(streams_of[12], (MODEL_DIMENSION, SH_FF), MODEL_DIMENSION ** -0.5, 0.125, ((0, 2),), jnp.float32)
    shared_up = normal_values(streams_of[13], (MODEL_DIMENSION, SH_FF), MODEL_DIMENSION ** -0.5, 0.125, ((0, 2),), jnp.float32)
    shared_down = normal_values(streams_of[14], (SH_FF, MODEL_DIMENSION), SH_FF ** -0.5, 0.109375, ((0, 2),), jnp.float32)
    expert_gate = normal_values(streams_of[15], (EXPERTS, MODEL_DIMENSION, FF), MODEL_DIMENSION ** -0.5, 0.125, ((0, 16), (1, 2)), jnp.float32)
    expert_up = normal_values(streams_of[16], (EXPERTS, MODEL_DIMENSION, FF), MODEL_DIMENSION ** -0.5, 0.125, ((0, 16), (1, 2)), jnp.float32)
    expert_down = normal_values(streams_of[17], (EXPERTS, FF, MODEL_DIMENSION), FF ** -0.5, 0.15625, ((0, 16), (1, 2)), jnp.float32)
    return {"tokens": tokens, "segment_ids": segment_ids, "routes": routes, "gate_weights": gate_weights, "out_grad": out_grad, "attn_gain": attn_gain, "q_weight": q_weight, "latent_weight": latent_weight, "latent_gain": latent_gain, "kv_weight": kv_weight, "out_weight": out_weight, "ffn_gain": ffn_gain, "shared_gate": shared_gate, "shared_up": shared_up, "shared_down": shared_down, "expert_gate": expert_gate, "expert_up": expert_up, "expert_down": expert_down}


@jax.custom_vjp
def reduced_precision(v):
    return lax.optimization_barrier(v.astype(jnp.bfloat16)).astype(jnp.float32)

@jax.custom_vjp
def reduced_backward(v):
    return v

def low_keep(v):
    return (reduced_precision(v), None)

def low_pass(kept, grad):
    return (grad,)

def back_keep(v):
    return (v, None)

def back_low(kept, grad):
    return (reduced_precision(grad),)
reduced_precision.defvjp(low_keep, low_pass)
reduced_backward.defvjp(back_keep, back_low)
EPS = 1e-06
NEG = -1e+30
THETA = 10000.0

def multiply_product(left_matrix, right_matrix):
    return jnp.dot(left_matrix, right_matrix, precision=lax.Precision.HIGHEST, preferred_element_type=jnp.float32)

def rms_scale(values):
    return lax.rsqrt(lax.optimization_barrier(jnp.mean(values * values, axis=-1, keepdims=True)) + EPS)

def rope_tables():
    places = jnp.arange(SEQUENCE_TOKENS, dtype=jnp.float32)
    exponent = jnp.arange(ROPE // 2, dtype=jnp.float32) * (-2.0 / ROPE)
    frequency = jnp.power(THETA, exponent)
    angles = places[:, None] * frequency[None, :]
    angles = jnp.concatenate([angles, angles], axis=-1)
    return (jnp.cos(angles)[:, None, :], jnp.sin(angles)[:, None, :])

def rotate(values, cosine_table, sine_table):
    half_dims = values.shape[-1] // 2
    turned = jnp.concatenate([-values[..., half_dims:], values[..., :half_dims]], axis=-1)
    return values * cosine_table + turned * sine_table

def attention_row(query_rot, key_rot, value_heads, segments):
    block_rows = min(512, SEQUENCE_TOKENS)
    block_count = SEQUENCE_TOKENS // block_rows
    places = jnp.arange(SEQUENCE_TOKENS, dtype=jnp.int32)
    scale_factor = 1.0 / math.sqrt(NOPE + ROPE)

    def block_fn(block_index):
        offset = block_index * block_rows
        query_block = lax.dynamic_slice_in_dim(query_rot, offset, block_rows, 0)
        query_place = offset + jnp.arange(block_rows, dtype=jnp.int32)
        query_segment = lax.dynamic_slice_in_dim(segments, offset, block_rows, 0)
        raw_scores = reduced_backward(jnp.einsum('qhd,khd->hqk', query_block, key_rot, precision=lax.Precision.HIGHEST))
        scores = raw_scores * scale_factor
        allowed = (places[None, :] <= query_place[:, None]) & (segments[None, :] == query_segment[:, None])
        scores = jnp.where(allowed[None, :, :], scores, NEG)
        row_peak = lax.optimization_barrier(jnp.max(scores, axis=-1, keepdims=True))
        raised = jnp.exp(scores - row_peak)
        layer_weights = reduced_precision(raised / lax.optimization_barrier(jnp.sum(raised, axis=-1, keepdims=True)))
        return jnp.einsum('hqk,khd->qhd', layer_weights, value_heads, precision=lax.Precision.HIGHEST)
    blocks = lax.map(jax.checkpoint(block_fn), jnp.arange(block_count, dtype=jnp.int32))
    return blocks.reshape(SEQUENCE_TOKENS, HEADS, V_DIM)

def layer_row(row_tokens, row_segments, row_routes, row_gates, layer_weights):
    first_norm_gain, query_matrix, latent_down_weight, latent_norm_gain, expand_weight, output_matrix, second_norm_gain, shared_gate_weight, shared_up_weight, shared_down_weight, expert_gate_weight, expert_up_weight, expert_down_weight = layer_weights
    cosine_table, sine_table = rope_tables()
    act_one = reduced_precision(row_tokens * rms_scale(row_tokens) * first_norm_gain)
    q_proj = reduced_backward(reduced_precision(multiply_product(act_one, query_matrix))).reshape(SEQUENCE_TOKENS, HEADS, NOPE + ROPE)
    latent = reduced_backward(multiply_product(act_one, latent_down_weight))
    compressed = latent[:, :KV_RANK]
    key_rope = latent[:, KV_RANK:]
    comp_norm = reduced_precision(compressed * rms_scale(compressed) * latent_norm_gain)
    key_value = reduced_backward(reduced_precision(multiply_product(comp_norm, expand_weight))).reshape(SEQUENCE_TOKENS, HEADS, NOPE + V_DIM)
    head_rope = reduced_backward(jnp.broadcast_to(reduced_precision(key_rope)[:, None, :], (SEQUENCE_TOKENS, HEADS, ROPE)))
    query_rot = reduced_precision(jnp.concatenate([q_proj[..., :NOPE], rotate(q_proj[..., NOPE:], cosine_table, sine_table)], axis=-1))
    key_rot = reduced_precision(jnp.concatenate([key_value[..., :NOPE], rotate(head_rope, cosine_table, sine_table)], axis=-1))
    attended = attention_row(query_rot, key_rot, key_value[..., NOPE:], row_segments)
    attended = reduced_backward(reduced_precision(attended)).reshape(SEQUENCE_TOKENS, HEADS * V_DIM)
    resid = row_tokens + reduced_backward(multiply_product(attended, output_matrix))
    act_two = reduced_precision(resid * rms_scale(resid) * second_norm_gain)
    shared_g = reduced_backward(multiply_product(act_two, shared_gate_weight))
    shared_u = reduced_backward(multiply_product(act_two, shared_up_weight))
    shared_out = multiply_product(reduced_precision(jax.nn.silu(shared_g) * shared_u), shared_down_weight)
    expert_ids = jnp.arange(EXPERTS, dtype=jnp.int32)
    select_experts = lax.optimization_barrier(jnp.sum(row_gates[:, :, None] * (row_routes[:, :, None] == expert_ids[None, None, :]).astype(jnp.float32), axis=1))

    def expert_pass_fn(running, pieces):
        gate_mat, up_matrix, down_matrix, share_col = pieces
        input_entry = reduced_backward(act_two)
        expert_gate_value = reduced_backward(multiply_product(input_entry, gate_mat))
        expert_up_value = reduced_backward(multiply_product(input_entry, up_matrix))
        expert_output_rows = reduced_backward(reduced_precision(multiply_product(reduced_precision(jax.nn.silu(expert_gate_value) * expert_up_value), down_matrix)))
        return (running + share_col[:, None] * expert_output_rows, None)
    routed_tokens, discarded_output = lax.scan(jax.checkpoint(expert_pass_fn), jnp.zeros((SEQUENCE_TOKENS, MODEL_DIMENSION), jnp.float32), (expert_gate_weight, expert_up_weight, expert_down_weight, select_experts.T))
    return resid + shared_out + routed_tokens

def reference(tokens, segment_ids, routes, gate_weights, out_grad, attn_gain, q_weight, latent_weight, latent_gain, kv_weight, out_weight, ffn_gain, shared_gate, shared_up, shared_down, expert_gate, expert_up, expert_down):
    masters = (attn_gain, q_weight, latent_weight, latent_gain, kv_weight, out_weight, ffn_gain, shared_gate, shared_up, shared_down, expert_gate, expert_up, expert_down)

    def forward(layer_in, params):
        layer_weights = tuple((reduced_precision(master) for master in params))

        def row_fn(pieces):
            row_tokens, row_segments, row_routes, row_gates = pieces
            return layer_row(row_tokens, row_segments, row_routes, row_gates, layer_weights)
        return lax.map(row_fn, (layer_in, segment_ids, routes, gate_weights))
    primal, pullback = jax.vjp(forward, tokens.astype(jnp.float32), masters)
    input_grad, grads = pullback(out_grad.astype(jnp.float32))
    return (primal.astype(jnp.bfloat16), input_grad, grads[0], grads[1], grads[2], grads[3], grads[4], grads[5], grads[6], grads[7], grads[8], grads[9], grads[10], grads[11], grads[12])
```

```python
import functools
import math

import jax
import jax.numpy as jnp
import numpy as np
from jax import lax
from jax.experimental import pallas as pl
from jax.experimental.pallas import tpu as pltpu
from jax.sharding import PartitionSpec as P

HEADS = 16
NOPE = 128
ROPE = 64
QD = NOPE + ROPE
KV_RANK = 512
V_DIM = 128
TOP = 6
MOST = 96

EPS = 1e-06
NEG = -1e30
THETA = 10000.0
SCALE = 1.0 / math.sqrt(QD)
MESH = pl.DeviceIdType.MESH
BF = jnp.bfloat16
F32 = jnp.float32
VMEM_LIMIT = 60 * 2**20


def norm_scale(values):
    return lax.rsqrt(jnp.mean(values * values, axis=-1, keepdims=True) + EPS)


def norm_back(values, inverse, gradient):
    return inverse * gradient - values * inverse * inverse * inverse * jnp.mean(
        gradient * values, axis=-1, keepdims=True
    )


def mm(a, b):
    return jnp.dot(a, b, preferred_element_type=F32)


def mm_tn(a, b):
    return lax.dot_general(a, b, (((0,), (0,)), ((), ())), preferred_element_type=F32)


def mm_nt(a, b):
    return lax.dot_general(a, b, (((1,), (1,)), ((), ())), preferred_element_type=F32)


def rope_tables(length):
    places = np.arange(length, dtype=np.float32)
    frequency = np.power(np.float32(THETA), np.arange(ROPE // 2, dtype=np.float32) * np.float32(-2.0 / ROPE))
    angles = places[:, None] * frequency[None, :].astype(np.float32)
    angles = np.concatenate([angles, angles], axis=-1)
    return jnp.asarray(np.cos(angles), F32), jnp.asarray(np.sin(angles), F32)


def ring_place():
    me = lax.axis_index("seq")
    core, chip = me % 2, me // 2
    z, y = chip // 2, chip % 2
    half = lax.axis_size("seq") // 4
    return me, core, jnp.where(y == 0, z, 2 * half - 1 - z), 2 * half


def ring_seq(r, core, n):
    low = r < n // 2
    return (jnp.where(low, r, n - 1 - r) * 2 + jnp.where(low, 0, 1)) * 2 + core


def greet(devices):
    barrier = pltpu.get_barrier_semaphore()
    for device in devices:
        pl.semaphore_signal(barrier, inc=1, device_id={"seq": device}, device_id_type=MESH)
    pl.semaphore_wait(barrier, len(devices))


def remote(src, dst, send, recv, device):
    return pltpu.make_async_remote_copy(src, dst, send, recv, device_id={"seq": device}, device_id_type=MESH)


def gather_kernel(n, pieces, x_ref, o_ref, own_sem, local_sem, send, recv, fsend, frecv):
    me, core, r, _ = ring_place()
    targets = (ring_seq((r + 1) % n, core, n), ring_seq((r + n - 1) % n, core, n))
    sibling = ring_seq(r, 1 - core, n)
    greet((*targets, sibling))
    height = x_ref.shape[0] // (2 * pieces)

    def rows(d, k):
        return pl.ds((d * pieces + k) * height, height)

    def block(t, d):
        return ring_seq((r + (-t if d == 0 else t) + n) % n, core, n)

    def onward(t, d, k):
        at = o_ref.at[block(t, d), rows(d, k)]
        source = x_ref.at[rows(d, k)] if t == 0 else at
        return remote(source, at, send.at[t, d, k], recv.at[t, d, k], targets[d])

    def across(t, d, k):
        at = o_ref.at[block(t, d), rows(d, k)]
        return remote(at, at, fsend.at[t - 1, d, k], frecv.at[t - 1, d, k], sibling)

    local = pltpu.make_async_copy(x_ref, o_ref.at[me], local_sem)
    local.start()
    own = remote(x_ref, o_ref.at[me], own_sem.at[0], own_sem.at[1], sibling)
    for k in range(pieces):
        for d in range(2):
            onward(0, d, k).start()
    own.start()
    for t in range(n - 1):
        for k in range(pieces):
            for d in range(2):
                onward(t, d, k).wait_recv()
                if t < n - 2:
                    onward(t + 1, d, k).start()
                across(t + 1, d, k).start()
    local.wait()
    own.wait()
    for t in range(n - 1):
        for k in range(pieces):
            for d in range(2):
                onward(t, d, k).wait_send()
                across(t + 1, d, k).wait()


def ring_gather(x, collective_id, pieces=2):
    devices = lax.axis_size("seq")
    n = devices // 2
    rows, columns = x.shape
    size = devices * rows * columns * x.dtype.itemsize
    sems = pltpu.SemaphoreType.DMA((n - 1, 2, pieces))
    out = pl.pallas_call(
        functools.partial(gather_kernel, n, pieces),
        out_shape=jax.ShapeDtypeStruct((devices, rows, columns), x.dtype),
        in_specs=[pl.BlockSpec(memory_space=pl.ANY)],
        out_specs=pl.BlockSpec(memory_space=pl.ANY),
        scratch_shapes=[pltpu.SemaphoreType.DMA((2,)), pltpu.SemaphoreType.DMA] + [sems] * 4,
        compiler_params=pltpu.CompilerParams(collective_id=collective_id, has_side_effects=True),
        cost_estimate=pl.CostEstimate(flops=0, bytes_accessed=22 * size, transcendentals=0),
        name="ring_gather",
    )(x)
    return out.reshape(devices * rows, columns)


def scatter_kernel(n, cut, with_weight, *refs):
    if with_weight:
        a_ref, w_ref, o_ref, stage, sibbuf, rbuf, sbuf, send, recv, fsend, frecv = refs
    else:
        a_ref, o_ref, sibbuf, rbuf, sbuf, send, recv, fsend, frecv = refs
    me, core, r, _ = ring_place()
    targets = (ring_seq((r + 1) % n, core, n), ring_seq((r + n - 1) % n, core, n))
    sibling = ring_seq(r, 1 - core, n)
    greet((*targets, sibling))
    height, columns = o_ref.shape
    spans = (pl.ds(0, cut), pl.ds(cut, columns - cut))

    def chip(t, d):
        return (r + (-t - 1 if d == 0 else t + 1) + n) % n

    def part(t, d, c):
        block = ring_seq(chip(t, d), c, n)
        if not with_weight:
            return a_ref[block, :, spans[d]].astype(F32)
        rows = a_ref[pl.ds(block * height, height), :]
        return mm_nt(rows, w_ref[spans[d], :])

    def across(t, d):
        if with_weight:
            source = stage.at[t, :, spans[d]]
        else:
            source = a_ref.at[ring_seq(chip(t, d), 1 - core, n), :, spans[d]]
        return remote(source, sibbuf.at[t, :, spans[d]], fsend.at[t, d], frecv.at[t, d], sibling)

    def onward(t, d):
        return remote(sbuf.at[t, :, spans[d]], rbuf.at[t, :, spans[d]], send.at[t, d], recv.at[t, d], targets[d])

    def give(t, d):
        if with_weight:
            stage[t, :, spans[d]] = part(t, d, 1 - core).astype(BF)
        across(t, d).start()

    if with_weight:
        for d in range(2):
            give(0, d)
    else:
        for t in range(n):
            for d in range(2):
                give(t, d)
    for t in range(n):
        for d in range(2):
            if with_weight and t < n - 1:
                give(t + 1, d)
            value = part(t, d, core)
            across(t, d).wait_recv()
            value = value + sibbuf[t, :, spans[d]].astype(F32)
            if t > 0:
                onward(t - 1, d).wait_recv()
                value = value + rbuf[t - 1, :, spans[d]].astype(F32)
            if t < n - 1:
                sbuf[t, :, spans[d]] = value.astype(BF)
                onward(t, d).start()
            else:
                o_ref[:, spans[d]] = value
    for t in range(n):
        for d in range(2):
            across(t, d).wait_send()
            if t < n - 1:
                onward(t, d).wait_send()


def ring_scatter(a, w, collective_id):
    devices = lax.axis_size("seq")
    n = devices // 2
    rows = a.shape[0] // devices
    columns = a.shape[1] if w is None else w.shape[0]
    cut = columns // 256 * 128
    size = devices * rows * columns * 2
    vmem = pl.BlockSpec(memory_space=pltpu.VMEM)
    operands = (a.reshape(devices, rows, columns),) if w is None else (a, w)
    buffers = [
        pltpu.VMEM((n, rows, columns), BF),
        pltpu.VMEM((n - 1, rows, columns), BF),
        pltpu.VMEM((n - 1, rows, columns), BF),
    ]
    if w is not None:
        buffers = [pltpu.VMEM((n, rows, columns), BF)] + buffers
    return pl.pallas_call(
        functools.partial(scatter_kernel, n, cut, w is not None),
        out_shape=jax.ShapeDtypeStruct((rows, columns), F32),
        in_specs=[vmem] * len(operands),
        out_specs=vmem,
        scratch_shapes=buffers
        + [pltpu.SemaphoreType.DMA((n - 1, 2))] * 2
        + [pltpu.SemaphoreType.DMA((n, 2))] * 2,
        compiler_params=pltpu.CompilerParams(
            collective_id=collective_id, has_side_effects=True, vmem_limit_bytes=VMEM_LIMIT
        ),
        cost_estimate=pl.CostEstimate(flops=0, bytes_accessed=22 * size, transcendentals=0),
        name="ring_scatter",
    )(*operands)


def fsdp_pair(x):
    return lax.ppermute(x, "fsdp", [(0, 1), (1, 0)])


def fsdp_gather(x):
    count = lax.axis_size("fsdp")
    if count != 2:
        return lax.all_gather(x, "fsdp", axis=0, tiled=True)
    other = fsdp_pair(x)
    first = lax.axis_index("fsdp") == 0
    return jnp.concatenate([jnp.where(first, x, other), jnp.where(first, other, x)], axis=0)


def fsdp_pick(x, owner):
    count = lax.axis_size("fsdp")
    if count != 2:
        return lax.dynamic_index_in_dim(lax.all_gather(x, "fsdp", axis=0), owner, 0, keepdims=False)
    return jnp.where(lax.axis_index("fsdp") == owner, x, fsdp_pair(x))


def fsdp_scatter(x):
    count = lax.axis_size("fsdp")
    if count != 2:
        return lax.psum_scatter(x.astype(BF), "fsdp", scatter_dimension=0, tiled=True).astype(F32)
    half = x.shape[0] // 2
    at = lax.axis_index("fsdp")
    kept = lax.dynamic_slice_in_dim(x, at * half, half, 0)
    given = lax.dynamic_slice_in_dim(x, (1 - at) * half, half, 0).astype(BF)
    return kept.astype(F32) + fsdp_pair(given).astype(F32)


def fsdp_sum(x):
    if lax.axis_size("fsdp") != 2:
        return lax.psum(x, "fsdp")
    return x + fsdp_pair(x)


def turn(values, cosine, sine):
    half = values.shape[-1] // 2
    turned = jnp.concatenate([-values[:, half:], values[:, :half]], axis=-1)
    return values * cosine + turned * sine


def turn_back(gradient, cosine, sine):
    half = gradient.shape[-1] // 2
    scaled = gradient * sine
    return gradient * cosine + jnp.concatenate([scaled[:, half:], -scaled[:, :half]], axis=-1)


def spans_of(length):
    step = length // 8
    for i in range(8):
        start = i * step
        yield start, step, max(0, start - (3 * step if i % 2 == 0 else 2 * step))


def allowed_of(seg_col, seg_row, start, step, low):
    width = start + step - low
    query = start + lax.broadcasted_iota(jnp.int32, (step, width), 0)
    key = low + lax.broadcasted_iota(jnp.int32, (step, width), 1)
    return (key <= query) & (seg_col[start : start + step, :] == seg_row[:, low : start + step])


def attend_kernel(q_ref, kv_ref, kr_ref, cos_ref, sin_ref, segc_ref, segr_ref, heads_ref, lse_ref, qh_ref, kh_ref):
    cosine, sine = cos_ref[...], sin_ref[...]
    qh_ref[:, :NOPE] = q_ref[:, :NOPE]
    qh_ref[:, NOPE:] = turn(q_ref[:, NOPE:].astype(F32), cosine, sine).astype(BF)
    kh_ref[:, :NOPE] = kv_ref[:, :NOPE]
    kh_ref[:, NOPE:] = turn(kr_ref[...].astype(F32), cosine, sine).astype(BF)
    for start, step, low in spans_of(q_ref.shape[0]):
        scores = mm_nt(qh_ref[start : start + step, :], kh_ref[low : start + step, :]) * SCALE
        scores = jnp.where(allowed_of(segc_ref, segr_ref, start, step, low), scores, NEG)
        peak = jnp.max(scores, axis=-1, keepdims=True)
        raised = jnp.exp(scores - peak)
        total = jnp.sum(raised, axis=-1, keepdims=True)
        prob = (raised * (1.0 / total)).astype(BF)
        heads_ref[start : start + step, :] = mm(prob, kv_ref[low : start + step, NOPE:]).astype(BF)
        lse_ref[start : start + step, :] = peak + jnp.log(total)


def attend_back_kernel(
    qh_ref, kh_ref, kv_ref, lse_ref, do_ref, cos_ref, sin_ref, segc_ref, segr_ref, dq_ref, dkv_ref, dkr_ref, dk_acc, dv_acc
):
    dk_acc[...] = jnp.zeros_like(dk_acc)
    dv_acc[...] = jnp.zeros_like(dv_acc)
    for start, step, low in spans_of(qh_ref.shape[0]):
        end = start + step
        query = qh_ref[start:end, :]
        grad = do_ref[start:end, :]
        keys = kh_ref[low:end, :]
        scores = mm_nt(query, keys) * SCALE
        allowed = allowed_of(segc_ref, segr_ref, start, step, low)
        prob = jnp.where(allowed, jnp.exp(scores - lse_ref[start:end, :]), 0.0)
        dv_acc[low:end, :] += mm_tn(prob.astype(BF), grad)
        dprob = mm_nt(grad, kv_ref[low:end, NOPE:])
        delta = jnp.sum(prob * dprob, axis=-1, keepdims=True)
        dscore = (prob * (dprob - delta) * SCALE).astype(BF)
        dquery = mm(dscore, keys)
        dq_ref[start:end, :NOPE] = dquery[:, :NOPE].astype(BF)
        dq_ref[start:end, NOPE:] = turn_back(dquery[:, NOPE:], cos_ref[start:end, :], sin_ref[start:end, :]).astype(BF)
        dk_acc[low:end, :] += mm_tn(dscore, query)
    dkv_ref[:, :NOPE] = dk_acc[:, :NOPE].astype(BF)
    dkv_ref[:, NOPE:] = dv_acc[...].astype(BF)
    dkr_ref[...] = turn_back(dk_acc[:, NOPE:], cos_ref[...], sin_ref[...]).astype(BF)


def local_call(kernel, outs, scratch, name, *operands):
    vmem = pl.BlockSpec(memory_space=pltpu.VMEM)
    return pl.pallas_call(
        kernel,
        out_shape=[jax.ShapeDtypeStruct(shape, dtype) for shape, dtype in outs],
        in_specs=[vmem] * len(operands),
        out_specs=[vmem] * len(outs),
        scratch_shapes=scratch,
        compiler_params=pltpu.CompilerParams(vmem_limit_bytes=VMEM_LIMIT),
        cost_estimate=pl.CostEstimate(flops=0, bytes_accessed=70 * 2**20, transcendentals=0),
        name=name,
    )(*operands)


def columns_of(weight, at, width):
    return lax.dynamic_slice_in_dim(weight, at * width, width, 1).astype(BF)


def rows_of(weight, at, height):
    return lax.dynamic_slice_in_dim(weight, at * height, height, 0).astype(BF)


def per_device(
    tokens,
    segment_ids,
    routes,
    gate_weights,
    out_grad,
    attn_gain,
    q_weight,
    latent_weight,
    latent_gain,
    kv_weight,
    out_weight,
    ffn_gain,
    shared_gate,
    shared_up,
    shared_down,
    expert_gate,
    expert_up,
    expert_down,
):
    _, rows, width = tokens.shape
    devices = lax.axis_size("seq")
    at = lax.axis_index("seq")
    parts = lax.axis_size("fsdp")
    part = lax.axis_index("fsdp")
    length = rows * devices
    own_x = tokens[0]
    own_g = out_grad[0]

    gains = jnp.concatenate([attn_gain, ffn_gain, latent_gain]).astype(BF)[None, :]
    gains = fsdp_gather(gains).astype(F32)
    per = attn_gain.shape[0]
    gain_one = gains[:, :per].reshape(1, -1)
    gain_two = gains[:, per : 2 * per].reshape(1, -1)
    gain_lat = gains[:, 2 * per :].reshape(1, -1)
    w_query = fsdp_gather(columns_of(q_weight, at, QD))
    w_latent = fsdp_gather(latent_weight.astype(BF))
    w_expand = fsdp_gather(columns_of(kv_weight, at, NOPE + V_DIM))
    out_rows = out_weight.shape[0]
    head_owner = at * V_DIM // out_rows
    w_out = fsdp_pick(lax.dynamic_slice_in_dim(out_weight, at * V_DIM % out_rows, V_DIM, 0).astype(BF), head_owner)
    hidden = shared_down.shape[0] * parts
    share = shared_down.shape[0] // devices

    def shared_columns(weight):
        pieces = [
            lax.dynamic_slice_in_dim(weight, p * (hidden // parts) + at * share, share, 1) for p in range(parts)
        ]
        return fsdp_gather(jnp.concatenate(pieces, axis=1).astype(BF))

    w_sgate = shared_columns(shared_gate)
    w_sup = shared_columns(shared_up)
    w_sdown = fsdp_gather(rows_of(shared_down, at, share))
    w_egate = fsdp_gather(expert_gate[0].astype(BF))
    w_eup = fsdp_gather(expert_up[0].astype(BF))
    w_edown = fsdp_gather(expert_down[0].astype(BF))

    experts = jnp.arange(devices, dtype=jnp.int32)
    spread = jnp.sum(
        jnp.where(routes[0][:, :, None] == experts[None, None, :], gate_weights[0][:, :, None], 0.0), axis=1
    )
    share_of = lax.all_to_all(spread.T, "seq", 0, 0, tiled=True)

    x_all = ring_gather(own_x, 1).astype(F32)
    r1_all = norm_scale(x_all)
    act_one = (x_all * r1_all * gain_one).astype(BF)
    q_proj = mm(act_one, w_query).astype(BF)
    latent = mm(act_one, w_latent)
    comp_all = latent[:, :KV_RANK]
    r2_all = norm_scale(comp_all)
    cnorm = (comp_all * r2_all * gain_lat).astype(BF)
    kv = mm(cnorm, w_expand).astype(BF)
    key_rope = latent[:, KV_RANK:].astype(BF)
    cosine, sine = rope_tables(length)
    seg_col, seg_row = segment_ids.reshape(length, 1), segment_ids
    heads, lse, qh, kh = local_call(
        attend_kernel,
        [((length, V_DIM), BF), ((length, 1), F32), ((length, QD), BF), ((length, QD), BF)],
        [],
        "attend",
        q_proj,
        kv,
        key_rope,
        cosine,
        sine,
        seg_col,
        seg_row,
    )
    own_xf = own_x.astype(F32)
    x1 = own_xf + ring_scatter(heads, w_out.T, 2)
    r3 = norm_scale(x1)
    act_two = (x1 * r3 * gain_two).astype(BF)
    g_all = ring_gather(own_g, 1)
    act_all = ring_gather(act_two, 1)

    sg, su = mm(act_all, w_sgate), mm(act_all, w_sup)
    sig = jax.nn.sigmoid(sg)
    silu = sg * sig
    sh = (silu * su).astype(BF)
    ys = mm(sh, w_sdown)
    dsh = mm_nt(g_all, w_sdown)
    dsg = (dsh * su * sig * (1.0 + sg * (1.0 - sig))).astype(BF)
    dsu = (dsh * silu).astype(BF)
    grad_sdown = fsdp_scatter(mm_tn(sh, g_all))
    grad_sgate = fsdp_scatter(mm_tn(act_all, dsg))
    grad_sup = fsdp_scatter(mm_tn(act_all, dsu))
    dact_shared = mm_nt(dsg, w_sgate) + mm_nt(dsu, w_sup)

    most = min(MOST, rows)
    named = share_of > 0.0
    rank = jnp.cumsum(named.astype(jnp.int32), axis=1) - 1
    pick = named[:, None, :] & (rank[:, None, :] == jnp.arange(most, dtype=jnp.int32)[None, :, None])
    pick_b = pick.astype(BF)
    share_packed = jnp.sum(jnp.where(pick, share_of[:, None, :], 0.0), axis=-1).reshape(-1, 1)

    def packed(values):
        blocks = values.reshape(devices, rows, width)
        return jnp.einsum("bct,btd->bcd", pick_b, blocks, preferred_element_type=F32).reshape(-1, width)

    def unpacked(values):
        blocks = values.reshape(devices, most, width)
        return jnp.einsum("bct,bcd->btd", pick_b, blocks, preferred_element_type=F32).reshape(-1, width)

    xe = packed(act_all).astype(BF)
    dye = (share_packed * packed(g_all)).astype(BF)
    ge, ue = mm(xe, w_egate), mm(xe, w_eup)
    sig_e = jax.nn.sigmoid(ge)
    silu_e = ge * sig_e
    he = (silu_e * ue).astype(BF)
    ye = mm(he, w_edown).astype(BF)
    dhe = mm_nt(dye, w_edown)
    dge = (dhe * ue * sig_e * (1.0 + ge * (1.0 - sig_e))).astype(BF)
    due = (dhe * silu_e).astype(BF)
    dxe = (mm_nt(dge, w_egate) + mm_nt(due, w_eup)).astype(BF)
    grad_edown = fsdp_scatter(mm_tn(he, dye))
    grad_egate = fsdp_scatter(mm_tn(xe, dge))
    grad_eup = fsdp_scatter(mm_tn(xe, due))
    dact_part = (dact_shared + unpacked(dxe)).astype(BF)
    y_part = (ys + unpacked((share_packed * ye.astype(F32)).astype(BF))).astype(BF)

    dact_two = ring_scatter(dact_part, None, 3)
    own_gf = own_g.astype(F32)
    grad_gain_two = jnp.sum(dact_two * x1 * r3, axis=0)
    dx1 = own_gf + norm_back(x1, r3, dact_two * gain_two)
    dattn_all = ring_gather(dx1.astype(BF), 1)
    y_sum = ring_scatter(y_part, None, 3)
    output = (x1 + y_sum).astype(BF)

    dheads = mm_nt(dattn_all, w_out).astype(BF)
    dqp, dkv, dkr = local_call(
        attend_back_kernel,
        [((length, QD), BF), ((length, NOPE + V_DIM), BF), ((length, ROPE), BF)],
        [pltpu.VMEM((length, QD), F32), pltpu.VMEM((length, V_DIM), F32)],
        "attend_back",
        qh,
        kh,
        kv,
        lse,
        dheads,
        cosine,
        sine,
        seg_col,
        seg_row,
    )
    back = jnp.concatenate([dqp, dkv, dkr], axis=1)
    kv_dim = NOPE + V_DIM
    w_back = jnp.concatenate(
        [
            jnp.pad(w_query, ((0, 0), (0, kv_dim + ROPE))),
            jnp.pad(w_expand, ((0, 0), (QD, ROPE))),
            jnp.pad(jnp.eye(ROPE, dtype=BF), ((0, 128 - ROPE), (QD + kv_dim, 0))),
        ],
        axis=0,
    )
    summed = ring_scatter(back, w_back, 4)
    grad_out = fsdp_sum(mm_tn(heads, dattn_all).astype(BF))
    grad_query = fsdp_scatter(mm_tn(act_one, dqp))
    grad_expand = fsdp_scatter(mm_tn(cnorm, dkv))

    r1 = norm_scale(own_xf)
    own_act = (own_xf * r1 * gain_one).astype(BF)
    own_comp = mm(own_act, w_latent)[:, :KV_RANK]
    r2 = norm_scale(own_comp)
    dcn = summed[:, width : width + KV_RANK]
    grad_gain_lat = jnp.sum(dcn * own_comp * r2, axis=0)
    dcomp = norm_back(own_comp, r2, dcn * gain_lat)
    dlatent = jnp.concatenate([dcomp, summed[:, width + KV_RANK : width + KV_RANK + ROPE]], axis=-1).astype(BF)
    dact_one = summed[:, :width] + mm_nt(dlatent, w_latent)
    grad_gain_one = jnp.sum(dact_one * own_xf * r1, axis=0)
    input_grad = dx1 + norm_back(own_xf, r1, dact_one * gain_one)

    dlatent_all = lax.all_gather(dlatent, "seq", axis=0, tiled=True)
    slab = width // parts // devices
    act_cols = jnp.concatenate(
        [lax.dynamic_slice_in_dim(act_one, p * (width // parts) + at * slab, slab, 1) for p in range(parts)], axis=1
    )
    grad_latent = fsdp_scatter(mm_tn(act_cols, dlatent_all)).astype(BF)

    def over_seq(x):
        return lax.all_gather(x.astype(BF), "seq", axis=0)

    def wide(x):
        stacked = over_seq(x)
        return jnp.swapaxes(stacked, 0, 1).reshape(x.shape[0], -1).astype(F32)

    def shared_wide(x):
        stacked = over_seq(x).reshape(devices, x.shape[0], parts, share)
        return jnp.transpose(stacked, (1, 2, 0, 3)).reshape(x.shape[0], -1).astype(F32)

    out_all = over_seq(grad_out).reshape(devices * V_DIM, width)
    out_grad_own = lax.dynamic_slice_in_dim(out_all, part * out_rows, out_rows, 0).astype(F32)
    small = jnp.concatenate([grad_gain_one, grad_gain_two, grad_gain_lat])
    small = fsdp_sum(jnp.sum(lax.all_gather(small, "seq", axis=0), axis=0))
    gain_rows = width // parts
    own_gains = [
        lax.dynamic_slice_in_dim(small, part * gain_rows, gain_rows),
        lax.dynamic_slice_in_dim(small, width + part * gain_rows, gain_rows),
        lax.dynamic_slice_in_dim(small, 2 * width + part * (KV_RANK // parts), KV_RANK // parts),
    ]
    return (
        output[None],
        input_grad[None],
        own_gains[0],
        wide(grad_query),
        over_seq(grad_latent).reshape(-1, grad_latent.shape[1]).astype(F32),
        own_gains[2],
        wide(grad_expand),
        out_grad_own,
        own_gains[1],
        shared_wide(grad_sgate),
        shared_wide(grad_sup),
        over_seq(grad_sdown).reshape(-1, width).astype(F32),
        grad_egate[None],
        grad_eup[None],
        grad_edown[None],
    )


def solution(mesh):
    token_spec = P("fsdp", "seq", None)
    row_spec = P("fsdp", None)
    gain_spec = P("fsdp")
    expert_spec = P("seq", "fsdp", None)
    dense = (gain_spec, row_spec, row_spec, gain_spec, row_spec, row_spec, gain_spec, row_spec, row_spec, row_spec)
    weights = dense + (expert_spec,) * 3
    return jax.shard_map(
        per_device,
        mesh=mesh,
        in_specs=(token_spec, row_spec, token_spec, token_spec, token_spec) + weights,
        out_specs=(token_spec, token_spec) + weights,
        check_vma=False,
    )
```

```python
import functools
import math

import jax
import jax.numpy as jnp
import numpy as np
from jax import lax
from jax.experimental import pallas as pl
from jax.experimental.pallas import tpu as pltpu
from jax.sharding import PartitionSpec as P

HEADS = 16
NOPE = 128
ROPE = 64
QD = NOPE + ROPE
KV_RANK = 512
V_DIM = 128
TOP = 6
MOST = 96

EPS = 1e-06
NEG = -1e30
THETA = 10000.0
SCALE = 1.0 / math.sqrt(QD)
KV_END = 2 * NOPE + V_DIM
QK_END = KV_END + ROPE
MESH = pl.DeviceIdType.MESH
BF = jnp.bfloat16
F32 = jnp.float32
VMEM_LIMIT = 60 * 2**20
COST = pl.CostEstimate(flops=0, bytes_accessed=2**20, transcendentals=0)


def norm_scale(values):
    return lax.rsqrt(jnp.mean(values * values, axis=-1, keepdims=True) + EPS)


def norm_back(values, inverse, gradient):
    return inverse * gradient - values * inverse * inverse * inverse * jnp.mean(
        gradient * values, axis=-1, keepdims=True
    )


def mm(a, b):
    return jnp.dot(a, b, preferred_element_type=F32)


def mm_tn(a, b):
    return lax.dot_general(a, b, (((0,), (0,)), ((), ())), preferred_element_type=F32)


def mm_nt(a, b):
    return lax.dot_general(a, b, (((1,), (1,)), ((), ())), preferred_element_type=F32)


def rope_tables(length):
    places = np.arange(length, dtype=np.float32)
    frequency = np.power(np.float32(THETA), np.arange(ROPE // 2, dtype=np.float32) * np.float32(-2.0 / ROPE))
    angles = places[:, None] * frequency[None, :].astype(np.float32)
    angles = np.concatenate([angles, angles], axis=-1)
    return jnp.asarray(np.cos(angles), F32), jnp.asarray(np.sin(angles), F32)


def ring_place():
    me = lax.axis_index("seq")
    core, chip = me % 2, me // 2
    z, y = chip // 2, chip % 2
    half = lax.axis_size("seq") // 4
    return me, core, jnp.where(y == 0, z, 2 * half - 1 - z), 2 * half


def ring_seq(r, core, n):
    low = r < n // 2
    return (jnp.where(low, r, n - 1 - r) * 2 + jnp.where(low, 0, 1)) * 2 + core


def greet(devices, across=False):
    barrier = pltpu.get_barrier_semaphore()
    for device in devices:
        pl.semaphore_signal(barrier, inc=1, device_id={"seq": device}, device_id_type=MESH)
    if across:
        other = 1 - lax.axis_index("fsdp")
        pl.semaphore_signal(barrier, inc=1, device_id={"fsdp": other}, device_id_type=MESH)
    pl.semaphore_wait(barrier, len(devices) + across)


def swap_copies(gives, takes, sems):
    other = 1 - lax.axis_index("fsdp")
    return [
        pltpu.make_async_remote_copy(
            give, take, sems.at[i, 0], sems.at[i, 1], device_id={"fsdp": other}, device_id_type=MESH
        )
        for i, (give, take) in enumerate(zip(gives, takes))
    ]


def remote(src, dst, send, recv, device):
    return pltpu.make_async_remote_copy(src, dst, send, recv, device_id={"seq": device}, device_id_type=MESH)


def gather_kernel(n, cuts, actives, swaps, shared, *refs):
    count = len(cuts)
    total = count + swaps
    x_refs, give_refs = refs[:count], refs[count:total]
    o_refs, take_refs = refs[total : total + count], refs[total + count : 2 * total]
    own_sem, local_sem, swap_sems, hand_sem = refs[2 * total : 2 * total + 4]
    sems = refs[2 * total + 4 :]
    me, core, r, _ = ring_place()
    targets = (ring_seq((r + 1) % n, core, n), ring_seq((r + n - 1) % n, core, n))
    sibling = ring_seq(r, 1 - core, n)
    greet((*targets, sibling), swaps > 0)

    def half_of(ref, c):
        height = ref.shape[0] // 2
        return ref.at[pl.ds(pl.multiple_of(c * height, height), height), :]

    gives, takes = list(give_refs), list(take_refs)
    if shared is not None:
        gives[shared], takes[shared] = half_of(gives[shared], core), half_of(takes[shared], core)
    swapped = swap_copies(gives, takes, swap_sems)
    for copy in swapped:
        copy.start()

    def handed(c):
        half = half_of(take_refs[shared], c)
        return remote(half, half, hand_sem.at[0], hand_sem.at[1], sibling)

    def block(t, d, c):
        return ring_seq((r + (-t if d == 0 else t) + n) % n, c, n)

    def guarded(i, source, action):
        if actives[i] is None:
            action()
        else:
            pl.when(actives[i](source))(action)

    def parts_of(i):
        height = x_refs[i].shape[0] // (2 * cuts[i])
        for k in range(cuts[i]):
            for d in range(2):
                yield k, d, pl.ds((d * cuts[i] + k) * height, height)

    def onward(i, t, d, k, rows):
        at = o_refs[i].at[block(t, d, core), rows]
        source = x_refs[i].at[rows] if t == 0 else at
        return remote(source, at, sems[4 * i].at[t, d, k], sems[4 * i + 1].at[t, d, k], targets[d])

    def across(i, t, d, k, rows, c):
        at = o_refs[i].at[block(t, d, c), rows]
        return remote(at, at, sems[4 * i + 2].at[t - 1, d, k], sems[4 * i + 3].at[t - 1, d, k], sibling)

    def local(i):
        return pltpu.make_async_copy(x_refs[i], o_refs[i].at[me], local_sem.at[i])

    def own(i):
        return remote(x_refs[i], o_refs[i].at[me], own_sem.at[i, 0], own_sem.at[i, 1], sibling)

    for i in range(count):
        local(i).start()
        for k, d, rows in parts_of(i):
            guarded(i, me, lambda: onward(i, 0, d, k, rows).start())
        guarded(i, me, lambda: own(i).start())
    for t in range(n - 1):
        for i in range(count):
            for k, d, rows in parts_of(i):

                def step():
                    arriving = onward(i, t, d, k, rows)
                    arriving.wait_recv()
                    if t < n - 2:
                        onward(i, t + 1, d, k, rows).start()
                    across(i, t + 1, d, k, rows, core).start()

                guarded(i, block(t + 1, d, core), step)
    for i in range(count):
        local(i).wait()
        guarded(i, me, lambda: own(i).wait_send())
        guarded(i, sibling, lambda: own(i).wait_recv())
        for t in range(n - 1):
            for k, d, rows in parts_of(i):
                guarded(i, block(t, d, core), lambda: onward(i, t, d, k, rows).wait_send())
                guarded(i, block(t + 1, d, core), lambda: across(i, t + 1, d, k, rows, core).wait_send())
                guarded(i, block(t + 1, d, 1 - core), lambda: across(i, t + 1, d, k, rows, 1 - core).wait_recv())
    if shared is not None:
        swapped[shared].wait_recv()
        handed(core).start()
    for i, copy in enumerate(swapped):
        copy.wait_send()
        if i != shared:
            copy.wait_recv()
    if shared is not None:
        handed(core).wait_send()
        handed(1 - core).wait_recv()


def ring_gather_many(operands, collective_id, actives=None, swaps=(), shared=None):
    devices = lax.axis_size("seq")
    n = devices // 2
    cuts = [2 if x.shape[0] % 64 == 0 else 1 for x in operands]
    anywhere = pl.BlockSpec(memory_space=pl.ANY)
    sems = [pltpu.SemaphoreType.DMA((n - 1, 2, cut)) for cut in cuts for _ in range(4)]
    return pl.pallas_call(
        functools.partial(gather_kernel, n, cuts, actives or [None] * len(operands), len(swaps), shared),
        out_shape=[jax.ShapeDtypeStruct((devices, *x.shape), x.dtype) for x in operands]
        + [jax.ShapeDtypeStruct(x.shape, x.dtype) for x in swaps],
        in_specs=[anywhere] * (len(operands) + len(swaps)),
        out_specs=[anywhere] * (len(operands) + len(swaps)),
        scratch_shapes=[
            pltpu.SemaphoreType.DMA((len(operands), 2)),
            pltpu.SemaphoreType.DMA((len(operands),)),
            pltpu.SemaphoreType.DMA((max(1, len(swaps)), 2)),
            pltpu.SemaphoreType.DMA((2,)),
        ]
        + sems,
        compiler_params=pltpu.CompilerParams(collective_id=collective_id, has_side_effects=True),
        cost_estimate=COST,
        name="ring_gather",
    )(*operands, *swaps)


def ring_gather(x, collective_id, swaps=()):
    out, *taken = ring_gather_many([x], collective_id, None, swaps)
    return out.reshape(-1, x.shape[1]), taken


def scatter_kernel(n, cut, swaps, *refs):
    a_ref, w_ref = refs[:2]
    o_ref = refs[2 + swaps]
    stage, sibbuf, rbuf, sbuf, send, recv, fsend, frecv, swap_sems = refs[3 + 2 * swaps :]
    me, core, r, _ = ring_place()
    targets = (ring_seq((r + 1) % n, core, n), ring_seq((r + n - 1) % n, core, n))
    sibling = ring_seq(r, 1 - core, n)
    greet((*targets, sibling), swaps > 0)
    swapped = swap_copies(refs[2 : 2 + swaps], refs[3 + swaps : 3 + 2 * swaps], swap_sems)
    for copy in swapped:
        copy.start()
    height, columns = o_ref.shape
    spans = (pl.ds(0, cut), pl.ds(cut, columns - cut))

    def chip(t, d):
        return (r + (-t - 1 if d == 0 else t + 1) + n) % n

    def part(t, d, c):
        block = ring_seq(chip(t, d), c, n)
        rows = a_ref[pl.ds(block * height, height), :]
        return mm_nt(rows, w_ref[spans[d], :])

    def across(t, d):
        return remote(stage.at[t, :, spans[d]], sibbuf.at[t, :, spans[d]], fsend.at[t, d], frecv.at[t, d], sibling)

    def onward(t, d):
        return remote(sbuf.at[t, :, spans[d]], rbuf.at[t, :, spans[d]], send.at[t, d], recv.at[t, d], targets[d])

    def give(t, d):
        stage[t, :, spans[d]] = part(t, d, 1 - core).astype(BF)
        across(t, d).start()

    for d in range(2):
        give(0, d)
    for t in range(n):
        for d in range(2):
            if t < n - 1:
                give(t + 1, d)
            value = part(t, d, core)
            across(t, d).wait_recv()
            value = value + sibbuf[t, :, spans[d]].astype(F32)
            if t > 0:
                onward(t - 1, d).wait_recv()
                value = value + rbuf[t - 1, :, spans[d]].astype(F32)
            if t < n - 1:
                sbuf[t, :, spans[d]] = value.astype(BF)
                onward(t, d).start()
            else:
                o_ref[:, spans[d]] = value
    for t in range(n):
        for d in range(2):
            across(t, d).wait_send()
            if t < n - 1:
                onward(t, d).wait_send()
    for copy in swapped:
        copy.wait()


def ring_scatter(a, w, collective_id, swaps=()):
    devices = lax.axis_size("seq")
    n = devices // 2
    rows = a.shape[0] // devices
    columns = w.shape[0]
    cut = columns // 256 * 128
    vmem = pl.BlockSpec(memory_space=pltpu.VMEM)
    anywhere = [pl.BlockSpec(memory_space=pl.ANY)] * len(swaps)
    out, *taken = pl.pallas_call(
        functools.partial(scatter_kernel, n, cut, len(swaps)),
        out_shape=[jax.ShapeDtypeStruct((rows, columns), F32)] + [jax.ShapeDtypeStruct(x.shape, x.dtype) for x in swaps],
        in_specs=[vmem, vmem] + anywhere,
        out_specs=[vmem] + anywhere,
        scratch_shapes=[
            pltpu.VMEM((n, rows, columns), BF),
            pltpu.VMEM((n, rows, columns), BF),
            pltpu.VMEM((n - 1, rows, columns), BF),
            pltpu.VMEM((n - 1, rows, columns), BF),
        ]
        + [pltpu.SemaphoreType.DMA((n - 1, 2))] * 2
        + [pltpu.SemaphoreType.DMA((n, 2))] * 2
        + [pltpu.SemaphoreType.DMA((max(1, len(swaps)), 2))],
        compiler_params=pltpu.CompilerParams(
            collective_id=collective_id, has_side_effects=True, vmem_limit_bytes=VMEM_LIMIT
        ),
        cost_estimate=COST,
        name="ring_scatter",
    )(a, w, *swaps)
    return out, taken


def fsdp_gather(x, other=None):
    count = lax.axis_size("fsdp")
    if count != 2:
        return lax.all_gather(x, "fsdp", axis=0, tiled=True)
    first = lax.axis_index("fsdp") == 0
    return jnp.concatenate([jnp.where(first, x, other), jnp.where(first, other, x)], axis=0)


def fsdp_pick(x, owner, other):
    count = lax.axis_size("fsdp")
    if count != 2:
        return lax.dynamic_index_in_dim(lax.all_gather(x, "fsdp", axis=0), owner, 0, keepdims=False)
    return jnp.where(lax.axis_index("fsdp") == owner, x, other)


def fsdp_given(x):
    half = x.shape[0] // 2
    return lax.dynamic_slice_in_dim(x, (1 - lax.axis_index("fsdp")) * half, half, 0)


def fsdp_scatter(x, taken=None):
    if taken is None:
        return lax.psum_scatter(x.astype(BF), "fsdp", scatter_dimension=0, tiled=True).astype(F32)
    half = x.shape[0] // 2
    kept = lax.dynamic_slice_in_dim(x, lax.axis_index("fsdp") * half, half, 0)
    return kept.astype(F32) + taken.astype(F32)


def fsdp_sum(x, taken=None):
    return lax.psum(x, "fsdp") if taken is None else x + taken


def turn(values, cosine, sine):
    half = values.shape[-1] // 2
    turned = jnp.concatenate([-values[:, half:], values[:, :half]], axis=-1)
    return values * cosine + turned * sine


def turn_back(gradient, cosine, sine):
    half = gradient.shape[-1] // 2
    scaled = gradient * sine
    return gradient * cosine + jnp.concatenate([scaled[:, half:], -scaled[:, :half]], axis=-1)


def spans_of(length):
    step = length // 8
    for i in range(8):
        start = i * step
        yield start, step, max(0, start - (3 * step if i % 2 == 0 else 2 * step))


def allowed_of(seg_col, seg_row, start, step, low):
    width = start + step - low
    query = start + lax.broadcasted_iota(jnp.int32, (step, width), 0)
    key = low + lax.broadcasted_iota(jnp.int32, (step, width), 1)
    return (key <= query) & (seg_col[start : start + step, :] == seg_row[:, low : start + step])


def attend_block(start, step, low, qh_ref, kh_ref, v_ref, segc_ref, segr_ref, heads_ref, lse_ref):
    end = start + step
    scores = mm_nt(qh_ref[start:end, :], kh_ref[low:end, :]) * SCALE
    scores = jnp.where(allowed_of(segc_ref, segr_ref, start, step, low), scores, NEG)
    peak = jnp.max(scores, axis=-1, keepdims=True)
    raised = jnp.exp(scores - peak)
    total = jnp.sum(raised, axis=-1, keepdims=True)
    prob = (raised * (1.0 / total)).astype(BF)
    heads_ref[start:end, :] = mm(prob, v_ref[low:end, :]).astype(BF)
    lse_ref[start:end, :] = peak + jnp.log(total)


def weights_back(wb_ref, wq, we):
    width = wq.shape[0]
    rank = we.shape[0]
    wb_ref[:, :] = jnp.zeros(wb_ref.shape, BF)
    wb_ref[:width, :NOPE] = wq[:, :NOPE]
    wb_ref[:width, KV_END:QK_END] = wq[:, NOPE:]
    wb_ref[width : width + rank, NOPE:KV_END] = we[...]
    shape = (ROPE, 2 * ROPE)
    eye = lax.broadcasted_iota(jnp.int32, shape, 0) + ROPE == lax.broadcasted_iota(jnp.int32, shape, 1)
    wb_ref[width + rank : width + rank + ROPE, KV_END:] = eye.astype(F32).astype(BF)


def front_kernel(count, swaps, chunks, *refs):
    wq_parts, wl_parts, we_parts = refs[:count], refs[count : 2 * count], refs[2 * count : 3 * count]
    x_ref, gain_ref, lgain_ref, cos_ref, sin_ref, segc_ref, segr_ref = refs[3 * count : 3 * count + 7]
    refs = refs[3 * count + 7 :]
    gives, refs = refs[:swaps], refs[swaps:]
    act_ref, cn_ref, qh_ref, kh_ref, v_ref, heads_ref, lse_ref, wb_ref = refs[:8]
    takes, refs = refs[8 : 8 + swaps], refs[8 + swaps :]
    wq, wl, we, sems, swap_sems = refs
    i = pl.program_id(0)
    length = qh_ref.shape[0]
    step = length // chunks
    swapped = swap_copies(gives, takes, swap_sems) if swaps else []
    copies = [fill(p, w, sems.at[j]) for j, (p, w) in enumerate(((wq_parts, wq), (wl_parts, wl), (we_parts, we)))]
    start_first(copies)

    @pl.when(i == 0)
    def _():
        if swaps:
            greet((), True)
            for copy in swapped:
                copy.start()

    wait_first(copies)

    @pl.when(i < chunks)
    def _():
        rows = pl.ds(pl.multiple_of(i * step, step), step)
        x = x_ref[...].astype(F32)
        act_ref[...] = (x * norm_scale(x) * gain_ref[...]).astype(BF)
        cosine, sine = cos_ref[...], sin_ref[...]
        query = mm(act_ref[...], wq[...])
        qh_ref[rows, :NOPE] = query[:, :NOPE].astype(BF)
        qh_ref[rows, NOPE:] = turn(query[:, NOPE:].astype(BF).astype(F32), cosine, sine).astype(BF)
        latent = mm(act_ref[...], wl[...])
        comp = latent[:, :KV_RANK]
        cn_ref[...] = (comp * norm_scale(comp) * lgain_ref[...]).astype(BF)
        kh_ref[rows, NOPE:] = turn(latent[:, KV_RANK:].astype(BF).astype(F32), cosine, sine).astype(BF)
        kv = mm(cn_ref[...], we[...])
        kh_ref[rows, :NOPE] = kv[:, :NOPE].astype(BF)
        v_ref[rows, :] = kv[:, NOPE:].astype(BF)

    @pl.when(i == chunks)
    def _():
        for start, size, low in spans_of(length):
            attend_block(start, size, low, qh_ref, kh_ref, v_ref, segc_ref, segr_ref, heads_ref, lse_ref)
        weights_back(wb_ref, wq, we)
        for copy in swapped:
            copy.wait()


def front(pieces, x, gain, lgain, cosine, sine, seg_col, seg_row, swaps, collective_id):
    length, width = x.shape
    chunks = 4
    step = length // chunks
    count = len(pieces[0])
    vmem = pl.BlockSpec(memory_space=pltpu.VMEM)
    anywhere = pl.BlockSpec(memory_space=pl.ANY)

    def tile(columns):
        return pl.BlockSpec((step, columns), lambda i: (jnp.minimum(i, chunks - 1), 0))

    def held(rows, columns):
        return pl.BlockSpec((rows, columns), lambda i: (0, 0))

    full = lambda group: (group[0].shape[0] * count, group[0].shape[1])
    backs = (width + KV_RANK + 2 * ROPE, QK_END + ROPE)
    outs = [
        (tile(width), (length, width), BF),
        (tile(KV_RANK), (length, KV_RANK), BF),
        (held(length, QD), (length, QD), BF),
        (held(length, QD), (length, QD), BF),
        (held(length, V_DIM), (length, V_DIM), BF),
        (held(length, V_DIM), (length, V_DIM), BF),
        (held(length, 1), (length, 1), F32),
        (held(*backs), backs, BF),
    ]
    return pl.pallas_call(
        functools.partial(front_kernel, count, len(swaps), chunks),
        grid=(chunks + 1,),
        out_shape=[jax.ShapeDtypeStruct(shape, dtype) for _, shape, dtype in outs]
        + [jax.ShapeDtypeStruct(w.shape, w.dtype) for w in swaps],
        in_specs=[anywhere] * (3 * count) + [tile(width), vmem, vmem, tile(ROPE), tile(ROPE), vmem, vmem]
        + [anywhere] * len(swaps),
        out_specs=[spec for spec, _, _ in outs] + [anywhere] * len(swaps),
        scratch_shapes=[pltpu.VMEM(full(group), BF) for group in pieces]
        + [pltpu.SemaphoreType.DMA((3, count)), pltpu.SemaphoreType.DMA((max(1, len(swaps)), 2))],
        compiler_params=pltpu.CompilerParams(
            vmem_limit_bytes=VMEM_LIMIT, collective_id=collective_id, has_side_effects=len(swaps) > 0
        ),
        cost_estimate=COST,
        name="front",
    )(*sum(pieces, ()), x, gain, lgain, cosine, sine, seg_col, seg_row, *swaps)


def attend_back_kernel(
    qh_ref, kh_ref, v_ref, lse_ref, heads_ref, da_ref, wo_ref, cos_ref, sin_ref, segc_ref, segr_ref, back_ref, gout_ref, dk_acc, dv_acc
):
    dk_acc[...] = jnp.zeros_like(dk_acc)
    dv_acc[...] = jnp.zeros_like(dv_acc)
    for start, step, low in spans_of(qh_ref.shape[0]):
        end = start + step
        query = qh_ref[start:end, :]
        grad = mm_nt(da_ref[start:end, :], wo_ref[...]).astype(BF)
        keys = kh_ref[low:end, :]
        scores = mm_nt(query, keys) * SCALE
        allowed = allowed_of(segc_ref, segr_ref, start, step, low)
        prob = jnp.where(allowed, jnp.exp(scores - lse_ref[start:end, :]), 0.0)
        dv_acc[low:end, :] += mm_tn(prob.astype(BF), grad)
        dprob = mm_nt(grad, v_ref[low:end, :])
        delta = jnp.sum(prob * dprob, axis=-1, keepdims=True)
        dscore = (prob * (dprob - delta) * SCALE).astype(BF)
        dquery = mm(dscore, keys)
        back_ref[start:end, :NOPE] = dquery[:, :NOPE].astype(BF)
        turned = turn_back(dquery[:, NOPE:], cos_ref[start:end, :], sin_ref[start:end, :])
        back_ref[start:end, KV_END:QK_END] = turned.astype(BF)
        dk_acc[low:end, :] += mm_tn(dscore, query)
    back_ref[:, NOPE : 2 * NOPE] = dk_acc[:, :NOPE].astype(BF)
    back_ref[:, 2 * NOPE : KV_END] = dv_acc[...].astype(BF)
    back_ref[:, QK_END:] = turn_back(dk_acc[:, NOPE:], cos_ref[...], sin_ref[...]).astype(BF)
    gout_ref[...] = mm_tn(heads_ref[...], da_ref[...]).astype(BF)


def local_call(kernel, outs, scratch, name, *operands):
    vmem = pl.BlockSpec(memory_space=pltpu.VMEM)
    return pl.pallas_call(
        kernel,
        out_shape=[jax.ShapeDtypeStruct(shape, dtype) for shape, dtype in outs],
        in_specs=[vmem] * len(operands),
        out_specs=[vmem] * len(outs),
        scratch_shapes=scratch,
        compiler_params=pltpu.CompilerParams(vmem_limit_bytes=VMEM_LIMIT),
        cost_estimate=COST,
        name=name,
    )(*operands)


def fsdp_pieces(x, other):
    if lax.axis_size("fsdp") != 2:
        return (lax.all_gather(x, "fsdp", axis=0, tiled=True),)
    return (x, other)


def fill(pieces, dst, sems):
    if len(pieces) == 1:
        return [pltpu.make_async_copy(pieces[0], dst, sems.at[0])]
    part = lax.axis_index("fsdp")
    height = pieces[0].shape[0]
    starts = (part * height, (1 - part) * height)
    return [
        pltpu.make_async_copy(piece, dst.at[pl.ds(pl.multiple_of(start, height), height), :], sems.at[i])
        for i, (piece, start) in enumerate(zip(pieces, starts))
    ]


def picks(slot_ref, share_ref, b, most):
    slots = slot_ref[b]
    pick = slots == lax.broadcasted_iota(jnp.int32, (most, slots.shape[1]), 0)
    return pick.astype(BF), jnp.sum(jnp.where(pick, share_ref[b], 0.0), axis=-1, keepdims=True)


def hidden_spans(hidden):
    cut = -(-hidden // 256) * 128
    return ((0, cut), (cut, hidden))


def start_first(groups):
    @pl.when(pl.program_id(0) == 0)
    def _():
        for group in groups:
            for copy in group:
                copy.start()


def wait_first(groups):
    @pl.when(pl.program_id(0) == 0)
    def _():
        for group in groups:
            for copy in group:
                copy.wait()


def expert_in_kernel(count, most, swaps, *refs):
    wg_parts, wu_parts = refs[:count], refs[count : 2 * count]
    act_ref, slot_ref, share_ref, wsg_ref, wsu_ref = refs[2 * count : 2 * count + 5]
    gives, refs = refs[2 * count + 5 : 2 * count + 5 + swaps], refs[2 * count + 5 + swaps :]
    xe_ref, ge_ref, ue_ref, he_ref, sg_ref, su_ref, sh_ref = refs[:7]
    takes, (wg, wu, sems, swap_sems) = refs[7 : 7 + swaps], refs[7 + swaps :]
    swapped = swap_copies(gives, takes, swap_sems) if swaps else []
    if swaps:

        @pl.when(pl.program_id(0) == 0)
        def _():
            greet((), True)
            for copy in swapped:
                copy.start()

    copies = [fill(wg_parts, wg, sems.at[0]), fill(wu_parts, wu, sems.at[1])]
    start_first(copies)
    blocks, rows = slot_ref.shape[0], slot_ref.shape[2]
    for b in range(blocks):
        pick, _ = picks(slot_ref, share_ref, b, most)
        xe_ref[b * most : (b + 1) * most, :] = mm(pick, act_ref[b * rows : (b + 1) * rows, :]).astype(BF)
    act = act_ref[...]
    sg, su = mm(act, wsg_ref[...]), mm(act, wsu_ref[...])
    sg_ref[...] = sg
    su_ref[...] = su
    sh_ref[...] = (sg * jax.nn.sigmoid(sg) * su).astype(BF)
    wait_first(copies)
    for low, high in hidden_spans(wg.shape[1]):
        ge = mm(xe_ref[...], wg[:, low:high])
        ue = mm(xe_ref[...], wu[:, low:high])
        ge_ref[:, low:high] = ge
        ue_ref[:, low:high] = ue
        he_ref[:, low:high] = (ge * jax.nn.sigmoid(ge) * ue).astype(BF)
    if swaps:

        @pl.when(pl.program_id(0) == pl.num_programs(0) - 1)
        def _():
            for copy in swapped:
                copy.wait()


def expert_out_kernel(count, most, swaps, *refs):
    wd_parts = refs[:count]
    he_ref, slot_ref, share_ref, wsd_ref, sh_ref, y_ref, wd, sems, _ = refs[count:]
    copies = [fill(wd_parts, wd, sems.at[0])]
    start_first(copies)
    wait_first(copies)
    blocks, rows = slot_ref.shape[0], slot_ref.shape[2]
    z = mm(he_ref[...], wd[...]).astype(BF)
    for b in range(blocks):
        pick, share = picks(slot_ref, share_ref, b, most)
        ye = z[b * most : (b + 1) * most, :].astype(F32)
        ys = mm(sh_ref[b * rows : (b + 1) * rows, :], wsd_ref[...])
        y_ref[b * rows : (b + 1) * rows, :] = (ys + mm_tn(pick, (share * ye).astype(BF))).astype(BF)


def expert_back_kernel(count, most, swaps, *refs):
    wg_parts, wu_parts, wd_parts = refs[:count], refs[count : 2 * count], refs[2 * count : 3 * count]
    g_ref, slot_ref, share_ref, wsg_ref, wsu_ref, wsd_ref, ge_ref, ue_ref, sg_ref, su_ref = refs[3 * count : 3 * count + 10]
    dact_ref, dye_ref, dge_ref, due_ref, dsg_ref, dsu_ref = refs[3 * count + 10 : 3 * count + 16]
    wg, wu, wd, sems, _ = refs[3 * count + 16 :]
    copies = [fill(p, w, sems.at[i]) for i, (p, w) in enumerate(((wg_parts, wg), (wu_parts, wu), (wd_parts, wd)))]
    start_first(copies)
    blocks, rows = slot_ref.shape[0], slot_ref.shape[2]
    for b in range(blocks):
        pick, share = picks(slot_ref, share_ref, b, most)
        packed = mm(pick, g_ref[b * rows : (b + 1) * rows, :])
        dye_ref[b * most : (b + 1) * most, :] = (share * packed).astype(BF)
    dsh = mm_nt(g_ref[...], wsd_ref[...])
    sg, su = sg_ref[...], su_ref[...]
    sig = jax.nn.sigmoid(sg)
    dsg_ref[...] = (dsh * su * sig * (1.0 + sg * (1.0 - sig))).astype(BF)
    dsu_ref[...] = (dsh * sg * sig).astype(BF)
    wait_first(copies)
    for low, high in hidden_spans(wg.shape[1]):
        dhe = mm_nt(dye_ref[...], wd[low:high, :])
        ge, ue = ge_ref[:, low:high], ue_ref[:, low:high]
        sig = jax.nn.sigmoid(ge)
        dge_ref[:, low:high] = (dhe * ue * sig * (1.0 + ge * (1.0 - sig))).astype(BF)
        due_ref[:, low:high] = (dhe * ge * sig).astype(BF)
    dxe = (mm_nt(dge_ref[...], wg[...]) + mm_nt(due_ref[...], wu[...])).astype(BF)
    for b in range(blocks):
        pick, _ = picks(slot_ref, share_ref, b, most)
        block = slice(b * rows, (b + 1) * rows)
        shared = mm_nt(dsg_ref[block, :], wsg_ref[...]) + mm_nt(dsu_ref[block, :], wsu_ref[...])
        dact_ref[block, :] = (shared + mm_tn(pick, dxe[b * most : (b + 1) * most, :])).astype(BF)


def expert_call(kernel, name, pieces, most, steps, slot, share, whole, tiled, outs, swaps=(), collective_id=None):
    devices, rows = slot.shape[0], slot.shape[2]
    per = devices // steps
    anywhere = pl.BlockSpec(memory_space=pl.ANY)
    vmem = pl.BlockSpec(memory_space=pltpu.VMEM)

    def tile(total, columns):
        return pl.BlockSpec((total // steps, columns), lambda i: (i, 0))

    cut = pl.BlockSpec((per, 1, rows), lambda i: (i, 0, 0))
    count = len(pieces[0])
    full = lambda group: (group[0].shape[0] * count, group[0].shape[1])
    return pl.pallas_call(
        functools.partial(kernel, count, most, len(swaps)),
        grid=(steps,),
        out_shape=[jax.ShapeDtypeStruct((total, columns), dtype) for total, columns, dtype in outs]
        + [jax.ShapeDtypeStruct(x.shape, x.dtype) for x in swaps],
        in_specs=[anywhere] * (len(pieces) * count) + [tile(*tiled[0].shape), cut, cut] + [vmem] * len(whole)
        + [tile(*t.shape) for t in tiled[1:]]
        + [anywhere] * len(swaps),
        out_specs=[tile(total, columns) for total, columns, _ in outs] + [anywhere] * len(swaps),
        scratch_shapes=[pltpu.VMEM(full(group), BF) for group in pieces]
        + [pltpu.SemaphoreType.DMA((len(pieces), count)), pltpu.SemaphoreType.DMA((max(1, len(swaps)), 2))],
        compiler_params=pltpu.CompilerParams(
            vmem_limit_bytes=VMEM_LIMIT, collective_id=collective_id, has_side_effects=len(swaps) > 0
        ),
        cost_estimate=COST,
        name=name,
    )(*sum(pieces, ()), tiled[0], slot, share, *whole, *tiled[1:], *swaps)


def weight_grads_kernel(n, cut, *refs):
    xe_ref, dge_ref, due_ref, he_ref, dye_ref, act_ref, dsg_ref, dsu_ref, sh_ref, g_ref, part_ref = refs[:11]
    o_ref, gate_ref, up_ref, down_ref, sgate_ref, sup_ref, sdown_ref = refs[11:18]
    sibbuf, rbuf, sbuf, send, recv, fsend, frecv = refs[18:]
    t = pl.program_id(0)
    me, core, r, _ = ring_place()
    targets = (ring_seq((r + 1) % n, core, n), ring_seq((r + n - 1) % n, core, n))
    sibling = ring_seq(r, 1 - core, n)
    columns = o_ref.shape[1]
    spans = (pl.ds(0, cut), pl.ds(cut, columns - cut))

    def block(step, d, c):
        return ring_seq((r + (-step - 1 if d == 0 else step + 1) + n) % n, c, n)

    def across(step, d):
        source = part_ref.at[block(step, d, 1 - core), :, spans[d]]
        return remote(source, sibbuf.at[step, :, spans[d]], fsend.at[step, d], frecv.at[step, d], sibling)

    def onward(step, d):
        return remote(
            sbuf.at[step, :, spans[d]], rbuf.at[step, :, spans[d]], send.at[step, d], recv.at[step, d], targets[d]
        )

    @pl.when(t == 0)
    def _():
        greet((*targets, sibling))
        for step in range(n):
            for d in range(2):
                across(step, d).start()

    for d in range(2):
        across(t, d).wait_recv()

        def both():
            return part_ref[block(t, d, core), :, spans[d]].astype(F32) + sibbuf[t, :, spans[d]].astype(F32)

        @pl.when(t == 0)
        def _():
            sbuf[0, :, spans[d]] = both().astype(BF)
            onward(0, d).start()

        @pl.when((t > 0) & (t < n - 1))
        def _():
            onward(t - 1, d).wait_recv()
            sbuf[t, :, spans[d]] = (both() + rbuf[t - 1, :, spans[d]].astype(F32)).astype(BF)
            onward(t, d).start()

        @pl.when(t == n - 1)
        def _():
            onward(n - 2, d).wait_recv()
            o_ref[:, spans[d]] = both() + rbuf[n - 2, :, spans[d]].astype(F32)

    gate_ref[...] = mm_tn(xe_ref[...], dge_ref[...]).astype(BF)
    up_ref[...] = mm_tn(xe_ref[...], due_ref[...]).astype(BF)
    down_ref[...] = mm_tn(he_ref[...], dye_ref[...]).astype(BF)
    sgate_ref[...] = mm_tn(act_ref[...], dsg_ref[...]).astype(BF)
    sup_ref[...] = mm_tn(act_ref[...], dsu_ref[...]).astype(BF)
    sdown_ref[...] = mm_tn(sh_ref[...], g_ref[...]).astype(BF)

    @pl.when(t == n - 1)
    def _():
        for step in range(n):
            for d in range(2):
                across(step, d).wait_send()
                if step < n - 1:
                    onward(step, d).wait_send()


def weight_grads(xe, dge, due, he, dye, act, dsg, dsu, sh, g, part, collective_id):
    devices = lax.axis_size("seq")
    n = devices // 2
    length, columns = part.shape
    rows = length // devices
    cut = columns // 256 * 128

    def tile(x):
        return pl.BlockSpec((x.shape[0], x.shape[1] // n), lambda i: (0, i))

    def held(x):
        return pl.BlockSpec(memory_space=pltpu.VMEM)

    ff, units = dge.shape[1], dsg.shape[1]
    slab = columns // n
    down = lambda width: pl.BlockSpec((slab, width), lambda i: (i, 0))
    along = lambda height: pl.BlockSpec((height, slab), lambda i: (0, i))
    return pl.pallas_call(
        functools.partial(weight_grads_kernel, n, cut),
        grid=(n,),
        out_shape=[jax.ShapeDtypeStruct((rows, columns), F32)]
        + [
            jax.ShapeDtypeStruct(shape, BF)
            for shape in ((columns, ff), (columns, ff), (ff, columns), (columns, units), (columns, units), (units, columns))
        ],
        in_specs=[tile(xe), held(dge), held(due), held(he), tile(dye), tile(act), held(dsg), held(dsu), held(sh), tile(g)]
        + [held(part)],
        out_specs=[pl.BlockSpec((rows, columns), lambda i: (0, 0)), down(ff), down(ff), along(ff)]
        + [down(units), down(units), along(units)],
        scratch_shapes=[
            pltpu.VMEM((n, rows, columns), BF),
            pltpu.VMEM((n - 1, rows, columns), BF),
            pltpu.VMEM((n - 1, rows, columns), BF),
        ]
        + [pltpu.SemaphoreType.DMA((n - 1, 2))] * 2
        + [pltpu.SemaphoreType.DMA((n, 2))] * 2,
        compiler_params=pltpu.CompilerParams(
            collective_id=collective_id, has_side_effects=True, vmem_limit_bytes=VMEM_LIMIT
        ),
        cost_estimate=COST,
        name="weight_grads",
    )(xe, dge, due, he, dye, act, dsg, dsu, sh, g, part.reshape(devices, rows, columns))


def widen(stacked, parts, name):
    devices, rows, columns = stacked.shape
    share = columns // parts
    steps = 8

    def kernel(i_ref, o_ref):
        for p in range(parts):
            for d in range(devices):
                at = (p * devices + d) * share
                o_ref[:, at : at + share] = i_ref[d, :, p * share : (p + 1) * share].astype(F32)

    return pl.pallas_call(
        kernel,
        grid=(steps,),
        out_shape=jax.ShapeDtypeStruct((rows, devices * columns), F32),
        in_specs=[pl.BlockSpec((devices, rows // steps, columns), lambda i: (0, i, 0))],
        out_specs=pl.BlockSpec((rows // steps, devices * columns), lambda i: (i, 0)),
        compiler_params=pltpu.CompilerParams(vmem_limit_bytes=VMEM_LIMIT),
        cost_estimate=COST,
        name=name,
    )(stacked)


def columns_of(weight, at, width):
    return lax.dynamic_slice_in_dim(weight, at * width, width, 1).astype(BF)


def rows_of(weight, at, height):
    return lax.dynamic_slice_in_dim(weight, at * height, height, 0).astype(BF)


def per_device(
    tokens,
    segment_ids,
    routes,
    gate_weights,
    out_grad,
    attn_gain,
    q_weight,
    latent_weight,
    latent_gain,
    kv_weight,
    out_weight,
    ffn_gain,
    shared_gate,
    shared_up,
    shared_down,
    expert_gate,
    expert_up,
    expert_down,
):
    _, rows, width = tokens.shape
    devices = lax.axis_size("seq")
    at = lax.axis_index("seq")
    parts = lax.axis_size("fsdp")
    part = lax.axis_index("fsdp")
    length = rows * devices
    own_x = tokens[0]
    own_g = out_grad[0]

    per, per_latent = attn_gain.shape[0], latent_gain.shape[0]
    gains = jnp.concatenate([attn_gain, ffn_gain, latent_gain]).astype(BF)
    gains_size = gains.shape[0]
    gains_rows = -(-gains_size // 2048) * 16
    gains = jnp.pad(gains, (0, gains_rows * 128 - gains_size)).reshape(gains_rows, 128)
    out_rows = out_weight.shape[0]
    early_latent = 2
    early = (
        gains,
        columns_of(q_weight, at, QD),
        latent_weight.astype(BF),
        columns_of(kv_weight, at, NOPE + V_DIM),
        lax.dynamic_slice_in_dim(out_weight, at * V_DIM % out_rows, V_DIM, 0).astype(BF),
    )
    pair = parts == 2

    def crossing(*arrays):
        return arrays if pair else ()

    def crossed(taken, count):
        return taken if pair else [None] * count

    experts = jnp.arange(devices, dtype=jnp.int32)
    spread = jnp.sum(
        jnp.where(routes[0].T[None, :, :] == experts[:, None, None], gate_weights[0].T[None, :, :], 0.0), axis=1
    )
    x_all, spread_all, *others = ring_gather_many(
        [own_x, spread], 8, None, crossing(*early), early_latent if pair else None
    )
    x_all = x_all.reshape(length, width)
    share_of = lax.dynamic_index_in_dim(spread_all, at, 1, keepdims=False)
    others = crossed(others, len(early))
    gains = fsdp_gather(gains, others[0]).reshape(parts, -1)[:, :gains_size].astype(F32)
    gain_one = gains[:, :per].reshape(1, -1)
    gain_two = gains[:, per : 2 * per].reshape(1, -1)
    gain_lat = gains[:, 2 * per :].reshape(1, -1)
    w_latent = fsdp_gather(early[2], others[2])
    w_out = fsdp_pick(early[4], at * V_DIM // out_rows, others[4])

    hidden = shared_down.shape[0] * parts
    share = shared_down.shape[0] // devices

    def shared_columns(weight):
        pieces = [
            lax.dynamic_slice_in_dim(weight, p * (hidden // parts) + at * share, share, 1) for p in range(parts)
        ]
        return jnp.concatenate(pieces, axis=1).astype(BF)

    share_pad = -(-share // 32) * 32
    sgate, sup = shared_columns(shared_gate), shared_columns(shared_up)
    sdown = jnp.pad(rows_of(shared_down, at, share), ((0, share_pad - share), (0, 0)))
    egate, eup, edown = expert_gate[0].astype(BF), expert_up[0].astype(BF), expert_down[0].astype(BF)

    cosine, sine = rope_tables(length)
    seg_col, seg_row = segment_ids.reshape(length, 1), segment_ids
    act_one, cnorm, qh, kh, values, heads, lse, w_back, *taken = front(
        tuple(fsdp_pieces(early[i], others[i]) for i in (1, 2, 3)),
        x_all,
        gain_one,
        gain_lat,
        cosine,
        sine,
        seg_col,
        seg_row,
        crossing(sgate, sup, sdown),
        11 if pair else None,
    )
    sgate_other, sup_other, sdown_other = crossed(taken, 3)
    own_xf = own_x.astype(F32)
    attended, taken = ring_scatter(heads, w_out.T, 2, crossing(egate))
    (egate_other,) = crossed(taken, 1)
    x1 = own_xf + attended
    r3 = norm_scale(x1)
    act_two = (x1 * r3 * gain_two).astype(BF)
    act_all, taken = ring_gather(act_two, 9, crossing(eup))
    (eup_other,) = crossed(taken, 1)
    w_egate, w_eup = fsdp_pieces(egate, egate_other), fsdp_pieces(eup, eup_other)
    w_sgate, w_sup = fsdp_gather(sgate, sgate_other), fsdp_gather(sup, sup_other)
    late_g, act_all = lax.optimization_barrier((own_g, act_all))
    g_all = lax.all_gather(late_g, "seq", axis=0, tiled=True)

    most = min(MOST, rows)
    named = share_of > 0.0
    rank = jnp.cumsum(named.astype(jnp.int32), axis=1) - 1
    slot = jnp.where(named, rank, -1)[:, None, :]
    share_of = share_of[:, None, :]
    packed = devices * most
    ff = expert_gate.shape[2]
    units = parts * share
    steps = 4
    xe, ge, ue, he, sg, su, sh, *taken = expert_call(
        expert_in_kernel,
        "experts_in",
        (w_egate, w_eup),
        most,
        steps,
        slot,
        share_of,
        (w_sgate, w_sup),
        (act_all,),
        (
            (packed, width, BF),
            (packed, ff, F32),
            (packed, ff, F32),
            (packed, ff, BF),
            (length, units, F32),
            (length, units, F32),
            (length, units, BF),
        ),
        crossing(edown),
        10 if pair else None,
    )
    (edown_other,) = crossed(taken, 1)
    w_edown = fsdp_pieces(edown, edown_other)
    w_sdown = fsdp_gather(sdown[:share], sdown_other[:share] if pair else None)
    (y_part,) = expert_call(
        expert_out_kernel,
        "experts_out",
        (w_edown,),
        most,
        steps,
        slot,
        share_of,
        (w_sdown,),
        (he, sh),
        ((length, width, BF),),
    )
    y_sum = lax.psum_scatter(y_part, "seq", scatter_dimension=0, tiled=True).astype(F32)
    dact_part, dye, dge, due, dsg, dsu = expert_call(
        expert_back_kernel,
        "experts_back",
        (w_egate, w_eup, w_edown),
        most,
        steps,
        slot,
        share_of,
        (w_sgate, w_sup, w_sdown),
        (g_all, ge, ue, sg, su),
        (
            (length, width, BF),
            (packed, width, BF),
            (packed, ff, BF),
            (packed, ff, BF),
            (length, units, BF),
            (length, units, BF),
        ),
    )
    dact_two, grad_egate, grad_eup, grad_edown, grad_sgate, grad_sup, grad_sdown = weight_grads(
        xe, dge, due, he, dye, act_all, dsg, dsu, sh, g_all, dact_part, 3
    )
    own_gf = own_g.astype(F32)
    grad_gain_two = jnp.sum(dact_two * x1 * r3, axis=0)
    dx1 = own_gf + norm_back(x1, r3, dact_two * gain_two)
    sdown_given = jnp.pad(fsdp_given(grad_sdown), ((0, share_pad - share), (0, 0))) if pair else None
    dattn_all, taken = ring_gather(
        dx1.astype(BF), 1, crossing(fsdp_given(grad_sgate), fsdp_given(grad_sup), sdown_given) if pair else ()
    )
    sgate_taken, sup_taken, sdown_taken = crossed(taken, 3)
    grad_sgate = fsdp_scatter(grad_sgate, sgate_taken).astype(BF)
    grad_sup = fsdp_scatter(grad_sup, sup_taken).astype(BF)
    grad_sdown = fsdp_scatter(grad_sdown, sdown_taken[:share] if pair else None).astype(BF)
    output = (x1 + y_sum).astype(BF)

    back, grad_out = local_call(
        attend_back_kernel,
        [((length, QK_END + ROPE), BF), ((V_DIM, width), BF)],
        [pltpu.VMEM((length, QD), F32), pltpu.VMEM((length, V_DIM), F32)],
        "attend_back",
        qh,
        kh,
        values,
        lse,
        heads,
        dattn_all,
        w_out,
        cosine,
        sine,
        seg_col,
        seg_row,
    )
    grad_back = mm_tn(act_one, back).astype(BF)
    grad_query = jnp.concatenate([grad_back[:, :NOPE], grad_back[:, KV_END:QK_END]], 1)
    grad_expand = mm_tn(cnorm, back[:, NOPE:KV_END]).astype(BF)
    summed, taken = ring_scatter(back, w_back, 4, (fsdp_given(grad_edown),) if pair else ())
    grad_edown = fsdp_scatter(grad_edown, *taken)

    r1 = norm_scale(own_xf)
    own_act = (own_xf * r1 * gain_one).astype(BF)
    own_comp = mm(own_act, w_latent)[:, :KV_RANK]
    r2 = norm_scale(own_comp)
    dcn = summed[:, width : width + KV_RANK]
    grad_gain_lat = jnp.sum(dcn * own_comp * r2, axis=0)
    dcomp = norm_back(own_comp, r2, dcn * gain_lat)
    dlatent = jnp.concatenate([dcomp, summed[:, width + KV_RANK : width + KV_RANK + ROPE]], axis=-1).astype(BF)
    dact_one = summed[:, :width] + mm_nt(dlatent, w_latent)
    grad_gain_one = jnp.sum(dact_one * own_xf * r1, axis=0)
    input_grad = dx1 + norm_back(own_xf, r1, dact_one * gain_one)

    small = jnp.concatenate([grad_gain_one, grad_gain_two, grad_gain_lat])
    small = jnp.pad(small, (0, 64 * 128 - small.shape[0])).reshape(64, 128)

    def in_part(device):
        return device * V_DIM // out_rows == lax.axis_index("fsdp")

    gate_all, up_all, dlatent_all, *taken = ring_gather_many(
        [grad_sgate, grad_sup, dlatent],
        5,
        None,
        (fsdp_given(grad_query), fsdp_given(grad_expand), grad_out, small) if pair else (),
    )
    query_taken, expand_taken, out_taken, small_taken = crossed(taken, 4)
    grad_query = fsdp_scatter(grad_query, query_taken).astype(BF)
    grad_expand = fsdp_scatter(grad_expand, expand_taken).astype(BF)
    grad_out = fsdp_sum(grad_out, out_taken)
    small = fsdp_sum(small, small_taken)
    slab = width // parts // devices
    act_cols = jnp.concatenate(
        [lax.dynamic_slice_in_dim(act_one, p * (width // parts) + at * slab, slab, 1) for p in range(parts)], axis=1
    )
    grad_latent = mm_tn(act_cols, dlatent_all.reshape(length, -1)).astype(BF)
    sdown_pad = jnp.pad(grad_sdown, ((0, share_pad - share), (0, 0)))
    query_all, sdown_all, *taken = ring_gather_many(
        [grad_query, sdown_pad], 6, None, (fsdp_given(grad_latent), fsdp_given(grad_egate)) if pair else ()
    )
    latent_taken, egate_taken = crossed(taken, 2)
    grad_latent = fsdp_scatter(grad_latent, latent_taken).astype(BF)
    grad_egate = fsdp_scatter(grad_egate, egate_taken)
    latent_pad = -(-slab // 32) * 32
    out_all, expand_all, latent_all, small_all, *taken = ring_gather_many(
        [grad_out, grad_expand, jnp.pad(grad_latent, ((0, latent_pad - slab), (0, 0))), small],
        7,
        [in_part, None, None, None],
        (fsdp_given(grad_eup),) if pair else (),
    )
    (eup_taken,) = crossed(taken, 1)
    grad_eup = fsdp_scatter(grad_eup, eup_taken)
    latent_all = latent_all[:, :slab]
    out_grad_own = lax.dynamic_slice_in_dim(
        out_all.reshape(devices * V_DIM, width), part * out_rows, out_rows, 0
    ).astype(F32)
    small = jnp.sum(small_all, axis=0).reshape(-1)
    gain_rows = width // parts
    own_gains = [
        lax.dynamic_slice_in_dim(small, part * gain_rows, gain_rows),
        lax.dynamic_slice_in_dim(small, width + part * gain_rows, gain_rows),
        lax.dynamic_slice_in_dim(small, 2 * width + part * (KV_RANK // parts), KV_RANK // parts),
    ]
    return (
        output[None],
        input_grad[None],
        own_gains[0],
        widen(query_all, 1, "wide_q"),
        latent_all.reshape(-1, grad_latent.shape[1]).astype(F32),
        own_gains[2],
        widen(expand_all, 1, "wide_kv"),
        out_grad_own,
        own_gains[1],
        widen(gate_all, parts, "wide_gate"),
        widen(up_all, parts, "wide_up"),
        sdown_all[:, :share].reshape(-1, width).astype(F32),
        grad_egate[None],
        grad_eup[None],
        grad_edown[None],
    )


def solution(mesh):
    token_spec = P("fsdp", "seq", None)
    row_spec = P("fsdp", None)
    gain_spec = P("fsdp")
    expert_spec = P("seq", "fsdp", None)
    dense = (gain_spec, row_spec, row_spec, gain_spec, row_spec, row_spec, gain_spec, row_spec, row_spec, row_spec)
    weights = dense + (expert_spec,) * 3
    return jax.shard_map(
        per_device,
        mesh=mesh,
        in_specs=(token_spec, row_spec, token_spec, token_spec, token_spec) + weights,
        out_specs=(token_spec, token_spec) + weights,
        check_vma=False,
    )
```

```python
import functools
import math

import jax
import jax.numpy as jnp
import numpy as np
from jax import lax
from jax.experimental import pallas as pl
from jax.experimental.pallas import tpu as pltpu
from jax.sharding import PartitionSpec as P

HEADS = 16
NOPE = 128
ROPE = 64
QD = NOPE + ROPE
KV_RANK = 512
V_DIM = 128
TOP = 6
MOST = 96

EPS = 1e-06
NEG = -1e30
THETA = 10000.0
SCALE = 1.0 / math.sqrt(QD)
KV_END = 2 * NOPE + V_DIM
QK_END = KV_END + ROPE
MESH = pl.DeviceIdType.MESH
BF = jnp.bfloat16
F32 = jnp.float32
VMEM_LIMIT = 60 * 2**20
COST = pl.CostEstimate(flops=0, bytes_accessed=2**20, transcendentals=0)


def norm_scale(values):
    return lax.rsqrt(jnp.mean(values * values, axis=-1, keepdims=True) + EPS)


def norm_back(values, inverse, gradient):
    return inverse * gradient - values * inverse * inverse * inverse * jnp.mean(
        gradient * values, axis=-1, keepdims=True
    )


def mm(a, b):
    return jnp.dot(a, b, preferred_element_type=F32)


def mm_tn(a, b):
    return lax.dot_general(a, b, (((0,), (0,)), ((), ())), preferred_element_type=F32)


def mm_nt(a, b):
    return lax.dot_general(a, b, (((1,), (1,)), ((), ())), preferred_element_type=F32)


def rope_tables(length):
    places = np.arange(length, dtype=np.float32)
    frequency = np.power(np.float32(THETA), np.arange(ROPE // 2, dtype=np.float32) * np.float32(-2.0 / ROPE))
    angles = places[:, None] * frequency[None, :].astype(np.float32)
    angles = np.concatenate([angles, angles], axis=-1)
    return jnp.asarray(np.cos(angles), F32), jnp.asarray(np.sin(angles), F32)


def ring_place():
    me = lax.axis_index("seq")
    core, chip = me % 2, me // 2
    z, y = chip // 2, chip % 2
    half = lax.axis_size("seq") // 4
    return me, core, jnp.where(y == 0, z, 2 * half - 1 - z), 2 * half


def ring_seq(r, core, n):
    low = r < n // 2
    return (jnp.where(low, r, n - 1 - r) * 2 + jnp.where(low, 0, 1)) * 2 + core


def greet(devices, across=False):
    barrier = pltpu.get_barrier_semaphore()
    for device in devices:
        pl.semaphore_signal(barrier, inc=1, device_id={"seq": device}, device_id_type=MESH)
    if across:
        other = 1 - lax.axis_index("fsdp")
        pl.semaphore_signal(barrier, inc=1, device_id={"fsdp": other}, device_id_type=MESH)
    pl.semaphore_wait(barrier, len(devices) + across)


def given(x):
    return (x, True)


def swap_arrays(swaps):
    return [x[0] if isinstance(x, tuple) else x for x in swaps]


def swap_shapes(swaps):
    shapes = [(x[0].shape[0] // 2, x[0].shape[1]) if isinstance(x, tuple) else x.shape for x in swaps]
    return [jax.ShapeDtypeStruct(shape, x.dtype) for shape, x in zip(shapes, swap_arrays(swaps))]


def swap_copies(gives, takes, sems):
    other = 1 - lax.axis_index("fsdp")

    def source(give, take):
        height = take.shape[0]
        return give if give.shape[0] == height else give.at[pl.ds(pl.multiple_of(other * height, height), height), :]

    return [
        pltpu.make_async_remote_copy(
            source(give, take), take, sems.at[i, 0], sems.at[i, 1], device_id={"fsdp": other}, device_id_type=MESH
        )
        for i, (give, take) in enumerate(zip(gives, takes))
    ]


def remote(src, dst, send, recv, device):
    return pltpu.make_async_remote_copy(src, dst, send, recv, device_id={"seq": device}, device_id_type=MESH)


def cast_pieces(rows):
    return next(pieces for pieces in (8, 4, 2, 1) if rows % (16 * pieces) == 0 or pieces == 1)


def cast_scratch(casts):
    shapes = []
    for x in casts:
        height = x.shape[0] // cast_pieces(x.shape[0])
        shapes += [
            pltpu.VMEM((2, height, x.shape[1]), F32),
            pltpu.VMEM((2, height, x.shape[1]), BF),
            pltpu.SemaphoreType.DMA((2,)),
            pltpu.SemaphoreType.DMA((2,)),
        ]
    return shapes


def cast_steps(sources, targets, scratch):
    for i, (source, target) in enumerate(zip(sources, targets)):
        wide, narrow, in_sem, out_sem = scratch[4 * i : 4 * i + 4]
        pieces = cast_pieces(source.shape[0])
        height = source.shape[0] // pieces

        def load(c):
            return pltpu.make_async_copy(source.at[pl.ds(c * height, height), :], wide.at[c % 2], in_sem.at[c % 2])

        def save(c):
            return pltpu.make_async_copy(narrow.at[c % 2], target.at[pl.ds(c * height, height), :], out_sem.at[c % 2])

        load(0).start()
        for c in range(pieces):
            if c + 1 < pieces:
                load(c + 1).start()
            load(c).wait()
            if c >= 2:
                save(c - 2).wait()
            narrow[c % 2] = wide[c % 2].astype(BF)
            save(c).start()
            yield
        for c in range(max(0, pieces - 2), pieces):
            save(c).wait()


def gather_kernel(n, cuts, actives, swaps, shared, casts, *refs):
    count = len(cuts)
    total = count + swaps
    x_refs, give_refs, wide_refs = refs[:count], refs[count:total], refs[total : total + casts]
    refs = refs[total + casts :]
    o_refs, take_refs, narrow_refs = refs[:count], refs[count:total], refs[total : total + casts]
    own_sem, local_sem, swap_sems, hand_sem = refs[total + casts : total + casts + 4]
    sems = refs[total + casts + 4 :]
    casting = cast_steps(wide_refs, narrow_refs, sems[4 * count :])
    me, core, r, _ = ring_place()
    targets = (ring_seq((r + 1) % n, core, n), ring_seq((r + n - 1) % n, core, n))
    sibling = ring_seq(r, 1 - core, n)
    greet((*targets, sibling), swaps > 0)

    def half_of(ref, c):
        height = ref.shape[0] // 2
        return ref.at[pl.ds(pl.multiple_of(c * height, height), height), :]

    gives, takes = list(give_refs), list(take_refs)
    if shared is not None:
        gives[shared], takes[shared] = half_of(gives[shared], core), half_of(takes[shared], core)
    swapped = swap_copies(gives, takes, swap_sems)
    for copy in swapped:
        copy.start()

    def handed(c):
        half = half_of(take_refs[shared], c)
        return remote(half, half, hand_sem.at[0], hand_sem.at[1], sibling)

    def block(t, d, c):
        return ring_seq((r + (-t if d == 0 else t) + n) % n, c, n)

    def guarded(i, source, action):
        if actives[i] is None:
            action()
        else:
            pl.when(actives[i](source))(action)

    def parts_of(i):
        height = x_refs[i].shape[0] // (2 * cuts[i])
        for k in range(cuts[i]):
            for d in range(2):
                yield k, d, pl.ds((d * cuts[i] + k) * height, height)

    def onward(i, t, d, k, rows):
        at = o_refs[i].at[block(t, d, core), rows]
        source = x_refs[i].at[rows] if t == 0 else at
        return remote(source, at, sems[4 * i].at[t, d, k], sems[4 * i + 1].at[t, d, k], targets[d])

    def across(i, t, d, k, rows, c):
        at = o_refs[i].at[block(t, d, c), rows]
        return remote(at, at, sems[4 * i + 2].at[t - 1, d, k], sems[4 * i + 3].at[t - 1, d, k], sibling)

    def local(i):
        return pltpu.make_async_copy(x_refs[i], o_refs[i].at[me], local_sem.at[i])

    def own(i):
        return remote(x_refs[i], o_refs[i].at[me], own_sem.at[i, 0], own_sem.at[i, 1], sibling)

    for i in range(count):
        local(i).start()
        for k, d, rows in parts_of(i):
            guarded(i, me, lambda: onward(i, 0, d, k, rows).start())
        guarded(i, me, lambda: own(i).start())
    for t in range(n - 1):
        for i in range(count):
            for k, d, rows in parts_of(i):

                def step():
                    arriving = onward(i, t, d, k, rows)
                    arriving.wait_recv()
                    if t < n - 2:
                        onward(i, t + 1, d, k, rows).start()
                    across(i, t + 1, d, k, rows, core).start()

                guarded(i, block(t + 1, d, core), step)
        for _ in range(4):
            next(casting, None)
    for _ in casting:
        pass
    for i in range(count):
        local(i).wait()
        guarded(i, me, lambda: own(i).wait_send())
        guarded(i, sibling, lambda: own(i).wait_recv())
        for t in range(n - 1):
            for k, d, rows in parts_of(i):
                guarded(i, block(t, d, core), lambda: onward(i, t, d, k, rows).wait_send())
                guarded(i, block(t + 1, d, core), lambda: across(i, t + 1, d, k, rows, core).wait_send())
                guarded(i, block(t + 1, d, 1 - core), lambda: across(i, t + 1, d, k, rows, 1 - core).wait_recv())
    if shared is not None:
        swapped[shared].wait_recv()
        handed(core).start()
    for i, copy in enumerate(swapped):
        copy.wait_send()
        if i != shared:
            copy.wait_recv()
    if shared is not None:
        handed(core).wait_send()
        handed(1 - core).wait_recv()


def ring_gather_many(operands, collective_id, actives=None, swaps=(), shared=None, casts=()):
    devices = lax.axis_size("seq")
    n = devices // 2
    cuts = [2 if x.shape[0] % 64 == 0 else 1 for x in operands]
    anywhere = pl.BlockSpec(memory_space=pl.ANY)
    sems = [pltpu.SemaphoreType.DMA((n - 1, 2, cut)) for cut in cuts for _ in range(4)]
    return pl.pallas_call(
        functools.partial(gather_kernel, n, cuts, actives or [None] * len(operands), len(swaps), shared, len(casts)),
        out_shape=[jax.ShapeDtypeStruct((devices, *x.shape), x.dtype) for x in operands]
        + swap_shapes(swaps)
        + [jax.ShapeDtypeStruct(x.shape, BF) for x in casts],
        in_specs=[anywhere] * (len(operands) + len(swaps) + len(casts)),
        out_specs=[anywhere] * (len(operands) + len(swaps) + len(casts)),
        scratch_shapes=[
            pltpu.SemaphoreType.DMA((len(operands), 2)),
            pltpu.SemaphoreType.DMA((len(operands),)),
            pltpu.SemaphoreType.DMA((max(1, len(swaps)), 2)),
            pltpu.SemaphoreType.DMA((2,)),
        ]
        + sems
        + cast_scratch(casts),
        compiler_params=pltpu.CompilerParams(
            collective_id=collective_id, has_side_effects=True, **({"vmem_limit_bytes": VMEM_LIMIT} if casts else {})
        ),
        cost_estimate=COST,
        name="ring_gather",
    )(*operands, *swap_arrays(swaps), *casts)


def ring_gather(x, collective_id, swaps=()):
    out, *taken = ring_gather_many([x], collective_id, None, swaps)
    return out.reshape(-1, x.shape[1]), taken


def scatter_kernel(n, cut, swaps, *refs):
    a_ref, w_ref = refs[:2]
    o_ref = refs[2 + swaps]
    stage, sibbuf, rbuf, sbuf, send, recv, fsend, frecv, swap_sems = refs[3 + 2 * swaps :]
    me, core, r, _ = ring_place()
    targets = (ring_seq((r + 1) % n, core, n), ring_seq((r + n - 1) % n, core, n))
    sibling = ring_seq(r, 1 - core, n)
    greet((*targets, sibling), swaps > 0)
    swapped = swap_copies(refs[2 : 2 + swaps], refs[3 + swaps : 3 + 2 * swaps], swap_sems)
    for copy in swapped:
        copy.start()
    height, columns = o_ref.shape
    spans = (pl.ds(0, cut), pl.ds(cut, columns - cut))

    def chip(t, d):
        return (r + (-t - 1 if d == 0 else t + 1) + n) % n

    def part(t, d, c):
        block = ring_seq(chip(t, d), c, n)
        rows = a_ref[pl.ds(block * height, height), :]
        return mm_nt(rows, w_ref[spans[d], :])

    def across(t, d):
        return remote(stage.at[t, :, spans[d]], sibbuf.at[t, :, spans[d]], fsend.at[t, d], frecv.at[t, d], sibling)

    def onward(t, d):
        return remote(sbuf.at[t, :, spans[d]], rbuf.at[t, :, spans[d]], send.at[t, d], recv.at[t, d], targets[d])

    def give(t, d):
        stage[t, :, spans[d]] = part(t, d, 1 - core).astype(BF)
        across(t, d).start()

    for d in range(2):
        give(0, d)
    for t in range(n):
        for d in range(2):
            if t < n - 1:
                give(t + 1, d)
            value = part(t, d, core)
            across(t, d).wait_recv()
            value = value + sibbuf[t, :, spans[d]].astype(F32)
            if t > 0:
                onward(t - 1, d).wait_recv()
                value = value + rbuf[t - 1, :, spans[d]].astype(F32)
            if t < n - 1:
                sbuf[t, :, spans[d]] = value.astype(BF)
                onward(t, d).start()
            else:
                o_ref[:, spans[d]] = value
    for t in range(n):
        for d in range(2):
            across(t, d).wait_send()
            if t < n - 1:
                onward(t, d).wait_send()
    for copy in swapped:
        copy.wait()


def ring_scatter(a, w, collective_id, swaps=()):
    devices = lax.axis_size("seq")
    n = devices // 2
    rows = a.shape[0] // devices
    columns = w.shape[0]
    cut = columns // 256 * 128
    vmem = pl.BlockSpec(memory_space=pltpu.VMEM)
    anywhere = [pl.BlockSpec(memory_space=pl.ANY)] * len(swaps)
    out, *taken = pl.pallas_call(
        functools.partial(scatter_kernel, n, cut, len(swaps)),
        out_shape=[jax.ShapeDtypeStruct((rows, columns), F32)] + swap_shapes(swaps),
        in_specs=[vmem, vmem] + anywhere,
        out_specs=[vmem] + anywhere,
        scratch_shapes=[
            pltpu.VMEM((n, rows, columns), BF),
            pltpu.VMEM((n, rows, columns), BF),
            pltpu.VMEM((n - 1, rows, columns), BF),
            pltpu.VMEM((n - 1, rows, columns), BF),
        ]
        + [pltpu.SemaphoreType.DMA((n - 1, 2))] * 2
        + [pltpu.SemaphoreType.DMA((n, 2))] * 2
        + [pltpu.SemaphoreType.DMA((max(1, len(swaps)), 2))],
        compiler_params=pltpu.CompilerParams(
            collective_id=collective_id, has_side_effects=True, vmem_limit_bytes=VMEM_LIMIT
        ),
        cost_estimate=COST,
        name="ring_scatter",
    )(a, w, *swap_arrays(swaps))
    return out, taken


def fsdp_gather(x, other=None):
    count = lax.axis_size("fsdp")
    if count != 2:
        return lax.all_gather(x, "fsdp", axis=0, tiled=True)
    first = lax.axis_index("fsdp") == 0
    return jnp.concatenate([jnp.where(first, x, other), jnp.where(first, other, x)], axis=0)


def fsdp_pick(x, owner, other):
    count = lax.axis_size("fsdp")
    if count != 2:
        return lax.dynamic_index_in_dim(lax.all_gather(x, "fsdp", axis=0), owner, 0, keepdims=False)
    return jnp.where(lax.axis_index("fsdp") == owner, x, other)


def fsdp_scatter(x, taken=None):
    if taken is None:
        return lax.psum_scatter(x.astype(BF), "fsdp", scatter_dimension=0, tiled=True).astype(F32)
    half = x.shape[0] // 2
    kept = lax.dynamic_slice_in_dim(x, lax.axis_index("fsdp") * half, half, 0)
    return kept.astype(F32) + taken.astype(F32)


def fsdp_sum(x, taken=None):
    return lax.psum(x, "fsdp") if taken is None else x + taken


def turn(values, cosine, sine):
    half = values.shape[-1] // 2
    turned = jnp.concatenate([-values[:, half:], values[:, :half]], axis=-1)
    return values * cosine + turned * sine


def turn_back(gradient, cosine, sine):
    half = gradient.shape[-1] // 2
    scaled = gradient * sine
    return gradient * cosine + jnp.concatenate([scaled[:, half:], -scaled[:, :half]], axis=-1)


def spans_of(length):
    step = length // 8
    for i in range(8):
        start = i * step
        yield start, step, max(0, start - (3 * step if i % 2 == 0 else 2 * step))


def allowed_of(seg_col, seg_row, start, step, low):
    width = start + step - low
    query = start + lax.broadcasted_iota(jnp.int32, (step, width), 0)
    key = low + lax.broadcasted_iota(jnp.int32, (step, width), 1)
    return (key <= query) & (seg_col[start : start + step, :] == seg_row[:, low : start + step])


def attend_block(start, step, low, qh_ref, kh_ref, v_ref, segc_ref, segr_ref, heads_ref, lse_ref):
    end = start + step
    scores = mm_nt(qh_ref[start:end, :], kh_ref[low:end, :]) * SCALE
    scores = jnp.where(allowed_of(segc_ref, segr_ref, start, step, low), scores, NEG)
    peak = jnp.max(scores, axis=-1, keepdims=True)
    raised = jnp.exp(scores - peak)
    total = jnp.sum(raised, axis=-1, keepdims=True)
    prob = (raised * (1.0 / total)).astype(BF)
    heads_ref[start:end, :] = mm(prob, v_ref[low:end, :]).astype(BF)
    lse_ref[start:end, :] = peak + jnp.log(total)


def weights_back(wb_ref, wq, we):
    width = wq.shape[0]
    rank = we.shape[0]
    wb_ref[:, :] = jnp.zeros(wb_ref.shape, BF)
    wb_ref[:width, :NOPE] = wq[:, :NOPE]
    wb_ref[:width, KV_END:QK_END] = wq[:, NOPE:]
    wb_ref[width : width + rank, NOPE:KV_END] = we[...]
    shape = (ROPE, 2 * ROPE)
    eye = lax.broadcasted_iota(jnp.int32, shape, 0) + ROPE == lax.broadcasted_iota(jnp.int32, shape, 1)
    wb_ref[width + rank : width + rank + ROPE, KV_END:] = eye.astype(F32).astype(BF)


def front_kernel(count, swaps, chunks, *refs):
    wq_parts, wl_parts, we_parts = refs[:count], refs[count : 2 * count], refs[2 * count : 3 * count]
    x_ref, gain_ref, lgain_ref, cos_ref, sin_ref, segc_ref, segr_ref = refs[3 * count : 3 * count + 7]
    refs = refs[3 * count + 7 :]
    gives, refs = refs[:swaps], refs[swaps:]
    act_ref, cn_ref, qh_ref, kh_ref, v_ref, heads_ref, lse_ref, wb_ref = refs[:8]
    takes, refs = refs[8 : 8 + swaps], refs[8 + swaps :]
    wq, wl, we, sems, swap_sems = refs
    i = pl.program_id(0)
    length = qh_ref.shape[0]
    step = length // chunks
    swapped = swap_copies(gives, takes, swap_sems) if swaps else []
    copies = [fill(p, w, sems.at[j]) for j, (p, w) in enumerate(((wq_parts, wq), (wl_parts, wl), (we_parts, we)))]
    start_first(copies)

    @pl.when(i == 0)
    def _():
        if swaps:
            greet((), True)
            for copy in swapped:
                copy.start()

    wait_first(copies)

    @pl.when(i < chunks)
    def _():
        rows = pl.ds(pl.multiple_of(i * step, step), step)
        x = x_ref[...].astype(F32)
        act_ref[...] = (x * norm_scale(x) * gain_ref[...]).astype(BF)
        cosine, sine = cos_ref[...], sin_ref[...]
        query = mm(act_ref[...], wq[...])
        qh_ref[rows, :NOPE] = query[:, :NOPE].astype(BF)
        qh_ref[rows, NOPE:] = turn(query[:, NOPE:].astype(BF).astype(F32), cosine, sine).astype(BF)
        latent = mm(act_ref[...], wl[...])
        comp = latent[:, :KV_RANK]
        cn_ref[...] = (comp * norm_scale(comp) * lgain_ref[...]).astype(BF)
        kh_ref[rows, NOPE:] = turn(latent[:, KV_RANK:].astype(BF).astype(F32), cosine, sine).astype(BF)
        kv = mm(cn_ref[...], we[...])
        kh_ref[rows, :NOPE] = kv[:, :NOPE].astype(BF)
        v_ref[rows, :] = kv[:, NOPE:].astype(BF)

    @pl.when(i == chunks)
    def _():
        for start, size, low in spans_of(length):
            attend_block(start, size, low, qh_ref, kh_ref, v_ref, segc_ref, segr_ref, heads_ref, lse_ref)
        weights_back(wb_ref, wq, we)
        for copy in swapped:
            copy.wait()


def front(pieces, x, gain, lgain, cosine, sine, seg_col, seg_row, swaps, collective_id):
    length, width = x.shape
    chunks = 4
    step = length // chunks
    count = len(pieces[0])
    vmem = pl.BlockSpec(memory_space=pltpu.VMEM)
    anywhere = pl.BlockSpec(memory_space=pl.ANY)

    def tile(columns):
        return pl.BlockSpec((step, columns), lambda i: (jnp.minimum(i, chunks - 1), 0))

    def held(rows, columns):
        return pl.BlockSpec((rows, columns), lambda i: (0, 0))

    full = lambda group: (group[0].shape[0] * count, group[0].shape[1])
    backs = (width + KV_RANK + 2 * ROPE, QK_END + ROPE)
    outs = [
        (tile(width), (length, width), BF),
        (tile(KV_RANK), (length, KV_RANK), BF),
        (held(length, QD), (length, QD), BF),
        (held(length, QD), (length, QD), BF),
        (held(length, V_DIM), (length, V_DIM), BF),
        (held(length, V_DIM), (length, V_DIM), BF),
        (held(length, 1), (length, 1), F32),
        (held(*backs), backs, BF),
    ]
    return pl.pallas_call(
        functools.partial(front_kernel, count, len(swaps), chunks),
        grid=(chunks + 1,),
        out_shape=[jax.ShapeDtypeStruct(shape, dtype) for _, shape, dtype in outs]
        + [jax.ShapeDtypeStruct(w.shape, w.dtype) for w in swaps],
        in_specs=[anywhere] * (3 * count) + [tile(width), vmem, vmem, tile(ROPE), tile(ROPE), vmem, vmem]
        + [anywhere] * len(swaps),
        out_specs=[spec for spec, _, _ in outs] + [anywhere] * len(swaps),
        scratch_shapes=[pltpu.VMEM(full(group), BF) for group in pieces]
        + [pltpu.SemaphoreType.DMA((3, count)), pltpu.SemaphoreType.DMA((max(1, len(swaps)), 2))],
        compiler_params=pltpu.CompilerParams(
            vmem_limit_bytes=VMEM_LIMIT, collective_id=collective_id, has_side_effects=len(swaps) > 0
        ),
        cost_estimate=COST,
        name="front",
    )(*sum(pieces, ()), x, gain, lgain, cosine, sine, seg_col, seg_row, *swaps)


def attend_back_kernel(
    qh_ref, kh_ref, v_ref, lse_ref, heads_ref, da_ref, wo_ref, cos_ref, sin_ref, segc_ref, segr_ref, back_ref, gout_ref, dk_acc, dv_acc
):
    dk_acc[...] = jnp.zeros_like(dk_acc)
    dv_acc[...] = jnp.zeros_like(dv_acc)
    for start, step, low in spans_of(qh_ref.shape[0]):
        end = start + step
        query = qh_ref[start:end, :]
        grad = mm_nt(da_ref[start:end, :], wo_ref[...]).astype(BF)
        keys = kh_ref[low:end, :]
        scores = mm_nt(query, keys) * SCALE
        allowed = allowed_of(segc_ref, segr_ref, start, step, low)
        prob = jnp.where(allowed, jnp.exp(scores - lse_ref[start:end, :]), 0.0)
        dv_acc[low:end, :] += mm_tn(prob.astype(BF), grad)
        dprob = mm_nt(grad, v_ref[low:end, :])
        delta = jnp.sum(prob * dprob, axis=-1, keepdims=True)
        dscore = (prob * (dprob - delta) * SCALE).astype(BF)
        dquery = mm(dscore, keys)
        back_ref[start:end, :NOPE] = dquery[:, :NOPE].astype(BF)
        turned = turn_back(dquery[:, NOPE:], cos_ref[start:end, :], sin_ref[start:end, :])
        back_ref[start:end, KV_END:QK_END] = turned.astype(BF)
        dk_acc[low:end, :] += mm_tn(dscore, query)
    back_ref[:, NOPE : 2 * NOPE] = dk_acc[:, :NOPE].astype(BF)
    back_ref[:, 2 * NOPE : KV_END] = dv_acc[...].astype(BF)
    back_ref[:, QK_END:] = turn_back(dk_acc[:, NOPE:], cos_ref[...], sin_ref[...]).astype(BF)
    gout_ref[...] = mm_tn(heads_ref[...], da_ref[...]).astype(BF)


def local_call(kernel, outs, scratch, name, *operands):
    vmem = pl.BlockSpec(memory_space=pltpu.VMEM)
    return pl.pallas_call(
        kernel,
        out_shape=[jax.ShapeDtypeStruct(shape, dtype) for shape, dtype in outs],
        in_specs=[vmem] * len(operands),
        out_specs=[vmem] * len(outs),
        scratch_shapes=scratch,
        compiler_params=pltpu.CompilerParams(vmem_limit_bytes=VMEM_LIMIT),
        cost_estimate=COST,
        name=name,
    )(*operands)


def fsdp_pieces(x, other):
    if lax.axis_size("fsdp") != 2:
        return (lax.all_gather(x, "fsdp", axis=0, tiled=True),)
    return (x, other)


def fill(pieces, dst, sems):
    if len(pieces) == 1:
        return [pltpu.make_async_copy(pieces[0], dst, sems.at[0])]
    part = lax.axis_index("fsdp")
    height = pieces[0].shape[0]
    starts = (part * height, (1 - part) * height)
    return [
        pltpu.make_async_copy(piece, dst.at[pl.ds(pl.multiple_of(start, height), height), :], sems.at[i])
        for i, (piece, start) in enumerate(zip(pieces, starts))
    ]


def picks(slot_ref, share_ref, b, most):
    slots = slot_ref[b]
    pick = slots == lax.broadcasted_iota(jnp.int32, (most, slots.shape[1]), 0)
    return pick.astype(BF), jnp.sum(jnp.where(pick, share_ref[b], 0.0), axis=-1, keepdims=True)


def hidden_spans(hidden):
    cut = -(-hidden // 256) * 128
    return ((0, cut), (cut, hidden))


def start_first(groups):
    @pl.when(pl.program_id(0) == 0)
    def _():
        for group in groups:
            for copy in group:
                copy.start()


def wait_first(groups):
    @pl.when(pl.program_id(0) == 0)
    def _():
        for group in groups:
            for copy in group:
                copy.wait()


def expert_in_kernel(count, most, swaps, *refs):
    wg_parts, wu_parts = refs[:count], refs[count : 2 * count]
    act_ref, slot_ref, share_ref, wsgu_ref, wsd_ref, g_ref = refs[2 * count : 2 * count + 6]
    gives, refs = refs[2 * count + 6 : 2 * count + 6 + swaps], refs[2 * count + 6 + swaps :]
    xe_ref, ge_ref, ue_ref, he_ref, sh_ref, dye_ref, dsgu_ref = refs[:7]
    takes, (wg, wu, sems, swap_sems) = refs[7 : 7 + swaps], refs[7 + swaps :]
    swapped = swap_copies(gives, takes, swap_sems) if swaps else []
    if swaps:

        @pl.when(pl.program_id(0) == 0)
        def _():
            greet((), True)
            for copy in swapped:
                copy.start()

    copies = [fill(wg_parts, wg, sems.at[0]), fill(wu_parts, wu, sems.at[1])]
    start_first(copies)
    blocks, rows = slot_ref.shape[0], slot_ref.shape[2]
    for b in range(blocks):
        pick, share = picks(slot_ref, share_ref, b, most)
        block, packed = slice(b * rows, (b + 1) * rows), slice(b * most, (b + 1) * most)
        xe_ref[packed, :] = mm(pick, act_ref[block, :]).astype(BF)
        dye_ref[packed, :] = (share * mm(pick, g_ref[block, :])).astype(BF)
    sgu = mm(act_ref[...], wsgu_ref[...])
    units = sh_ref.shape[1]
    sg, su = sgu[:, :units], sgu[:, units:]
    sig = jax.nn.sigmoid(sg)
    sh_ref[...] = (sg * sig * su).astype(BF)
    dsh = mm_nt(g_ref[...], wsd_ref[...])
    dsgu_ref[:, :units] = (dsh * su * sig * (1.0 + sg * (1.0 - sig))).astype(BF)
    dsgu_ref[:, units:] = (dsh * sg * sig).astype(BF)
    wait_first(copies)
    for low, high in hidden_spans(wg.shape[1]):
        ge = mm(xe_ref[...], wg[:, low:high])
        ue = mm(xe_ref[...], wu[:, low:high])
        ge_ref[:, low:high] = ge
        ue_ref[:, low:high] = ue
        he_ref[:, low:high] = (ge * jax.nn.sigmoid(ge) * ue).astype(BF)
    if swaps:

        @pl.when(pl.program_id(0) == pl.num_programs(0) - 1)
        def _():
            for copy in swapped:
                copy.wait()


def expert_out_kernel(count, most, swaps, *refs):
    wd_parts = refs[:count]
    he_ref, slot_ref, share_ref, wsd_ref, sh_ref, y_ref, wd, sems, _ = refs[count:]
    copies = [fill(wd_parts, wd, sems.at[0])]
    start_first(copies)
    wait_first(copies)
    blocks, rows = slot_ref.shape[0], slot_ref.shape[2]
    z = mm(he_ref[...], wd[...]).astype(BF)
    for b in range(blocks):
        pick, share = picks(slot_ref, share_ref, b, most)
        ye = z[b * most : (b + 1) * most, :].astype(F32)
        ys = mm(sh_ref[b * rows : (b + 1) * rows, :], wsd_ref[...])
        y_ref[b * rows : (b + 1) * rows, :] = (ys + mm_tn(pick, (share * ye).astype(BF))).astype(BF)


def expert_back_kernel(n, cut, count, most, swaps, *refs):
    wg_parts, wu_parts, wd_parts = refs[:count], refs[count : 2 * count], refs[2 * count : 3 * count]
    dye_ref, slot_ref, share_ref, wsgu_ref, part_ref, ge_ref, ue_ref, dsgu_ref = refs[3 * count : 3 * count + 8]
    dact_ref, dge_ref, due_ref, y_ref = refs[3 * count + 8 : 3 * count + 12]
    wg, wu, wd, sems, _, *buffers = refs[3 * count + 12 :]
    copies = [fill(p, w, sems.at[i]) for i, (p, w) in enumerate(((wg_parts, wg), (wu_parts, wu), (wd_parts, wd)))]
    start_first(copies)
    finish = scatter_in_grid(pl.program_id(0), n, cut, part_ref, y_ref, buffers)
    blocks, rows = slot_ref.shape[0], slot_ref.shape[2]
    wait_first(copies)
    for low, high in hidden_spans(wg.shape[1]):
        dhe = mm_nt(dye_ref[...], wd[low:high, :])
        ge, ue = ge_ref[:, low:high], ue_ref[:, low:high]
        sig = jax.nn.sigmoid(ge)
        dge_ref[:, low:high] = (dhe * ue * sig * (1.0 + ge * (1.0 - sig))).astype(BF)
        due_ref[:, low:high] = (dhe * ge * sig).astype(BF)
    dxe = (mm_nt(dge_ref[...], wg[...]) + mm_nt(due_ref[...], wu[...])).astype(BF)
    for b in range(blocks):
        pick, _ = picks(slot_ref, share_ref, b, most)
        block = slice(b * rows, (b + 1) * rows)
        shared = mm_nt(dsgu_ref[block, :], wsgu_ref[...])
        dact_ref[block, :] = (shared + mm_tn(pick, dxe[b * most : (b + 1) * most, :])).astype(BF)
    finish()


def expert_call(kernel, name, pieces, most, steps, slot, share, whole, tiled, outs, swaps=(), collective_id=None, summed=None):
    devices, rows = slot.shape[0], slot.shape[2]
    per = devices // steps
    anywhere = pl.BlockSpec(memory_space=pl.ANY)
    vmem = pl.BlockSpec(memory_space=pltpu.VMEM)

    def tile(total, columns):
        return pl.BlockSpec((total // steps, columns), lambda i: (i, 0))

    cut = pl.BlockSpec((per, 1, rows), lambda i: (i, 0, 0))
    count = len(pieces[0])
    full = lambda group: (group[0].shape[0] * count, group[0].shape[1])
    buffers, kept = [], []
    if summed is not None:
        buffers = scatter_buffers(devices // 2, *summed)
        kept = [(pl.BlockSpec(summed, lambda i: (0, 0)), jax.ShapeDtypeStruct(summed, F32))]
    return pl.pallas_call(
        functools.partial(kernel, count, most, len(swaps)),
        grid=(steps,),
        out_shape=[jax.ShapeDtypeStruct((total, columns), dtype) for total, columns, dtype in outs]
        + [shape for _, shape in kept]
        + [jax.ShapeDtypeStruct(x.shape, x.dtype) for x in swaps],
        in_specs=[anywhere] * (len(pieces) * count) + [tile(*tiled[0].shape), cut, cut] + [vmem] * len(whole)
        + [tile(*t.shape) for t in tiled[1:]]
        + [anywhere] * len(swaps),
        out_specs=[tile(total, columns) for total, columns, _ in outs]
        + [spec for spec, _ in kept]
        + [anywhere] * len(swaps),
        scratch_shapes=[pltpu.VMEM(full(group), BF) for group in pieces]
        + [pltpu.SemaphoreType.DMA((len(pieces), count)), pltpu.SemaphoreType.DMA((max(1, len(swaps)), 2))]
        + buffers,
        compiler_params=pltpu.CompilerParams(
            vmem_limit_bytes=VMEM_LIMIT, collective_id=collective_id, has_side_effects=collective_id is not None
        ),
        cost_estimate=COST,
        name=name,
    )(*sum(pieces, ()), tiled[0], slot, share, *whole, *tiled[1:], *swaps)


def trim(stacked, share):
    devices, room, width = stacked.shape
    if share % 8:
        return stacked[:, :share].reshape(-1, width).astype(F32)

    def kernel(i_ref, o_ref):
        for d in range(i_ref.shape[0]):
            o_ref[d * share : (d + 1) * share, :] = i_ref[d, :share, :].astype(F32)

    return pl.pallas_call(
        kernel,
        grid=(4,),
        out_shape=jax.ShapeDtypeStruct((devices * share, width), F32),
        in_specs=[pl.BlockSpec((devices // 4, room, width), lambda i: (i, 0, 0))],
        out_specs=pl.BlockSpec((devices // 4 * share, width), lambda i: (i, 0)),
        compiler_params=pltpu.CompilerParams(vmem_limit_bytes=VMEM_LIMIT),
        cost_estimate=COST,
        name="trim",
    )(stacked)


def scatter_in_grid(t, n, cut, part_ref, o_ref, buffers):
    sibbuf, rbuf, sbuf, send, recv, fsend, frecv = buffers
    me, core, r, _ = ring_place()
    targets = (ring_seq((r + 1) % n, core, n), ring_seq((r + n - 1) % n, core, n))
    sibling = ring_seq(r, 1 - core, n)
    columns = o_ref.shape[1]
    spans = (pl.ds(0, cut), pl.ds(cut, columns - cut))

    def block(step, d, c):
        return ring_seq((r + (-step - 1 if d == 0 else step + 1) + n) % n, c, n)

    def across(step, d):
        source = part_ref.at[block(step, d, 1 - core), :, spans[d]]
        return remote(source, sibbuf.at[step, :, spans[d]], fsend.at[step, d], frecv.at[step, d], sibling)

    def onward(step, d):
        return remote(
            sbuf.at[step, :, spans[d]], rbuf.at[step, :, spans[d]], send.at[step, d], recv.at[step, d], targets[d]
        )

    @pl.when(t == 0)
    def _():
        greet((*targets, sibling))
        for step in range(n):
            for d in range(2):
                across(step, d).start()

    for d in range(2):
        across(t, d).wait_recv()

        def both():
            return part_ref[block(t, d, core), :, spans[d]].astype(F32) + sibbuf[t, :, spans[d]].astype(F32)

        @pl.when(t == 0)
        def _():
            sbuf[0, :, spans[d]] = both().astype(BF)
            onward(0, d).start()

        @pl.when((t > 0) & (t < n - 1))
        def _():
            onward(t - 1, d).wait_recv()
            sbuf[t, :, spans[d]] = (both() + rbuf[t - 1, :, spans[d]].astype(F32)).astype(BF)
            onward(t, d).start()

        @pl.when(t == n - 1)
        def _():
            onward(n - 2, d).wait_recv()
            o_ref[:, spans[d]] = both() + rbuf[n - 2, :, spans[d]].astype(F32)

    def finish():
        @pl.when(t == n - 1)
        def _():
            for step in range(n):
                for d in range(2):
                    across(step, d).wait_send()
                    if step < n - 1:
                        onward(step, d).wait_send()

    return finish


def scatter_buffers(n, rows, columns):
    return (
        [pltpu.VMEM((n, rows, columns), BF), pltpu.VMEM((n - 1, rows, columns), BF), pltpu.VMEM((n - 1, rows, columns), BF)]
        + [pltpu.SemaphoreType.DMA((n - 1, 2))] * 2
        + [pltpu.SemaphoreType.DMA((n, 2))] * 2
    )


def weight_grads_kernel(n, cut, parts, *refs):
    xe_ref, dge_ref, due_ref, he_ref, dye_ref, act_ref, dsgu_ref, sh_ref, g_ref, part_ref = refs[:10]
    o_ref, gate_ref, up_ref, down_ref, sgu_ref, sdown_ref = refs[10:16]
    finish = scatter_in_grid(pl.program_id(0), n, cut, part_ref, o_ref, refs[16:])
    gate_ref[...] = mm_tn(xe_ref[...], dge_ref[...]).astype(BF)
    up_ref[...] = mm_tn(xe_ref[...], due_ref[...]).astype(BF)
    down_ref[...] = mm_tn(he_ref[...], dye_ref[...]).astype(BF)
    sgu_ref[...] = mm_tn(act_ref[...], dsgu_ref[...]).astype(BF)
    sdown = mm_tn(sh_ref[...], g_ref[...]).astype(BF)
    share = sdown.shape[0] // parts
    room = sdown_ref.shape[0] // parts
    for p in range(parts):
        sdown_ref[p * room : p * room + share, :] = sdown[p * share : (p + 1) * share, :]
        if room > share:
            sdown_ref[p * room + share : (p + 1) * room, :] = jnp.zeros((room - share, sdown.shape[1]), BF)

    finish()


def weight_grads(xe, dge, due, he, dye, act, dsgu, sh, g, part, parts, room, collective_id):
    devices = lax.axis_size("seq")
    n = devices // 2
    length, columns = part.shape
    rows = length // devices
    cut = columns // 256 * 128

    def tile(x):
        return pl.BlockSpec((x.shape[0], x.shape[1] // n), lambda i: (0, i))

    def held(x):
        return pl.BlockSpec(memory_space=pltpu.VMEM)

    ff, units = dge.shape[1], dsgu.shape[1]
    slab = columns // n
    down = lambda width: pl.BlockSpec((slab, width), lambda i: (i, 0))
    along = lambda height: pl.BlockSpec((height, slab), lambda i: (0, i))
    return pl.pallas_call(
        functools.partial(weight_grads_kernel, n, cut, parts),
        grid=(n,),
        out_shape=[jax.ShapeDtypeStruct((rows, columns), F32)]
        + [
            jax.ShapeDtypeStruct(shape, BF)
            for shape in ((columns, ff), (columns, ff), (ff, columns), (columns, units), (parts * room, columns))
        ],
        in_specs=[tile(xe), held(dge), held(due), held(he), tile(dye), tile(act), held(dsgu), held(sh), tile(g)]
        + [held(part)],
        out_specs=[pl.BlockSpec((rows, columns), lambda i: (0, 0)), down(ff), down(ff), along(ff)]
        + [down(units), along(parts * room)],
        scratch_shapes=scatter_buffers(n, rows, columns),
        compiler_params=pltpu.CompilerParams(
            collective_id=collective_id, has_side_effects=True, vmem_limit_bytes=VMEM_LIMIT
        ),
        cost_estimate=COST,
        name="weight_grads",
    )(xe, dge, due, he, dye, act, dsgu, sh, g, part.reshape(devices, rows, columns))


def widen(stacked, count, parts, name):
    devices, rows, columns = stacked.shape
    share = columns // parts // count
    width = devices * columns // count
    steps = 8

    def kernel(i_ref, *o_refs):
        for j, o_ref in enumerate(o_refs):
            for p in range(parts):
                for d in range(devices):
                    at, source = (p * devices + d) * share, (j * parts + p) * share
                    o_ref[:, at : at + share] = i_ref[d, :, source : source + share].astype(F32)

    return pl.pallas_call(
        kernel,
        grid=(steps,),
        out_shape=[jax.ShapeDtypeStruct((rows, width), F32)] * count,
        in_specs=[pl.BlockSpec((devices, rows // steps, columns), lambda i: (0, i, 0))],
        out_specs=[pl.BlockSpec((rows // steps, width), lambda i: (i, 0))] * count,
        compiler_params=pltpu.CompilerParams(vmem_limit_bytes=VMEM_LIMIT),
        cost_estimate=COST,
        name=name,
    )(stacked)


def columns_of(weight, at, width):
    return lax.dynamic_slice_in_dim(weight, at * width, width, 1).astype(BF)


def rows_of(weight, at, height):
    return lax.dynamic_slice_in_dim(weight, at * height, height, 0).astype(BF)


def per_device(
    tokens,
    segment_ids,
    routes,
    gate_weights,
    out_grad,
    attn_gain,
    q_weight,
    latent_weight,
    latent_gain,
    kv_weight,
    out_weight,
    ffn_gain,
    shared_gate,
    shared_up,
    shared_down,
    expert_gate,
    expert_up,
    expert_down,
):
    _, rows, width = tokens.shape
    devices = lax.axis_size("seq")
    at = lax.axis_index("seq")
    parts = lax.axis_size("fsdp")
    part = lax.axis_index("fsdp")
    length = rows * devices
    own_x = tokens[0]
    own_g = out_grad[0]

    per, per_latent = attn_gain.shape[0], latent_gain.shape[0]
    gains = jnp.concatenate([attn_gain, ffn_gain, latent_gain]).astype(BF)
    gains_size = gains.shape[0]
    gains_rows = -(-gains_size // 2048) * 16
    gains = jnp.pad(gains, (0, gains_rows * 128 - gains_size)).reshape(gains_rows, 128)
    out_rows = out_weight.shape[0]
    early_latent = 2
    early = (
        gains,
        columns_of(q_weight, at, QD),
        latent_weight.astype(BF),
        columns_of(kv_weight, at, NOPE + V_DIM),
        lax.dynamic_slice_in_dim(out_weight, at * V_DIM % out_rows, V_DIM, 0).astype(BF),
    )
    pair = parts == 2

    def crossing(*arrays):
        return arrays if pair else ()

    def crossed(taken, count):
        return taken if pair else [None] * count

    experts = jnp.arange(devices, dtype=jnp.int32)
    spread = jnp.sum(
        jnp.where(routes[0].T[None, :, :] == experts[:, None, None], gate_weights[0].T[None, :, :], 0.0), axis=1
    )
    x_all, spread_all, *others = ring_gather_many(
        [own_x, spread],
        8,
        None,
        crossing(*early),
        early_latent if pair else None,
        (expert_gate[0], expert_up[0], expert_down[0]),
    )
    others, (egate, eup, edown) = others[:-3], others[-3:]
    late_g, x_all = lax.optimization_barrier((own_g, x_all.reshape(length, width)))
    g_all = lax.all_gather(late_g, "seq", axis=0, tiled=True)
    share_of = lax.dynamic_index_in_dim(spread_all, at, 1, keepdims=False)
    others = crossed(others, len(early))
    gains = fsdp_gather(gains, others[0]).reshape(parts, -1)[:, :gains_size].astype(F32)
    gain_one = gains[:, :per].reshape(1, -1)
    gain_two = gains[:, per : 2 * per].reshape(1, -1)
    gain_lat = gains[:, 2 * per :].reshape(1, -1)
    w_latent = fsdp_gather(early[2], others[2])
    w_out = fsdp_pick(early[4], at * V_DIM // out_rows, others[4])

    hidden = shared_down.shape[0] * parts
    share = shared_down.shape[0] // devices

    def shared_columns(weight):
        pieces = [
            lax.dynamic_slice_in_dim(weight, p * (hidden // parts) + at * share, share, 1) for p in range(parts)
        ]
        return pieces

    share_pad = -(-share // 32) * 32
    sgu = jnp.concatenate(shared_columns(shared_gate) + shared_columns(shared_up), axis=1).astype(BF)
    sdown = jnp.pad(rows_of(shared_down, at, share), ((0, share_pad - share), (0, 0)))

    cosine, sine = rope_tables(length)
    seg_col, seg_row = segment_ids.reshape(length, 1), segment_ids
    act_one, cnorm, qh, kh, values, heads, lse, w_back, *taken = front(
        tuple(fsdp_pieces(early[i], others[i]) for i in (1, 2, 3)),
        x_all,
        gain_one,
        gain_lat,
        cosine,
        sine,
        seg_col,
        seg_row,
        crossing(sgu, sdown),
        11 if pair else None,
    )
    sgu_other, sdown_other = crossed(taken, 2)
    own_xf = own_x.astype(F32)
    attended, taken = ring_scatter(heads, w_out.T, 2, crossing(egate))
    (egate_other,) = crossed(taken, 1)
    x1 = own_xf + attended
    r3 = norm_scale(x1)
    act_two = (x1 * r3 * gain_two).astype(BF)
    act_all, taken = ring_gather(act_two, 9, crossing(eup))
    (eup_other,) = crossed(taken, 1)
    w_egate, w_eup = fsdp_pieces(egate, egate_other), fsdp_pieces(eup, eup_other)
    w_sgu = fsdp_gather(sgu, sgu_other)
    w_sdown = fsdp_gather(sdown[:share], sdown_other[:share] if pair else None)

    most = min(MOST, rows)
    named = share_of > 0.0
    rank = jnp.cumsum(named.astype(jnp.int32), axis=1) - 1
    slot = jnp.where(named, rank, -1)[:, None, :]
    share_of = share_of[:, None, :]
    packed = devices * most
    ff = expert_gate.shape[2]
    units = parts * share
    steps = 4
    xe, ge, ue, he, sh, dye, dsgu, *taken = expert_call(
        expert_in_kernel,
        "experts_in",
        (w_egate, w_eup),
        most,
        steps,
        slot,
        share_of,
        (w_sgu, w_sdown),
        (act_all, g_all),
        (
            (packed, width, BF),
            (packed, ff, F32),
            (packed, ff, F32),
            (packed, ff, BF),
            (length, units, BF),
            (packed, width, BF),
            (length, 2 * units, BF),
        ),
        crossing(edown),
        10 if pair else None,
    )
    (edown_other,) = crossed(taken, 1)
    w_edown = fsdp_pieces(edown, edown_other)
    (y_part,) = expert_call(
        expert_out_kernel,
        "experts_out",
        (w_edown,),
        most,
        steps,
        slot,
        share_of,
        (w_sdown,),
        (he, sh),
        ((length, width, BF),),
    )
    dact_part, dge, due, y_sum = expert_call(
        functools.partial(expert_back_kernel, devices // 2, width // 256 * 128),
        "experts_back",
        (w_egate, w_eup, w_edown),
        most,
        devices // 2,
        slot,
        share_of,
        (w_sgu, y_part.reshape(devices, rows, width)),
        (dye, ge, ue, dsgu),
        ((length, width, BF), (packed, ff, BF), (packed, ff, BF)),
        (),
        12,
        (rows, width),
    )
    dact_two, grad_egate, grad_eup, grad_edown, grad_sgu, grad_sdown = weight_grads(
        xe, dge, due, he, dye, act_all, dsgu, sh, g_all, dact_part, parts, share_pad, 3
    )
    own_gf = own_g.astype(F32)
    grad_gain_two = jnp.sum(dact_two * x1 * r3, axis=0)
    dx1 = own_gf + norm_back(x1, r3, dact_two * gain_two)
    dattn_all, taken = ring_gather(dx1.astype(BF), 1, (given(grad_sgu), given(grad_sdown)) if pair else ())
    sgu_taken, sdown_taken = crossed(taken, 2)
    grad_sgu = fsdp_scatter(grad_sgu, sgu_taken).astype(BF)
    grad_sdown = fsdp_scatter(grad_sdown, sdown_taken).astype(BF)
    output = (x1 + y_sum).astype(BF)

    back, grad_out = local_call(
        attend_back_kernel,
        [((length, QK_END + ROPE), BF), ((V_DIM, width), BF)],
        [pltpu.VMEM((length, QD), F32), pltpu.VMEM((length, V_DIM), F32)],
        "attend_back",
        qh,
        kh,
        values,
        lse,
        heads,
        dattn_all,
        w_out,
        cosine,
        sine,
        seg_col,
        seg_row,
    )
    grad_back = mm_tn(act_one, back).astype(BF)
    grad_query = jnp.concatenate([grad_back[:, :NOPE], grad_back[:, KV_END:QK_END]], 1)
    grad_expand = mm_tn(cnorm, back[:, NOPE:KV_END]).astype(BF)
    summed, taken = ring_scatter(back, w_back, 4, (given(grad_edown),) if pair else ())
    grad_edown = fsdp_scatter(grad_edown, *taken)

    r1 = norm_scale(own_xf)
    own_act = (own_xf * r1 * gain_one).astype(BF)
    own_comp = mm(own_act, w_latent)[:, :KV_RANK]
    r2 = norm_scale(own_comp)
    dcn = summed[:, width : width + KV_RANK]
    grad_gain_lat = jnp.sum(dcn * own_comp * r2, axis=0)
    dcomp = norm_back(own_comp, r2, dcn * gain_lat)
    dlatent = jnp.concatenate([dcomp, summed[:, width + KV_RANK : width + KV_RANK + ROPE]], axis=-1).astype(BF)
    dact_one = summed[:, :width] + mm_nt(dlatent, w_latent)
    grad_gain_one = jnp.sum(dact_one * own_xf * r1, axis=0)
    input_grad = dx1 + norm_back(own_xf, r1, dact_one * gain_one)

    small = jnp.concatenate([grad_gain_one, grad_gain_two, grad_gain_lat])
    small = jnp.pad(small, (0, 64 * 128 - small.shape[0])).reshape(64, 128)

    def in_part(device):
        return device * V_DIM // out_rows == lax.axis_index("fsdp")

    sgu_all, sdown_all, dlatent_all, *taken = ring_gather_many(
        [grad_sgu, grad_sdown, dlatent],
        5,
        None,
        (given(grad_query), given(grad_expand), grad_out, small, given(grad_egate)) if pair else (),
    )
    query_taken, expand_taken, out_taken, small_taken, egate_taken = crossed(taken, 5)
    grad_query = fsdp_scatter(grad_query, query_taken).astype(BF)
    grad_expand = fsdp_scatter(grad_expand, expand_taken).astype(BF)
    grad_out = fsdp_sum(grad_out, out_taken)
    small = fsdp_sum(small, small_taken)
    grad_egate = fsdp_scatter(grad_egate, egate_taken)
    slab = width // parts // devices
    act_cols = jnp.concatenate(
        [lax.dynamic_slice_in_dim(act_one, p * (width // parts) + at * slab, slab, 1) for p in range(parts)], axis=1
    )
    grad_latent = mm_tn(act_cols, dlatent_all.reshape(length, -1)).astype(BF)
    latent_taken = None
    if pair:
        latent_taken = lax.ppermute(
            lax.dynamic_slice_in_dim(grad_latent, (1 - part) * slab, slab, 0), "fsdp", [(0, 1), (1, 0)]
        )
    grad_latent = fsdp_scatter(grad_latent, latent_taken).astype(BF)
    latent_pad = -(-slab // 32) * 32
    query_all, expand_all, out_all, latent_all, small_all, *taken = ring_gather_many(
        [grad_query, grad_expand, grad_out, jnp.pad(grad_latent, ((0, latent_pad - slab), (0, 0))), small],
        7,
        [None, None, in_part, None, None],
        (given(grad_eup),) if pair else (),
    )
    (eup_taken,) = crossed(taken, 1)
    grad_eup = fsdp_scatter(grad_eup, eup_taken)
    latent_all = latent_all[:, :slab]
    out_grad_own = lax.dynamic_slice_in_dim(
        out_all.reshape(devices * V_DIM, width), part * out_rows, out_rows, 0
    ).astype(F32)
    small = jnp.sum(small_all, axis=0).reshape(-1)
    wide_gate, wide_up = widen(sgu_all, 2, parts, "wide_shared")
    gain_rows = width // parts
    own_gains = [
        lax.dynamic_slice_in_dim(small, part * gain_rows, gain_rows),
        lax.dynamic_slice_in_dim(small, width + part * gain_rows, gain_rows),
        lax.dynamic_slice_in_dim(small, 2 * width + part * (KV_RANK // parts), KV_RANK // parts),
    ]
    return (
        output[None],
        input_grad[None],
        own_gains[0],
        widen(query_all, 1, 1, "wide_q")[0],
        latent_all.reshape(-1, grad_latent.shape[1]).astype(F32),
        own_gains[2],
        widen(expand_all, 1, 1, "wide_kv")[0],
        out_grad_own,
        own_gains[1],
        wide_gate,
        wide_up,
        trim(sdown_all, share),
        grad_egate[None],
        grad_eup[None],
        grad_edown[None],
    )


def solution(mesh):
    token_spec = P("fsdp", "seq", None)
    row_spec = P("fsdp", None)
    gain_spec = P("fsdp")
    expert_spec = P("seq", "fsdp", None)
    dense = (gain_spec, row_spec, row_spec, gain_spec, row_spec, row_spec, gain_spec, row_spec, row_spec, row_spec)
    weights = dense + (expert_spec,) * 3
    return jax.shard_map(
        per_device,
        mesh=mesh,
        in_specs=(token_spec, row_spec, token_spec, token_spec, token_spec) + weights,
        out_specs=(token_spec, token_spec) + weights,
        check_vma=False,
    )
```

```python
import functools
import math

import jax
import jax.numpy as jnp
import numpy as np
from jax import lax
from jax.experimental import pallas as pl
from jax.experimental.pallas import tpu as pltpu
from jax.sharding import PartitionSpec as P

HEADS = 16
NOPE = 128
ROPE = 64
QD = NOPE + ROPE
KV_RANK = 512
V_DIM = 128
TOP = 6
MOST = 96

EPS = 1e-06
NEG = -1e30
THETA = 10000.0
SCALE = 1.0 / math.sqrt(QD)
KV_END = 2 * NOPE + V_DIM
QK_END = KV_END + ROPE
MESH = pl.DeviceIdType.MESH
BF = jnp.bfloat16
F32 = jnp.float32
VMEM_LIMIT = 60 * 2**20
COST = pl.CostEstimate(flops=0, bytes_accessed=2**20, transcendentals=0)


def norm_scale(values):
    return lax.rsqrt(jnp.mean(values * values, axis=-1, keepdims=True) + EPS)


def norm_back(values, inverse, gradient):
    return inverse * gradient - values * inverse * inverse * inverse * jnp.mean(
        gradient * values, axis=-1, keepdims=True
    )


def mm(a, b):
    return jnp.dot(a, b, preferred_element_type=F32)


def mm_tn(a, b):
    return lax.dot_general(a, b, (((0,), (0,)), ((), ())), preferred_element_type=F32)


def mm_nt(a, b):
    return lax.dot_general(a, b, (((1,), (1,)), ((), ())), preferred_element_type=F32)


def rope_tables(length):
    places = np.arange(length, dtype=np.float32)
    frequency = np.power(np.float32(THETA), np.arange(ROPE // 2, dtype=np.float32) * np.float32(-2.0 / ROPE))
    angles = places[:, None] * frequency[None, :].astype(np.float32)
    angles = np.concatenate([angles, angles], axis=-1)
    return jnp.asarray(np.cos(angles), F32), jnp.asarray(np.sin(angles), F32)


def ring_place():
    me = lax.axis_index("seq")
    core, chip = me % 2, me // 2
    z, y = chip // 2, chip % 2
    half = lax.axis_size("seq") // 4
    return me, core, jnp.where(y == 0, z, 2 * half - 1 - z), 2 * half


def ring_seq(r, core, n):
    low = r < n // 2
    return (jnp.where(low, r, n - 1 - r) * 2 + jnp.where(low, 0, 1)) * 2 + core


def greet(devices, across=False):
    barrier = pltpu.get_barrier_semaphore()
    for device in devices:
        pl.semaphore_signal(barrier, inc=1, device_id={"seq": device}, device_id_type=MESH)
    if across:
        other = 1 - lax.axis_index("fsdp")
        pl.semaphore_signal(barrier, inc=1, device_id={"fsdp": other}, device_id_type=MESH)
    pl.semaphore_wait(barrier, len(devices) + across)


def given(x):
    return (x, True)


def swap_arrays(swaps):
    return [x[0] if isinstance(x, tuple) else x for x in swaps]


def swap_shapes(swaps):
    shapes = [(x[0].shape[0] // 2, x[0].shape[1]) if isinstance(x, tuple) else x.shape for x in swaps]
    return [jax.ShapeDtypeStruct(shape, x.dtype) for shape, x in zip(shapes, swap_arrays(swaps))]


def swap_copies(gives, takes, sems):
    other = 1 - lax.axis_index("fsdp")

    def source(give, take):
        height = take.shape[0]
        return give if give.shape[0] == height else give.at[pl.ds(pl.multiple_of(other * height, height), height), :]

    return [
        pltpu.make_async_remote_copy(
            source(give, take), take, sems.at[i, 0], sems.at[i, 1], device_id={"fsdp": other}, device_id_type=MESH
        )
        for i, (give, take) in enumerate(zip(gives, takes))
    ]


def remote(src, dst, send, recv, device):
    return pltpu.make_async_remote_copy(src, dst, send, recv, device_id={"seq": device}, device_id_type=MESH)


def cast_pieces(rows):
    return next(pieces for pieces in (8, 4, 2, 1) if rows % (16 * pieces) == 0 or pieces == 1)


def cast_scratch(casts):
    shapes = []
    for x in casts:
        height = x.shape[0] // cast_pieces(x.shape[0])
        shapes += [
            pltpu.VMEM((2, height, x.shape[1]), F32),
            pltpu.VMEM((2, height, x.shape[1]), BF),
            pltpu.SemaphoreType.DMA((2,)),
            pltpu.SemaphoreType.DMA((2,)),
        ]
    return shapes


def cast_steps(sources, targets, scratch):
    for i, (source, target) in enumerate(zip(sources, targets)):
        wide, narrow, in_sem, out_sem = scratch[4 * i : 4 * i + 4]
        pieces = cast_pieces(source.shape[0])
        height = source.shape[0] // pieces

        def load(c):
            return pltpu.make_async_copy(source.at[pl.ds(c * height, height), :], wide.at[c % 2], in_sem.at[c % 2])

        def save(c):
            return pltpu.make_async_copy(narrow.at[c % 2], target.at[pl.ds(c * height, height), :], out_sem.at[c % 2])

        load(0).start()
        for c in range(pieces):
            if c + 1 < pieces:
                load(c + 1).start()
            load(c).wait()
            if c >= 2:
                save(c - 2).wait()
            narrow[c % 2] = wide[c % 2].astype(BF)
            save(c).start()
            yield
        for c in range(max(0, pieces - 2), pieces):
            save(c).wait()


def neighbours(n):
    _, core, r, _ = ring_place()
    return ring_seq((r + 1) % n, core, n), ring_seq((r + n - 1) % n, core, n), ring_seq(r, 1 - core, n)


def gather_steps(n, cuts, actives, x_refs, o_refs, own_sem, local_sem, sems):
    count = len(cuts)
    me, core, r, _ = ring_place()
    *targets, sibling = neighbours(n)

    def block(t, d, c):
        return ring_seq((r + (-t if d == 0 else t) + n) % n, c, n)

    def guarded(i, source, action):
        if actives[i] is None:
            action()
        else:
            pl.when(actives[i](source))(action)

    def parts_of(i):
        height = x_refs[i].shape[0] // (2 * cuts[i])
        for k in range(cuts[i]):
            for d in range(2):
                yield k, d, pl.ds((d * cuts[i] + k) * height, height)

    def onward(i, t, d, k, rows):
        at = o_refs[i].at[block(t, d, core), rows]
        source = x_refs[i].at[rows] if t == 0 else at
        return remote(source, at, sems[4 * i].at[t, d, k], sems[4 * i + 1].at[t, d, k], targets[d])

    def across(i, t, d, k, rows, c):
        at = o_refs[i].at[block(t, d, c), rows]
        return remote(at, at, sems[4 * i + 2].at[t - 1, d, k], sems[4 * i + 3].at[t - 1, d, k], sibling)

    def local(i):
        return pltpu.make_async_copy(x_refs[i], o_refs[i].at[me], local_sem.at[i])

    def own(i):
        return remote(x_refs[i], o_refs[i].at[me], own_sem.at[i, 0], own_sem.at[i, 1], sibling)

    for i in range(count):
        local(i).start()
        for k, d, rows in parts_of(i):
            guarded(i, me, lambda: onward(i, 0, d, k, rows).start())
        guarded(i, me, lambda: own(i).start())
    yield
    for t in range(n - 1):
        for i in range(count):
            for k, d, rows in parts_of(i):

                def step():
                    onward(i, t, d, k, rows).wait_recv()
                    if t < n - 2:
                        onward(i, t + 1, d, k, rows).start()
                    across(i, t + 1, d, k, rows, core).start()

                guarded(i, block(t + 1, d, core), step)
        yield
    for i in range(count):
        local(i).wait()
        guarded(i, me, lambda: own(i).wait_send())
        guarded(i, sibling, lambda: own(i).wait_recv())
        for t in range(n - 1):
            for k, d, rows in parts_of(i):
                guarded(i, block(t, d, core), lambda: onward(i, t, d, k, rows).wait_send())
                guarded(i, block(t + 1, d, core), lambda: across(i, t + 1, d, k, rows, core).wait_send())
                guarded(i, block(t + 1, d, 1 - core), lambda: across(i, t + 1, d, k, rows, 1 - core).wait_recv())


def gather_cut(height):
    return 2 if height % 64 == 0 else 1


def gather_sems(n, cuts):
    return [pltpu.SemaphoreType.DMA((n - 1, 2, cut)) for cut in cuts for _ in range(4)]


def gather_kernel(n, cuts, actives, swaps, shared, casts, *refs):
    count = len(cuts)
    total = count + swaps
    x_refs, give_refs, wide_refs = refs[:count], refs[count:total], refs[total : total + casts]
    refs = refs[total + casts :]
    o_refs, take_refs, narrow_refs = refs[:count], refs[count:total], refs[total : total + casts]
    own_sem, local_sem, swap_sems, hand_sem = refs[total + casts : total + casts + 4]
    sems = refs[total + casts + 4 :]
    casting = cast_steps(wide_refs, narrow_refs, sems[4 * count :])
    _, core, _, _ = ring_place()
    greet(neighbours(n), swaps > 0)
    sibling = neighbours(n)[2]

    def half_of(ref, c):
        height = ref.shape[0] // 2
        return ref.at[pl.ds(pl.multiple_of(c * height, height), height), :]

    gives, takes = list(give_refs), list(take_refs)
    if shared is not None:
        gives[shared], takes[shared] = half_of(gives[shared], core), half_of(takes[shared], core)
    swapped = swap_copies(gives, takes, swap_sems)
    for copy in swapped:
        copy.start()

    def handed(c):
        half = half_of(take_refs[shared], c)
        return remote(half, half, hand_sem.at[0], hand_sem.at[1], sibling)

    steps = gather_steps(n, cuts, actives, x_refs, o_refs, own_sem, local_sem, sems)
    next(steps)
    for _ in range(n - 1):
        next(steps)
        for _ in range(4):
            next(casting, None)
    for _ in casting:
        pass
    for _ in steps:
        pass
    if shared is not None:
        swapped[shared].wait_recv()
        handed(core).start()
    for i, copy in enumerate(swapped):
        copy.wait_send()
        if i != shared:
            copy.wait_recv()
    if shared is not None:
        handed(core).wait_send()
        handed(1 - core).wait_recv()


def ring_gather_many(operands, collective_id, actives=None, swaps=(), shared=None, casts=()):
    devices = lax.axis_size("seq")
    n = devices // 2
    cuts = [gather_cut(x.shape[0]) for x in operands]
    anywhere = pl.BlockSpec(memory_space=pl.ANY)
    sems = gather_sems(n, cuts)
    return pl.pallas_call(
        functools.partial(gather_kernel, n, cuts, actives or [None] * len(operands), len(swaps), shared, len(casts)),
        out_shape=[jax.ShapeDtypeStruct((devices, *x.shape), x.dtype) for x in operands]
        + swap_shapes(swaps)
        + [jax.ShapeDtypeStruct(x.shape, BF) for x in casts],
        in_specs=[anywhere] * (len(operands) + len(swaps) + len(casts)),
        out_specs=[anywhere] * (len(operands) + len(swaps) + len(casts)),
        scratch_shapes=[
            pltpu.SemaphoreType.DMA((len(operands), 2)),
            pltpu.SemaphoreType.DMA((len(operands),)),
            pltpu.SemaphoreType.DMA((max(1, len(swaps)), 2)),
            pltpu.SemaphoreType.DMA((2,)),
        ]
        + sems
        + cast_scratch(casts),
        compiler_params=pltpu.CompilerParams(
            collective_id=collective_id, has_side_effects=True, **({"vmem_limit_bytes": VMEM_LIMIT} if casts else {})
        ),
        cost_estimate=COST,
        name="ring_gather",
    )(*operands, *swap_arrays(swaps), *casts)


def ring_gather(x, collective_id, swaps=()):
    out, *taken = ring_gather_many([x], collective_id, None, swaps)
    return out.reshape(-1, x.shape[1]), taken


def scatter_kernel(n, cut, swaps, beside, *refs):
    a_ref, w_ref = refs[:2]
    gives, refs = refs[2 : 2 + swaps], refs[2 + swaps :]
    if beside:
        act_hbm, cn_hbm, *refs = refs
    o_ref, takes, refs = refs[0], refs[1 : 1 + swaps], refs[1 + swaps :]
    if beside:
        nope_ref, rope_ref, expand_ref, *refs = refs
    stage, sibbuf, rbuf, sbuf, send, recv, fsend, frecv, swap_sems, *refs = refs
    if beside:
        act, cn, sems = refs
        loads = [pltpu.make_async_copy(act_hbm, act, sems.at[0]), pltpu.make_async_copy(cn_hbm, cn, sems.at[1])]
        for load in loads:
            load.start()
    me, core, r, _ = ring_place()
    targets = (ring_seq((r + 1) % n, core, n), ring_seq((r + n - 1) % n, core, n))
    sibling = ring_seq(r, 1 - core, n)
    greet((*targets, sibling), swaps > 0)
    swapped = swap_copies(gives, takes, swap_sems)
    for copy in swapped:
        copy.start()
    height, columns = o_ref.shape
    spans = (pl.ds(0, cut), pl.ds(cut, columns - cut))

    def chip(t, d):
        return (r + (-t - 1 if d == 0 else t + 1) + n) % n

    def part(t, d, c):
        block = ring_seq(chip(t, d), c, n)
        rows = a_ref[pl.ds(block * height, height), :]
        return mm_nt(rows, w_ref[spans[d], :])

    def across(t, d):
        return remote(stage.at[t, :, spans[d]], sibbuf.at[t, :, spans[d]], fsend.at[t, d], frecv.at[t, d], sibling)

    def onward(t, d):
        return remote(sbuf.at[t, :, spans[d]], rbuf.at[t, :, spans[d]], send.at[t, d], recv.at[t, d], targets[d])

    def give(t, d):
        stage[t, :, spans[d]] = part(t, d, 1 - core).astype(BF)
        across(t, d).start()

    for d in range(2):
        give(0, d)
    for t in range(n):
        for d in range(2):
            if t < n - 1:
                give(t + 1, d)
            value = part(t, d, core)
            across(t, d).wait_recv()
            value = value + sibbuf[t, :, spans[d]].astype(F32)
            if t > 0:
                onward(t - 1, d).wait_recv()
                value = value + rbuf[t - 1, :, spans[d]].astype(F32)
            if t < n - 1:
                sbuf[t, :, spans[d]] = value.astype(BF)
                onward(t, d).start()
            else:
                o_ref[:, spans[d]] = value
        if beside and t == 0:
            for load in loads:
                load.wait()
        if beside:
            slab = act.shape[1] // n
            rows = slice(t * slab, (t + 1) * slab)
            grad = mm_tn(act[:, rows], a_ref[...])
            nope_ref[rows, :] = grad[:, :NOPE].astype(BF)
            rope_ref[rows, :] = grad[:, KV_END:QK_END].astype(BF)
        if beside and t == 1:
            expand_ref[...] = mm_tn(cn[...], a_ref[:, NOPE:KV_END]).astype(BF)
    for t in range(n):
        for d in range(2):
            across(t, d).wait_send()
            if t < n - 1:
                onward(t, d).wait_send()
    for copy in swapped:
        copy.wait()


def ring_scatter(a, w, collective_id, swaps=(), beside=()):
    devices = lax.axis_size("seq")
    n = devices // 2
    rows = a.shape[0] // devices
    columns = w.shape[0]
    cut = columns // 256 * 128
    vmem = pl.BlockSpec(memory_space=pltpu.VMEM)
    anywhere = [pl.BlockSpec(memory_space=pl.ANY)] * len(swaps)
    grads, held = [], []
    if beside:
        width, rank = (x.shape[1] for x in beside)
        grads = [jax.ShapeDtypeStruct(shape, BF) for shape in ((width, NOPE), (width, ROPE), (rank, NOPE + V_DIM))]
        held = [pltpu.VMEM(x.shape, BF) for x in beside] + [pltpu.SemaphoreType.DMA((2,))]
    out, *taken = pl.pallas_call(
        functools.partial(scatter_kernel, n, cut, len(swaps), len(beside) > 0),
        out_shape=[jax.ShapeDtypeStruct((rows, columns), F32)] + swap_shapes(swaps) + grads,
        in_specs=[vmem, vmem] + anywhere + [pl.BlockSpec(memory_space=pl.ANY)] * len(beside),
        out_specs=[vmem] + anywhere + [vmem] * len(grads),
        scratch_shapes=[
            pltpu.VMEM((n, rows, columns), BF),
            pltpu.VMEM((n, rows, columns), BF),
            pltpu.VMEM((n - 1, rows, columns), BF),
            pltpu.VMEM((n - 1, rows, columns), BF),
        ]
        + [pltpu.SemaphoreType.DMA((n - 1, 2))] * 2
        + [pltpu.SemaphoreType.DMA((n, 2))] * 2
        + [pltpu.SemaphoreType.DMA((max(1, len(swaps)), 2))]
        + held,
        compiler_params=pltpu.CompilerParams(
            collective_id=collective_id, has_side_effects=True, vmem_limit_bytes=VMEM_LIMIT
        ),
        cost_estimate=COST,
        name="ring_scatter",
    )(a, w, *swap_arrays(swaps), *beside)
    return (out, *taken[len(swaps) :], taken[: len(swaps)])


def fsdp_gather(x, other=None):
    count = lax.axis_size("fsdp")
    if count != 2:
        return lax.all_gather(x, "fsdp", axis=0, tiled=True)
    first = lax.axis_index("fsdp") == 0
    return jnp.concatenate([jnp.where(first, x, other), jnp.where(first, other, x)], axis=0)


def fsdp_pick(x, owner, other):
    count = lax.axis_size("fsdp")
    if count != 2:
        return lax.dynamic_index_in_dim(lax.all_gather(x, "fsdp", axis=0), owner, 0, keepdims=False)
    return jnp.where(lax.axis_index("fsdp") == owner, x, other)


def fsdp_scatter(x, taken=None):
    if taken is None:
        return lax.psum_scatter(x.astype(BF), "fsdp", scatter_dimension=0, tiled=True).astype(F32)
    half = x.shape[0] // 2
    kept = lax.dynamic_slice_in_dim(x, lax.axis_index("fsdp") * half, half, 0)
    return kept.astype(F32) + taken.astype(F32)


def fsdp_sum(x, taken=None):
    return lax.psum(x, "fsdp") if taken is None else x + taken


def turn(values, cosine, sine):
    half = values.shape[-1] // 2
    turned = jnp.concatenate([-values[:, half:], values[:, :half]], axis=-1)
    return values * cosine + turned * sine


def turn_back(gradient, cosine, sine):
    half = gradient.shape[-1] // 2
    scaled = gradient * sine
    return gradient * cosine + jnp.concatenate([scaled[:, half:], -scaled[:, :half]], axis=-1)


def spans_of(length):
    step = length // 8
    for i in range(8):
        start = i * step
        yield start, step, max(0, start - (3 * step if i % 2 == 0 else 2 * step))


def allowed_of(seg_col, seg_row, start, step, low):
    width = start + step - low
    query = start + lax.broadcasted_iota(jnp.int32, (step, width), 0)
    key = low + lax.broadcasted_iota(jnp.int32, (step, width), 1)
    return (key <= query) & (seg_col[start : start + step, :] == seg_row[:, low : start + step])


def attend_block(start, step, low, qh_ref, kh_ref, v_ref, segc_ref, segr_ref, heads_ref, lse_ref):
    end = start + step
    scores = mm_nt(qh_ref[start:end, :], kh_ref[low:end, :]) * SCALE
    scores = jnp.where(allowed_of(segc_ref, segr_ref, start, step, low), scores, NEG)
    peak = jnp.max(scores, axis=-1, keepdims=True)
    raised = jnp.exp(scores - peak)
    total = jnp.sum(raised, axis=-1, keepdims=True)
    prob = (raised * (1.0 / total)).astype(BF)
    heads_ref[start:end, :] = mm(prob, v_ref[low:end, :]).astype(BF)
    lse_ref[start:end, :] = peak + jnp.log(total)


def weights_back(wb_ref, wq, we):
    width = wq.shape[0]
    rank = we.shape[0]
    wb_ref[:, :] = jnp.zeros(wb_ref.shape, BF)
    wb_ref[:width, :NOPE] = wq[:, :NOPE]
    wb_ref[:width, KV_END:QK_END] = wq[:, NOPE:]
    wb_ref[width : width + rank, NOPE:KV_END] = we[...]
    shape = (ROPE, 2 * ROPE)
    eye = lax.broadcasted_iota(jnp.int32, shape, 0) + ROPE == lax.broadcasted_iota(jnp.int32, shape, 1)
    wb_ref[width + rank : width + rank + ROPE, KV_END:] = eye.astype(F32).astype(BF)


def front_kernel(count, swaps, chunks, *refs):
    wq_parts, wl_parts, we_parts = refs[:count], refs[count : 2 * count], refs[2 * count : 3 * count]
    x_ref, gain_ref, lgain_ref, cos_ref, sin_ref, segc_ref, segr_ref = refs[3 * count : 3 * count + 7]
    refs = refs[3 * count + 7 :]
    gives, refs = refs[:swaps], refs[swaps:]
    act_ref, cn_ref, qh_ref, kh_ref, v_ref, heads_ref, lse_ref, wb_ref = refs[:8]
    takes, refs = refs[8 : 8 + swaps], refs[8 + swaps :]
    wq, wl, we, sems, swap_sems = refs
    i = pl.program_id(0)
    length = qh_ref.shape[0]
    step = length // chunks
    swapped = swap_copies(gives, takes, swap_sems) if swaps else []
    copies = [fill(p, w, sems.at[j]) for j, (p, w) in enumerate(((wq_parts, wq), (wl_parts, wl), (we_parts, we)))]
    start_first(copies)

    @pl.when(i == 0)
    def _():
        if swaps:
            greet((), True)
            for copy in swapped:
                copy.start()

    wait_first(copies)

    @pl.when(i < chunks)
    def _():
        rows = pl.ds(pl.multiple_of(i * step, step), step)
        x = x_ref[...].astype(F32)
        act_ref[...] = (x * norm_scale(x) * gain_ref[...]).astype(BF)
        cosine, sine = cos_ref[...], sin_ref[...]
        query = mm(act_ref[...], wq[...])
        qh_ref[rows, :NOPE] = query[:, :NOPE].astype(BF)
        qh_ref[rows, NOPE:] = turn(query[:, NOPE:].astype(BF).astype(F32), cosine, sine).astype(BF)
        latent = mm(act_ref[...], wl[...])
        comp = latent[:, :KV_RANK]
        cn_ref[...] = (comp * norm_scale(comp) * lgain_ref[...]).astype(BF)
        kh_ref[rows, NOPE:] = turn(latent[:, KV_RANK:].astype(BF).astype(F32), cosine, sine).astype(BF)
        kv = mm(cn_ref[...], we[...])
        kh_ref[rows, :NOPE] = kv[:, :NOPE].astype(BF)
        v_ref[rows, :] = kv[:, NOPE:].astype(BF)

    @pl.when(i == chunks)
    def _():
        for start, size, low in spans_of(length):
            attend_block(start, size, low, qh_ref, kh_ref, v_ref, segc_ref, segr_ref, heads_ref, lse_ref)
        weights_back(wb_ref, wq, we)
        for copy in swapped:
            copy.wait()


def front(pieces, x, gain, lgain, cosine, sine, seg_col, seg_row, swaps, collective_id):
    length, width = x.shape
    chunks = 4
    step = length // chunks
    count = len(pieces[0])
    vmem = pl.BlockSpec(memory_space=pltpu.VMEM)
    anywhere = pl.BlockSpec(memory_space=pl.ANY)

    def tile(columns):
        return pl.BlockSpec((step, columns), lambda i: (jnp.minimum(i, chunks - 1), 0))

    def held(rows, columns):
        return pl.BlockSpec((rows, columns), lambda i: (0, 0))

    full = lambda group: (group[0].shape[0] * count, group[0].shape[1])
    backs = (width + KV_RANK + 2 * ROPE, QK_END + ROPE)
    outs = [
        (tile(width), (length, width), BF),
        (tile(KV_RANK), (length, KV_RANK), BF),
        (held(length, QD), (length, QD), BF),
        (held(length, QD), (length, QD), BF),
        (held(length, V_DIM), (length, V_DIM), BF),
        (held(length, V_DIM), (length, V_DIM), BF),
        (held(length, 1), (length, 1), F32),
        (held(*backs), backs, BF),
    ]
    return pl.pallas_call(
        functools.partial(front_kernel, count, len(swaps), chunks),
        grid=(chunks + 1,),
        out_shape=[jax.ShapeDtypeStruct(shape, dtype) for _, shape, dtype in outs]
        + [jax.ShapeDtypeStruct(w.shape, w.dtype) for w in swaps],
        in_specs=[anywhere] * (3 * count) + [tile(width), vmem, vmem, tile(ROPE), tile(ROPE), vmem, vmem]
        + [anywhere] * len(swaps),
        out_specs=[spec for spec, _, _ in outs] + [anywhere] * len(swaps),
        scratch_shapes=[pltpu.VMEM(full(group), BF) for group in pieces]
        + [pltpu.SemaphoreType.DMA((3, count)), pltpu.SemaphoreType.DMA((max(1, len(swaps)), 2))],
        compiler_params=pltpu.CompilerParams(
            vmem_limit_bytes=VMEM_LIMIT, collective_id=collective_id, has_side_effects=len(swaps) > 0
        ),
        cost_estimate=COST,
        name="front",
    )(*sum(pieces, ()), x, gain, lgain, cosine, sine, seg_col, seg_row, *swaps)


def attend_back_kernel(*refs):
    qh_ref, kh_ref, v_ref, lse_ref, heads_ref, da_ref, wo_ref, cos_ref, sin_ref, segc_ref, segr_ref = refs[:11]
    back_ref, gout_ref, dk_acc, dv_acc = refs[11:]
    dk_acc[...] = jnp.zeros_like(dk_acc)
    dv_acc[...] = jnp.zeros_like(dv_acc)
    for start, step, low in spans_of(qh_ref.shape[0]):
        end = start + step
        query = qh_ref[start:end, :]
        grad = mm_nt(da_ref[start:end, :], wo_ref[...]).astype(BF)
        keys = kh_ref[low:end, :]
        scores = mm_nt(query, keys) * SCALE
        allowed = allowed_of(segc_ref, segr_ref, start, step, low)
        prob = jnp.where(allowed, jnp.exp(scores - lse_ref[start:end, :]), 0.0)
        dv_acc[low:end, :] += mm_tn(prob.astype(BF), grad)
        dprob = mm_nt(grad, v_ref[low:end, :])
        delta = jnp.sum(prob * dprob, axis=-1, keepdims=True)
        dscore = (prob * (dprob - delta) * SCALE).astype(BF)
        dquery = mm(dscore, keys)
        back_ref[start:end, :NOPE] = dquery[:, :NOPE].astype(BF)
        turned = turn_back(dquery[:, NOPE:], cos_ref[start:end, :], sin_ref[start:end, :])
        back_ref[start:end, KV_END:QK_END] = turned.astype(BF)
        dk_acc[low:end, :] += mm_tn(dscore, query)
    back_ref[:, NOPE : 2 * NOPE] = dk_acc[:, :NOPE].astype(BF)
    back_ref[:, 2 * NOPE : KV_END] = dv_acc[...].astype(BF)
    back_ref[:, QK_END:] = turn_back(dk_acc[:, NOPE:], cos_ref[...], sin_ref[...]).astype(BF)
    gout_ref[...] = mm_tn(heads_ref[...], da_ref[...]).astype(BF)


def attend_back(*operands):
    length, width = operands[5].shape
    vmem = pl.BlockSpec(memory_space=pltpu.VMEM)
    return pl.pallas_call(
        attend_back_kernel,
        out_shape=[jax.ShapeDtypeStruct((length, QK_END + ROPE), BF), jax.ShapeDtypeStruct((V_DIM, width), BF)],
        in_specs=[vmem] * len(operands),
        out_specs=[vmem, vmem],
        scratch_shapes=[pltpu.VMEM((length, QD), F32), pltpu.VMEM((length, V_DIM), F32)],
        compiler_params=pltpu.CompilerParams(vmem_limit_bytes=VMEM_LIMIT),
        cost_estimate=COST,
        name="attend_back",
    )(*operands)


def fsdp_pieces(x, other):
    if lax.axis_size("fsdp") != 2:
        return (lax.all_gather(x, "fsdp", axis=0, tiled=True),)
    return (x, other)


def fill(pieces, dst, sems):
    if len(pieces) == 1:
        return [pltpu.make_async_copy(pieces[0], dst, sems.at[0])]
    part = lax.axis_index("fsdp")
    height = pieces[0].shape[0]
    starts = (part * height, (1 - part) * height)
    return [
        pltpu.make_async_copy(piece, dst.at[pl.ds(pl.multiple_of(start, height), height), :], sems.at[i])
        for i, (piece, start) in enumerate(zip(pieces, starts))
    ]


def picks(slot_ref, share_ref, b, most):
    slots = slot_ref[b]
    pick = slots == lax.broadcasted_iota(jnp.int32, (most, slots.shape[1]), 0)
    return pick.astype(BF), jnp.sum(jnp.where(pick, share_ref[b], 0.0), axis=-1, keepdims=True)


def hidden_spans(hidden):
    cut = -(-hidden // 256) * 128
    return ((0, cut), (cut, hidden))


def start_first(groups):
    @pl.when(pl.program_id(0) == 0)
    def _():
        for group in groups:
            for copy in group:
                copy.start()


def wait_first(groups):
    @pl.when(pl.program_id(0) == 0)
    def _():
        for group in groups:
            for copy in group:
                copy.wait()


def expert_in_kernel(count, most, swaps, *refs):
    wg_parts, wu_parts = refs[:count], refs[count : 2 * count]
    act_ref, slot_ref, share_ref, wsgu_ref, wsd_ref, g_ref = refs[2 * count : 2 * count + 6]
    gives, refs = refs[2 * count + 6 : 2 * count + 6 + swaps], refs[2 * count + 6 + swaps :]
    xe_ref, ge_ref, ue_ref, he_ref, sh_ref, dye_ref, dsgu_ref, ys_ref, ds_ref = refs[:9]
    takes, (wg, wu, sems, swap_sems) = refs[9 : 9 + swaps], refs[9 + swaps :]
    swapped = swap_copies(gives, takes, swap_sems) if swaps else []
    if swaps:

        @pl.when(pl.program_id(0) == 0)
        def _():
            greet((), True)
            for copy in swapped:
                copy.start()

    copies = [fill(wg_parts, wg, sems.at[0]), fill(wu_parts, wu, sems.at[1])]
    start_first(copies)
    blocks, rows = slot_ref.shape[0], slot_ref.shape[2]
    for b in range(blocks):
        pick, share = picks(slot_ref, share_ref, b, most)
        block, packed = slice(b * rows, (b + 1) * rows), slice(b * most, (b + 1) * most)
        xe_ref[packed, :] = mm(pick, act_ref[block, :]).astype(BF)
        dye_ref[packed, :] = (share * mm(pick, g_ref[block, :])).astype(BF)
    sgu = mm(act_ref[...], wsgu_ref[...])
    units = sh_ref.shape[1]
    sg, su = sgu[:, :units], sgu[:, units:]
    sig = jax.nn.sigmoid(sg)
    sh_ref[...] = (sg * sig * su).astype(BF)
    dsh = mm_nt(g_ref[...], wsd_ref[...])
    dsgu_ref[:, :units] = (dsh * su * sig * (1.0 + sg * (1.0 - sig))).astype(BF)
    dsgu_ref[:, units:] = (dsh * sg * sig).astype(BF)
    ys_ref[...] = mm(sh_ref[...], wsd_ref[...]).astype(BF)
    ds_ref[...] = mm_nt(dsgu_ref[...], wsgu_ref[...]).astype(BF)
    wait_first(copies)
    for low, high in hidden_spans(wg.shape[1]):
        ge = mm(xe_ref[...], wg[:, low:high])
        ue = mm(xe_ref[...], wu[:, low:high])
        ge_ref[:, low:high] = ge
        ue_ref[:, low:high] = ue
        he_ref[:, low:high] = (ge * jax.nn.sigmoid(ge) * ue).astype(BF)
    if swaps:

        @pl.when(pl.program_id(0) == pl.num_programs(0) - 1)
        def _():
            for copy in swapped:
                copy.wait()


def expert_out_kernel(count, most, swaps, *refs):
    wd_parts = refs[:count]
    he_ref, slot_ref, share_ref, ys_ref, y_ref, wd, sems, _ = refs[count:]
    copies = [fill(wd_parts, wd, sems.at[0])]
    start_first(copies)
    wait_first(copies)
    blocks, rows = slot_ref.shape[0], slot_ref.shape[2]
    z = mm(he_ref[...], wd[...]).astype(BF)
    for b in range(blocks):
        pick, share = picks(slot_ref, share_ref, b, most)
        ye = z[b * most : (b + 1) * most, :].astype(F32)
        ys = ys_ref[b * rows : (b + 1) * rows, :].astype(F32)
        y_ref[b * rows : (b + 1) * rows, :] = (ys + mm_tn(pick, (share * ye).astype(BF))).astype(BF)


def expert_back_kernel(n, cut, count, most, swaps, *refs):
    wg_parts, wu_parts, wd_parts = refs[:count], refs[count : 2 * count], refs[2 * count : 3 * count]
    dye_ref, slot_ref, share_ref, part_ref, ge_ref, ue_ref, ds_ref = refs[3 * count : 3 * count + 7]
    dact_ref, dge_ref, due_ref, y_ref = refs[3 * count + 7 : 3 * count + 11]
    wg, wu, wd, sems, _, *buffers = refs[3 * count + 11 :]
    copies = [fill(p, w, sems.at[i]) for i, (p, w) in enumerate(((wg_parts, wg), (wu_parts, wu), (wd_parts, wd)))]
    start_first(copies)
    finish = scatter_in_grid(pl.program_id(0), n, cut, part_ref, y_ref, buffers)
    blocks, rows = slot_ref.shape[0], slot_ref.shape[2]
    wait_first(copies)
    for low, high in hidden_spans(wg.shape[1]):
        dhe = mm_nt(dye_ref[...], wd[low:high, :])
        ge, ue = ge_ref[:, low:high], ue_ref[:, low:high]
        sig = jax.nn.sigmoid(ge)
        dge_ref[:, low:high] = (dhe * ue * sig * (1.0 + ge * (1.0 - sig))).astype(BF)
        due_ref[:, low:high] = (dhe * ge * sig).astype(BF)
    dxe = (mm_nt(dge_ref[...], wg[...]) + mm_nt(due_ref[...], wu[...])).astype(BF)
    for b in range(blocks):
        pick, _ = picks(slot_ref, share_ref, b, most)
        block = slice(b * rows, (b + 1) * rows)
        shared = ds_ref[block, :].astype(F32)
        dact_ref[block, :] = (shared + mm_tn(pick, dxe[b * most : (b + 1) * most, :])).astype(BF)
    finish()


def expert_call(kernel, name, pieces, most, steps, slot, share, whole, tiled, outs, swaps=(), collective_id=None, summed=None):
    devices, rows = slot.shape[0], slot.shape[2]
    per = devices // steps
    anywhere = pl.BlockSpec(memory_space=pl.ANY)
    vmem = pl.BlockSpec(memory_space=pltpu.VMEM)

    def tile(total, columns):
        return pl.BlockSpec((total // steps, columns), lambda i: (i, 0))

    cut = pl.BlockSpec((per, 1, rows), lambda i: (i, 0, 0))
    count = len(pieces[0])
    full = lambda group: (group[0].shape[0] * count, group[0].shape[1])
    buffers, kept = [], []
    if summed is not None:
        buffers = scatter_buffers(devices // 2, *summed)
        kept = [(pl.BlockSpec(summed, lambda i: (0, 0)), jax.ShapeDtypeStruct(summed, F32))]
    return pl.pallas_call(
        functools.partial(kernel, count, most, len(swaps)),
        grid=(steps,),
        out_shape=[jax.ShapeDtypeStruct((total, columns), dtype) for total, columns, dtype in outs]
        + [shape for _, shape in kept]
        + [jax.ShapeDtypeStruct(x.shape, x.dtype) for x in swaps],
        in_specs=[anywhere] * (len(pieces) * count) + [tile(*tiled[0].shape), cut, cut] + [vmem] * len(whole)
        + [tile(*t.shape) for t in tiled[1:]]
        + [anywhere] * len(swaps),
        out_specs=[tile(total, columns) for total, columns, _ in outs]
        + [spec for spec, _ in kept]
        + [anywhere] * len(swaps),
        scratch_shapes=[pltpu.VMEM(full(group), BF) for group in pieces]
        + [pltpu.SemaphoreType.DMA((len(pieces), count)), pltpu.SemaphoreType.DMA((max(1, len(swaps)), 2))]
        + buffers,
        compiler_params=pltpu.CompilerParams(
            vmem_limit_bytes=VMEM_LIMIT, collective_id=collective_id, has_side_effects=collective_id is not None
        ),
        cost_estimate=COST,
        name=name,
    )(*sum(pieces, ()), tiled[0], slot, share, *whole, *tiled[1:], *swaps)


def widen_query(nope, rope):
    devices, rows, _ = nope.shape
    steps = 8
    step = rows // steps

    def kernel(n_ref, r_ref, o_ref):
        def put(first):
            for d in range(devices):
                o_ref[:, d * QD : d * QD + NOPE] = n_ref[d].astype(F32)
                o_ref[:, d * QD + NOPE : (d + 1) * QD] = r_ref[d, :, first : first + ROPE].astype(F32)

        low = pl.program_id(0) < steps // 2
        pl.when(low)(lambda: put(0))
        pl.when(jnp.logical_not(low))(lambda: put(ROPE))

    return pl.pallas_call(
        kernel,
        grid=(steps,),
        out_shape=jax.ShapeDtypeStruct((rows, devices * QD), F32),
        in_specs=[
            pl.BlockSpec((devices, step, NOPE), lambda i: (0, i, 0)),
            pl.BlockSpec((devices, step, 2 * ROPE), lambda i: (0, i % (steps // 2), 0)),
        ],
        out_specs=pl.BlockSpec((step, devices * QD), lambda i: (i, 0)),
        compiler_params=pltpu.CompilerParams(vmem_limit_bytes=VMEM_LIMIT),
        cost_estimate=COST,
        name="wide_query",
    )(nope, rope)


def trim(stacks, share):
    devices, _, width = stacks[0].shape
    if share % 8:
        return jnp.concatenate(stacks, axis=1)[:, :share].reshape(-1, width).astype(F32)

    def kernel(*refs):
        *i_refs, o_ref = refs
        for d in range(i_refs[0].shape[0]):
            at = d * share
            for i_ref in i_refs:
                height = min(i_ref.shape[1], (d + 1) * share - at)
                o_ref[at : at + height, :] = i_ref[d, :height, :].astype(F32)
                at += height

    return pl.pallas_call(
        kernel,
        grid=(4,),
        out_shape=jax.ShapeDtypeStruct((devices * share, width), F32),
        in_specs=[pl.BlockSpec((devices // 4, x.shape[1], width), lambda i: (i, 0, 0)) for x in stacks],
        out_specs=pl.BlockSpec((devices // 4 * share, width), lambda i: (i, 0)),
        compiler_params=pltpu.CompilerParams(vmem_limit_bytes=VMEM_LIMIT),
        cost_estimate=COST,
        name="trim",
    )(*stacks)


def scatter_in_grid(t, n, cut, part_ref, o_ref, buffers):
    sibbuf, rbuf, sbuf, send, recv, fsend, frecv = buffers
    me, core, r, _ = ring_place()
    targets = (ring_seq((r + 1) % n, core, n), ring_seq((r + n - 1) % n, core, n))
    sibling = ring_seq(r, 1 - core, n)
    columns = o_ref.shape[1]
    spans = (pl.ds(0, cut), pl.ds(cut, columns - cut))

    def block(step, d, c):
        return ring_seq((r + (-step - 1 if d == 0 else step + 1) + n) % n, c, n)

    def across(step, d):
        source = part_ref.at[block(step, d, 1 - core), :, spans[d]]
        return remote(source, sibbuf.at[step, :, spans[d]], fsend.at[step, d], frecv.at[step, d], sibling)

    def onward(step, d):
        return remote(
            sbuf.at[step, :, spans[d]], rbuf.at[step, :, spans[d]], send.at[step, d], recv.at[step, d], targets[d]
        )

    @pl.when(t == 0)
    def _():
        greet((*targets, sibling))
        for step in range(2):
            for d in range(2):
                across(step, d).start()

    @pl.when(t < n - 2)
    def _():
        for d in range(2):
            across(t + 2, d).start()

    for d in range(2):
        across(t, d).wait_recv()

        def both():
            return part_ref[block(t, d, core), :, spans[d]].astype(F32) + sibbuf[t, :, spans[d]].astype(F32)

        @pl.when(t == 0)
        def _():
            sbuf[0, :, spans[d]] = both().astype(BF)
            onward(0, d).start()

        @pl.when((t > 0) & (t < n - 1))
        def _():
            onward(t - 1, d).wait_recv()
            sbuf[t, :, spans[d]] = (both() + rbuf[t - 1, :, spans[d]].astype(F32)).astype(BF)
            onward(t, d).start()

        @pl.when(t == n - 1)
        def _():
            onward(n - 2, d).wait_recv()
            o_ref[:, spans[d]] = both() + rbuf[n - 2, :, spans[d]].astype(F32)

    def finish():
        @pl.when(t == n - 1)
        def _():
            for step in range(n):
                for d in range(2):
                    across(step, d).wait_send()
                    if step < n - 1:
                        onward(step, d).wait_send()

    return finish


def scatter_buffers(n, rows, columns):
    return (
        [pltpu.VMEM((n, rows, columns), BF), pltpu.VMEM((n - 1, rows, columns), BF), pltpu.VMEM((n - 1, rows, columns), BF)]
        + [pltpu.SemaphoreType.DMA((n - 1, 2))] * 2
        + [pltpu.SemaphoreType.DMA((n, 2))] * 2
    )


def weight_grads_kernel(n, cut, parts, *refs):
    xe_ref, dge_ref, due_ref, he_ref, dye_ref, act_ref, dsgu_ref, sh_ref, g_ref, part_ref = refs[:10]
    o_ref, gate_ref, up_ref, down_ref, sgu_ref, sdown_ref = refs[10:16]
    finish = scatter_in_grid(pl.program_id(0), n, cut, part_ref, o_ref, refs[16:])
    gate_ref[...] = mm_tn(xe_ref[...], dge_ref[...]).astype(BF)
    up_ref[...] = mm_tn(xe_ref[...], due_ref[...]).astype(BF)
    down_ref[...] = mm_tn(he_ref[...], dye_ref[...]).astype(BF)
    sgu_ref[...] = mm_tn(act_ref[...], dsgu_ref[...]).astype(BF)
    sdown = mm_tn(sh_ref[...], g_ref[...]).astype(BF)
    share = sdown.shape[0] // parts
    room = sdown_ref.shape[0] // parts
    for p in range(parts):
        sdown_ref[p * room : p * room + share, :] = sdown[p * share : (p + 1) * share, :]
        if room > share:
            sdown_ref[p * room + share : (p + 1) * room, :] = jnp.zeros((room - share, sdown.shape[1]), BF)

    finish()


def weight_grads(xe, dge, due, he, dye, act, dsgu, sh, g, part, parts, room, collective_id):
    devices = lax.axis_size("seq")
    n = devices // 2
    length, columns = part.shape
    rows = length // devices
    cut = columns // 256 * 128

    def tile(x):
        return pl.BlockSpec((x.shape[0], x.shape[1] // n), lambda i: (0, i))

    def held(x):
        return pl.BlockSpec(memory_space=pltpu.VMEM)

    ff, units = dge.shape[1], dsgu.shape[1]
    slab = columns // n
    down = lambda width: pl.BlockSpec((slab, width), lambda i: (i, 0))
    along = lambda height: pl.BlockSpec((height, slab), lambda i: (0, i))
    return pl.pallas_call(
        functools.partial(weight_grads_kernel, n, cut, parts),
        grid=(n,),
        out_shape=[jax.ShapeDtypeStruct((rows, columns), F32)]
        + [
            jax.ShapeDtypeStruct(shape, BF)
            for shape in ((columns, ff), (columns, ff), (ff, columns), (columns, units), (parts * room, columns))
        ],
        in_specs=[tile(xe), held(dge), held(due), held(he), tile(dye), tile(act), held(dsgu), held(sh), tile(g)]
        + [held(part)],
        out_specs=[pl.BlockSpec((rows, columns), lambda i: (0, 0)), down(ff), down(ff), along(ff)]
        + [down(units), along(parts * room)],
        scratch_shapes=scatter_buffers(n, rows, columns),
        compiler_params=pltpu.CompilerParams(
            collective_id=collective_id, has_side_effects=True, vmem_limit_bytes=VMEM_LIMIT
        ),
        cost_estimate=COST,
        name="weight_grads",
    )(xe, dge, due, he, dye, act, dsgu, sh, g, part.reshape(devices, rows, columns))


def widen(stacked, count, parts, name):
    devices, rows, columns = stacked.shape
    share = columns // parts // count
    width = devices * columns // count
    steps = 8

    def kernel(i_ref, *o_refs):
        for j, o_ref in enumerate(o_refs):
            for p in range(parts):
                for d in range(devices):
                    at, source = (p * devices + d) * share, (j * parts + p) * share
                    o_ref[:, at : at + share] = i_ref[d, :, source : source + share].astype(F32)

    return pl.pallas_call(
        kernel,
        grid=(steps,),
        out_shape=[jax.ShapeDtypeStruct((rows, width), F32)] * count,
        in_specs=[pl.BlockSpec((devices, rows // steps, columns), lambda i: (0, i, 0))],
        out_specs=[pl.BlockSpec((rows // steps, width), lambda i: (i, 0))] * count,
        compiler_params=pltpu.CompilerParams(vmem_limit_bytes=VMEM_LIMIT),
        cost_estimate=COST,
        name=name,
    )(stacked)


def columns_of(weight, at, width):
    return lax.dynamic_slice_in_dim(weight, at * width, width, 1).astype(BF)


def rows_of(weight, at, height):
    return lax.dynamic_slice_in_dim(weight, at * height, height, 0).astype(BF)


def per_device(
    tokens,
    segment_ids,
    routes,
    gate_weights,
    out_grad,
    attn_gain,
    q_weight,
    latent_weight,
    latent_gain,
    kv_weight,
    out_weight,
    ffn_gain,
    shared_gate,
    shared_up,
    shared_down,
    expert_gate,
    expert_up,
    expert_down,
):
    _, rows, width = tokens.shape
    devices = lax.axis_size("seq")
    at = lax.axis_index("seq")
    parts = lax.axis_size("fsdp")
    part = lax.axis_index("fsdp")
    length = rows * devices
    own_x = tokens[0]
    own_g = out_grad[0]

    per, per_latent = attn_gain.shape[0], latent_gain.shape[0]
    gains = jnp.concatenate([attn_gain, ffn_gain, latent_gain]).astype(BF)
    gains_size = gains.shape[0]
    gains_rows = -(-gains_size // 2048) * 16
    gains = jnp.pad(gains, (0, gains_rows * 128 - gains_size)).reshape(gains_rows, 128)
    out_rows = out_weight.shape[0]
    early_latent = 2
    share = shared_down.shape[0] // devices
    share_pad = -(-share // 32) * 32
    sdown = jnp.pad(rows_of(shared_down, at, share), ((0, share_pad - share), (0, 0)))
    early = (
        gains,
        columns_of(q_weight, at, QD),
        latent_weight.astype(BF),
        columns_of(kv_weight, at, NOPE + V_DIM),
        lax.dynamic_slice_in_dim(out_weight, at * V_DIM % out_rows, V_DIM, 0).astype(BF),
    )
    pair = parts == 2

    def crossing(*arrays):
        return arrays if pair else ()

    def crossed(taken, count):
        return taken if pair else [None] * count

    experts = jnp.arange(devices, dtype=jnp.int32)
    spread = jnp.sum(
        jnp.where(routes[0].T[None, :, :] == experts[:, None, None], gate_weights[0].T[None, :, :], 0.0), axis=1
    )
    x_all, spread_all, *others = ring_gather_many(
        [own_x, spread],
        8,
        None,
        crossing(*early),
        early_latent if pair else None,
        (expert_gate[0], expert_up[0], expert_down[0]),
    )
    others, (egate, eup, edown) = others[:-3], others[-3:]
    late_g, x_all = lax.optimization_barrier((own_g, x_all.reshape(length, width)))
    g_all = lax.all_gather(late_g, "seq", axis=0, tiled=True)
    share_of = lax.dynamic_index_in_dim(spread_all, at, 1, keepdims=False)
    others = crossed(others, len(early))
    gains = fsdp_gather(gains, others[0]).reshape(parts, -1)[:, :gains_size].astype(F32)
    gain_one = gains[:, :per].reshape(1, -1)
    gain_two = gains[:, per : 2 * per].reshape(1, -1)
    gain_lat = gains[:, 2 * per :].reshape(1, -1)
    w_latent = fsdp_gather(early[2], others[2])
    w_out = fsdp_pick(early[4], at * V_DIM // out_rows, others[4])

    hidden = shared_down.shape[0] * parts

    def shared_columns(weight):
        pieces = [
            lax.dynamic_slice_in_dim(weight, p * (hidden // parts) + at * share, share, 1) for p in range(parts)
        ]
        return pieces

    sgu = jnp.concatenate(shared_columns(shared_gate) + shared_columns(shared_up), axis=1).astype(BF)

    cosine, sine = rope_tables(length)
    seg_col, seg_row = segment_ids.reshape(length, 1), segment_ids
    act_one, cnorm, qh, kh, values, heads, lse, w_back, *taken = front(
        tuple(fsdp_pieces(early[i], others[i]) for i in (1, 2, 3)),
        x_all,
        gain_one,
        gain_lat,
        cosine,
        sine,
        seg_col,
        seg_row,
        crossing(sgu, sdown),
        11 if pair else None,
    )
    sgu_other, sdown_other = crossed(taken, 2)
    own_xf = own_x.astype(F32)
    attended, taken = ring_scatter(heads, w_out.T, 2, crossing(egate))
    (egate_other,) = crossed(taken, 1)
    x1 = own_xf + attended
    r3 = norm_scale(x1)
    act_two = (x1 * r3 * gain_two).astype(BF)
    act_all, taken = ring_gather(act_two, 9, crossing(eup))
    (eup_other,) = crossed(taken, 1)
    w_egate, w_eup = fsdp_pieces(egate, egate_other), fsdp_pieces(eup, eup_other)
    w_sgu = fsdp_gather(sgu, sgu_other)
    w_sdown = fsdp_gather(sdown[:share], sdown_other[:share] if pair else None)

    most = min(MOST, rows)
    named = share_of > 0.0
    rank = jnp.cumsum(named.astype(jnp.int32), axis=1) - 1
    slot = jnp.where(named, rank, -1)[:, None, :]
    share_of = share_of[:, None, :]
    packed = devices * most
    ff = expert_gate.shape[2]
    units = parts * share
    steps = 4
    xe, ge, ue, he, sh, dye, dsgu, ys, ds, *taken = expert_call(
        expert_in_kernel,
        "experts_in",
        (w_egate, w_eup),
        most,
        steps,
        slot,
        share_of,
        (w_sgu, w_sdown),
        (act_all, g_all),
        (
            (packed, width, BF),
            (packed, ff, F32),
            (packed, ff, F32),
            (packed, ff, BF),
            (length, units, BF),
            (packed, width, BF),
            (length, 2 * units, BF),
            (length, width, BF),
            (length, width, BF),
        ),
        crossing(edown),
        10 if pair else None,
    )
    (edown_other,) = crossed(taken, 1)
    w_edown = fsdp_pieces(edown, edown_other)
    (y_part,) = expert_call(
        expert_out_kernel,
        "experts_out",
        (w_edown,),
        most,
        steps,
        slot,
        share_of,
        (),
        (he, ys),
        ((length, width, BF),),
    )
    dact_part, dge, due, y_sum = expert_call(
        functools.partial(expert_back_kernel, devices // 2, width // 256 * 128),
        "experts_back",
        (w_egate, w_eup, w_edown),
        most,
        devices // 2,
        slot,
        share_of,
        (y_part.reshape(devices, rows, width),),
        (dye, ge, ue, ds),
        ((length, width, BF), (packed, ff, BF), (packed, ff, BF)),
        (),
        12,
        (rows, width),
    )
    dact_two, grad_egate, grad_eup, grad_edown, grad_sgu, grad_sdown = weight_grads(
        xe, dge, due, he, dye, act_all, dsgu, sh, g_all, dact_part, parts, share_pad, 3
    )
    own_gf = own_g.astype(F32)
    grad_gain_two = jnp.sum(dact_two * x1 * r3, axis=0)
    dx1 = own_gf + norm_back(x1, r3, dact_two * gain_two)
    dattn_all, taken = ring_gather(dx1.astype(BF), 1, (given(grad_sgu), given(grad_sdown)) if pair else ())
    sgu_taken, sdown_taken = crossed(taken, 2)
    grad_sgu = fsdp_scatter(grad_sgu, sgu_taken).astype(BF)
    grad_sdown = fsdp_scatter(grad_sdown, sdown_taken).astype(BF)
    output = (x1 + y_sum).astype(BF)

    back, grad_out = attend_back(qh, kh, values, lse, heads, dattn_all, w_out, cosine, sine, seg_col, seg_row)
    summed, grad_nope, grad_rope, grad_expand, taken = ring_scatter(
        back, w_back, 4, (given(grad_edown),) if pair else (), (act_one, cnorm)
    )
    grad_edown = fsdp_scatter(grad_edown, *taken)

    r1 = norm_scale(own_xf)
    own_act = (own_xf * r1 * gain_one).astype(BF)
    own_comp = mm(own_act, w_latent)[:, :KV_RANK]
    r2 = norm_scale(own_comp)
    dcn = summed[:, width : width + KV_RANK]
    grad_gain_lat = jnp.sum(dcn * own_comp * r2, axis=0)
    dcomp = norm_back(own_comp, r2, dcn * gain_lat)
    dlatent = jnp.concatenate([dcomp, summed[:, width + KV_RANK : width + KV_RANK + ROPE]], axis=-1).astype(BF)
    dact_one = summed[:, :width] + mm_nt(dlatent, w_latent)
    grad_gain_one = jnp.sum(dact_one * own_xf * r1, axis=0)
    input_grad = dx1 + norm_back(own_xf, r1, dact_one * gain_one)

    small = jnp.concatenate([grad_gain_one, grad_gain_two, grad_gain_lat])
    small = jnp.pad(small, (0, 64 * 128 - small.shape[0])).reshape(64, 128)

    def in_part(device):
        return device * V_DIM // out_rows == lax.axis_index("fsdp")

    sgu_all, dlatent_all, sdown_all, *taken = ring_gather_many(
        [grad_sgu, dlatent, grad_sdown],
        5,
        None,
        (given(grad_nope), given(grad_rope), given(grad_expand), grad_out, small, given(grad_egate)) if pair else (),
    )
    nope_taken, rope_taken, expand_taken, out_taken, small_taken, egate_taken = crossed(taken, 6)
    grad_nope = fsdp_scatter(grad_nope, nope_taken).astype(BF)
    grad_rope = fsdp_scatter(grad_rope, rope_taken).astype(BF)
    grad_rope = jnp.concatenate(jnp.split(grad_rope, 2, axis=0), axis=1)
    grad_expand = fsdp_scatter(grad_expand, expand_taken).astype(BF)
    grad_out = fsdp_sum(grad_out, out_taken)
    small = fsdp_sum(small, small_taken)
    grad_egate = fsdp_scatter(grad_egate, egate_taken)
    slab = width // parts // devices
    act_cols = jnp.concatenate(
        [lax.dynamic_slice_in_dim(act_one, p * (width // parts) + at * slab, slab, 1) for p in range(parts)], axis=1
    )
    grad_latent = mm_tn(act_cols, dlatent_all.reshape(length, -1)).astype(BF)
    latent_taken = None
    if pair:
        latent_taken = lax.ppermute(
            lax.dynamic_slice_in_dim(grad_latent, (1 - part) * slab, slab, 0), "fsdp", [(0, 1), (1, 0)]
        )
    grad_latent = fsdp_scatter(grad_latent, latent_taken).astype(BF)
    latent_pad = -(-slab // 32) * 32
    nope_all, rope_all, expand_all, out_all, latent_all, small_all, *taken = ring_gather_many(
        [grad_nope, grad_rope, grad_expand, grad_out, jnp.pad(grad_latent, ((0, latent_pad - slab), (0, 0))), small],
        7,
        [None, None, None, in_part, None, None],
        (given(grad_eup),) if pair else (),
    )
    (eup_taken,) = crossed(taken, 1)
    grad_eup = fsdp_scatter(grad_eup, eup_taken)
    latent_all = latent_all[:, :slab]
    out_grad_own = lax.dynamic_slice_in_dim(
        out_all.reshape(devices * V_DIM, width), part * out_rows, out_rows, 0
    ).astype(F32)
    small = jnp.sum(small_all, axis=0).reshape(-1)
    wide_gate, wide_up = widen(sgu_all, 2, parts, "wide_shared")
    gain_rows = width // parts
    own_gains = [
        lax.dynamic_slice_in_dim(small, part * gain_rows, gain_rows),
        lax.dynamic_slice_in_dim(small, width + part * gain_rows, gain_rows),
        lax.dynamic_slice_in_dim(small, 2 * width + part * (KV_RANK // parts), KV_RANK // parts),
    ]
    return (
        output[None],
        input_grad[None],
        own_gains[0],
        widen_query(nope_all, rope_all),
        latent_all.reshape(-1, grad_latent.shape[1]).astype(F32),
        own_gains[2],
        widen(expand_all, 1, 1, "wide_kv")[0],
        out_grad_own,
        own_gains[1],
        wide_gate,
        wide_up,
        trim([sdown_all], share),
        grad_egate[None],
        grad_eup[None],
        grad_edown[None],
    )


def solution(mesh):
    token_spec = P("fsdp", "seq", None)
    row_spec = P("fsdp", None)
    gain_spec = P("fsdp")
    expert_spec = P("seq", "fsdp", None)
    dense = (gain_spec, row_spec, row_spec, gain_spec, row_spec, row_spec, gain_spec, row_spec, row_spec, row_spec)
    weights = dense + (expert_spec,) * 3
    return jax.shard_map(
        per_device,
        mesh=mesh,
        in_specs=(token_spec, row_spec, token_spec, token_spec, token_spec) + weights,
        out_specs=(token_spec, token_spec) + weights,
        check_vma=False,
    )
```

```python
import functools
import math

import jax
import jax.numpy as jnp
import numpy as np
from jax import lax
from jax.experimental import pallas as pl
from jax.experimental.pallas import tpu as pltpu
from jax.sharding import PartitionSpec as P

HEADS = 16
NOPE = 128
ROPE = 64
QD = NOPE + ROPE
KV_RANK = 512
V_DIM = 128
TOP = 6
MOST = 96

EPS = 1e-06
NEG = -1e30
THETA = 10000.0
SCALE = 1.0 / math.sqrt(QD)
KV_END = 2 * NOPE + V_DIM
QK_END = KV_END + ROPE
MESH = pl.DeviceIdType.MESH
BF = jnp.bfloat16
F32 = jnp.float32
VMEM_LIMIT = 60 * 2**20
COST = pl.CostEstimate(flops=0, bytes_accessed=2**20, transcendentals=0)


def norm_scale(values):
    return lax.rsqrt(jnp.mean(values * values, axis=-1, keepdims=True) + EPS)


def norm_back(values, inverse, gradient):
    return inverse * gradient - values * inverse * inverse * inverse * jnp.mean(
        gradient * values, axis=-1, keepdims=True
    )


def mm(a, b):
    return jnp.dot(a, b, preferred_element_type=F32)


def mm_tn(a, b):
    return lax.dot_general(a, b, (((0,), (0,)), ((), ())), preferred_element_type=F32)


def mm_nt(a, b):
    return lax.dot_general(a, b, (((1,), (1,)), ((), ())), preferred_element_type=F32)


def rope_tables(length):
    places = np.arange(length, dtype=np.float32)
    frequency = np.power(np.float32(THETA), np.arange(ROPE // 2, dtype=np.float32) * np.float32(-2.0 / ROPE))
    angles = places[:, None] * frequency[None, :].astype(np.float32)
    angles = np.concatenate([angles, angles], axis=-1)
    return jnp.asarray(np.cos(angles), F32), jnp.asarray(np.sin(angles), F32)


def ring_place():
    me = lax.axis_index("seq")
    core, chip = me % 2, me // 2
    z, y = chip // 2, chip % 2
    half = lax.axis_size("seq") // 4
    return me, core, jnp.where(y == 0, z, 2 * half - 1 - z), 2 * half


def ring_seq(r, core, n):
    low = r < n // 2
    return (jnp.where(low, r, n - 1 - r) * 2 + jnp.where(low, 0, 1)) * 2 + core


def greet(devices, across=False):
    barrier = pltpu.get_barrier_semaphore()
    for device in devices:
        pl.semaphore_signal(barrier, inc=1, device_id={"seq": device}, device_id_type=MESH)
    if across:
        other = 1 - lax.axis_index("fsdp")
        pl.semaphore_signal(barrier, inc=1, device_id={"fsdp": other}, device_id_type=MESH)
    pl.semaphore_wait(barrier, len(devices) + across)


def given(x):
    return (x, True)


def swap_arrays(swaps):
    return [x[0] if isinstance(x, tuple) else x for x in swaps]


def swap_shapes(swaps):
    shapes = [(x[0].shape[0] // 2, x[0].shape[1]) if isinstance(x, tuple) else x.shape for x in swaps]
    return [jax.ShapeDtypeStruct(shape, x.dtype) for shape, x in zip(shapes, swap_arrays(swaps))]


def swap_copies(gives, takes, sems):
    other = 1 - lax.axis_index("fsdp")

    def source(give, take):
        height = take.shape[0]
        return give if give.shape[0] == height else give.at[pl.ds(pl.multiple_of(other * height, height), height), :]

    return [
        pltpu.make_async_remote_copy(
            source(give, take), take, sems.at[i, 0], sems.at[i, 1], device_id={"fsdp": other}, device_id_type=MESH
        )
        for i, (give, take) in enumerate(zip(gives, takes))
    ]


def remote(src, dst, send, recv, device):
    return pltpu.make_async_remote_copy(src, dst, send, recv, device_id={"seq": device}, device_id_type=MESH)


def cast_pieces(rows):
    return next(pieces for pieces in (8, 4, 2, 1) if rows % (16 * pieces) == 0 or pieces == 1)


def cast_scratch(casts):
    shapes = []
    for x in casts:
        height = x.shape[0] // cast_pieces(x.shape[0])
        shapes += [
            pltpu.VMEM((2, height, x.shape[1]), F32),
            pltpu.VMEM((2, height, x.shape[1]), BF),
            pltpu.SemaphoreType.DMA((2,)),
            pltpu.SemaphoreType.DMA((2,)),
        ]
    return shapes


def cast_steps(sources, targets, scratch):
    for i, (source, target) in enumerate(zip(sources, targets)):
        wide, narrow, in_sem, out_sem = scratch[4 * i : 4 * i + 4]
        pieces = cast_pieces(source.shape[0])
        height = source.shape[0] // pieces

        def load(c):
            return pltpu.make_async_copy(source.at[pl.ds(c * height, height), :], wide.at[c % 2], in_sem.at[c % 2])

        def save(c):
            return pltpu.make_async_copy(narrow.at[c % 2], target.at[pl.ds(c * height, height), :], out_sem.at[c % 2])

        load(0).start()
        for c in range(pieces):
            if c + 1 < pieces:
                load(c + 1).start()
            load(c).wait()
            if c >= 2:
                save(c - 2).wait()
            narrow[c % 2] = wide[c % 2].astype(BF)
            save(c).start()
            yield
        for c in range(max(0, pieces - 2), pieces):
            save(c).wait()


def neighbours(n):
    _, core, r, _ = ring_place()
    return ring_seq((r + 1) % n, core, n), ring_seq((r + n - 1) % n, core, n), ring_seq(r, 1 - core, n)


def gather_steps(n, cuts, actives, x_refs, o_refs, own_sem, local_sem, sems):
    count = len(cuts)
    me, core, r, _ = ring_place()
    *targets, sibling = neighbours(n)

    def block(t, d, c):
        return ring_seq((r + (-t if d == 0 else t) + n) % n, c, n)

    def guarded(i, source, action):
        if actives[i] is None:
            action()
        else:
            pl.when(actives[i](source))(action)

    def parts_of(i):
        height = x_refs[i].shape[0] // (2 * cuts[i])
        for k in range(cuts[i]):
            for d in range(2):
                yield k, d, pl.ds((d * cuts[i] + k) * height, height)

    def onward(i, t, d, k, rows):
        at = o_refs[i].at[block(t, d, core), rows]
        source = x_refs[i].at[rows] if t == 0 else at
        return remote(source, at, sems[4 * i].at[t, d, k], sems[4 * i + 1].at[t, d, k], targets[d])

    def across(i, t, d, k, rows, c):
        at = o_refs[i].at[block(t, d, c), rows]
        return remote(at, at, sems[4 * i + 2].at[t - 1, d, k], sems[4 * i + 3].at[t - 1, d, k], sibling)

    def local(i):
        return pltpu.make_async_copy(x_refs[i], o_refs[i].at[me], local_sem.at[i])

    def own(i):
        return remote(x_refs[i], o_refs[i].at[me], own_sem.at[i, 0], own_sem.at[i, 1], sibling)

    for i in range(count):
        local(i).start()
        for k, d, rows in parts_of(i):
            guarded(i, me, lambda: onward(i, 0, d, k, rows).start())
        guarded(i, me, lambda: own(i).start())
    yield
    for t in range(n - 1):
        for i in range(count):
            for k, d, rows in parts_of(i):

                def step():
                    onward(i, t, d, k, rows).wait_recv()
                    if t < n - 2:
                        onward(i, t + 1, d, k, rows).start()
                    across(i, t + 1, d, k, rows, core).start()

                guarded(i, block(t + 1, d, core), step)
        yield
    for i in range(count):
        local(i).wait()
        guarded(i, me, lambda: own(i).wait_send())
        guarded(i, sibling, lambda: own(i).wait_recv())
        for t in range(n - 1):
            for k, d, rows in parts_of(i):
                guarded(i, block(t, d, core), lambda: onward(i, t, d, k, rows).wait_send())
                guarded(i, block(t + 1, d, core), lambda: across(i, t + 1, d, k, rows, core).wait_send())
                guarded(i, block(t + 1, d, 1 - core), lambda: across(i, t + 1, d, k, rows, 1 - core).wait_recv())


def gather_cut(height):
    return 2 if height % 64 == 0 else 1


def gather_sems(n, cuts):
    return [pltpu.SemaphoreType.DMA((n - 1, 2, cut)) for cut in cuts for _ in range(4)]


def gather_kernel(n, cuts, actives, swaps, shared, casts, *refs):
    count = len(cuts)
    total = count + swaps
    x_refs, give_refs, wide_refs = refs[:count], refs[count:total], refs[total : total + casts]
    refs = refs[total + casts :]
    o_refs, take_refs, narrow_refs = refs[:count], refs[count:total], refs[total : total + casts]
    own_sem, local_sem, swap_sems, hand_sem = refs[total + casts : total + casts + 4]
    sems = refs[total + casts + 4 :]
    casting = cast_steps(wide_refs, narrow_refs, sems[4 * count :])
    _, core, _, _ = ring_place()
    greet(neighbours(n), swaps > 0)
    sibling = neighbours(n)[2]

    def half_of(ref, c):
        height = ref.shape[0] // 2
        return ref.at[pl.ds(pl.multiple_of(c * height, height), height), :]

    gives, takes = list(give_refs), list(take_refs)
    if shared is not None:
        gives[shared], takes[shared] = half_of(gives[shared], core), half_of(takes[shared], core)
    swapped = swap_copies(gives, takes, swap_sems)
    for copy in swapped:
        copy.start()

    def handed(c):
        half = half_of(take_refs[shared], c)
        return remote(half, half, hand_sem.at[0], hand_sem.at[1], sibling)

    steps = gather_steps(n, cuts, actives, x_refs, o_refs, own_sem, local_sem, sems)
    next(steps)
    for _ in range(n - 1):
        next(steps)
        for _ in range(4):
            next(casting, None)
    for _ in casting:
        pass
    for _ in steps:
        pass
    if shared is not None:
        swapped[shared].wait_recv()
        handed(core).start()
    for i, copy in enumerate(swapped):
        copy.wait_send()
        if i != shared:
            copy.wait_recv()
    if shared is not None:
        handed(core).wait_send()
        handed(1 - core).wait_recv()


def ring_gather_many(operands, collective_id, actives=None, swaps=(), shared=None, casts=()):
    devices = lax.axis_size("seq")
    n = devices // 2
    cuts = [gather_cut(x.shape[0]) for x in operands]
    anywhere = pl.BlockSpec(memory_space=pl.ANY)
    sems = gather_sems(n, cuts)
    return pl.pallas_call(
        functools.partial(gather_kernel, n, cuts, actives or [None] * len(operands), len(swaps), shared, len(casts)),
        out_shape=[jax.ShapeDtypeStruct((devices, *x.shape), x.dtype) for x in operands]
        + swap_shapes(swaps)
        + [jax.ShapeDtypeStruct(x.shape, BF) for x in casts],
        in_specs=[anywhere] * (len(operands) + len(swaps) + len(casts)),
        out_specs=[anywhere] * (len(operands) + len(swaps) + len(casts)),
        scratch_shapes=[
            pltpu.SemaphoreType.DMA((len(operands), 2)),
            pltpu.SemaphoreType.DMA((len(operands),)),
            pltpu.SemaphoreType.DMA((max(1, len(swaps)), 2)),
            pltpu.SemaphoreType.DMA((2,)),
        ]
        + sems
        + cast_scratch(casts),
        compiler_params=pltpu.CompilerParams(
            collective_id=collective_id, has_side_effects=True, **({"vmem_limit_bytes": VMEM_LIMIT} if casts else {})
        ),
        cost_estimate=COST,
        name="ring_gather",
    )(*operands, *swap_arrays(swaps), *casts)


def ring_gather(x, collective_id, swaps=()):
    out, *taken = ring_gather_many([x], collective_id, None, swaps)
    return out.reshape(-1, x.shape[1]), taken


def scatter_kernel(n, cut, swaps, beside, *refs):
    a_ref, w_ref = refs[:2]
    gives, refs = refs[2 : 2 + swaps], refs[2 + swaps :]
    if beside:
        act_hbm, cn_hbm, *refs = refs
    o_ref, takes, refs = refs[0], refs[1 : 1 + swaps], refs[1 + swaps :]
    if beside:
        nope_ref, rope_ref, expand_ref, *refs = refs
    stage, sibbuf, rbuf, sbuf, send, recv, fsend, frecv, swap_sems, *refs = refs
    if beside:
        act, cn, sems = refs
        loads = [pltpu.make_async_copy(act_hbm, act, sems.at[0]), pltpu.make_async_copy(cn_hbm, cn, sems.at[1])]
        for load in loads:
            load.start()
    me, core, r, _ = ring_place()
    targets = (ring_seq((r + 1) % n, core, n), ring_seq((r + n - 1) % n, core, n))
    sibling = ring_seq(r, 1 - core, n)
    greet((*targets, sibling), swaps > 0)
    swapped = swap_copies(gives, takes, swap_sems)
    for copy in swapped:
        copy.start()
    height, columns = o_ref.shape
    spans = (pl.ds(0, cut), pl.ds(cut, columns - cut))

    def chip(t, d):
        return (r + (-t - 1 if d == 0 else t + 1) + n) % n

    def part(t, d, c):
        block = ring_seq(chip(t, d), c, n)
        rows = a_ref[pl.ds(block * height, height), :]
        return mm_nt(rows, w_ref[spans[d], :])

    def across(t, d):
        return remote(stage.at[t, :, spans[d]], sibbuf.at[t, :, spans[d]], fsend.at[t, d], frecv.at[t, d], sibling)

    half = height // 2

    def onward(t, d, k):
        at = (t, pl.ds(k * half, half), spans[d])
        return remote(sbuf.at[at], rbuf.at[at], send.at[t, d, k], recv.at[t, d, k], targets[d])

    def give(t, d):
        stage[t, :, spans[d]] = part(t, d, 1 - core).astype(BF)
        across(t, d).start()

    for d in range(2):
        give(0, d)
    for t in range(n):
        values = []
        for d in range(2):
            if t < n - 1:
                give(t + 1, d)
            values.append(part(t, d, core))
        for k in range(2):
            for d in range(2):
                if k == 0:
                    across(t, d).wait_recv()
                rows = slice(k * half, (k + 1) * half)
                value = values[d][rows] + sibbuf[t, rows, spans[d]].astype(F32)
                if t > 0:
                    onward(t - 1, d, k).wait_recv()
                    value = value + rbuf[t - 1, rows, spans[d]].astype(F32)
                if t < n - 1:
                    sbuf[t, rows, spans[d]] = value.astype(BF)
                    onward(t, d, k).start()
                else:
                    o_ref[rows, spans[d]] = value
        if beside and t == 0:
            for load in loads:
                load.wait()
        if beside:
            slab = act.shape[1] // n
            rows = slice(t * slab, (t + 1) * slab)
            grad = mm_tn(act[:, rows], a_ref[...])
            nope_ref[rows, :] = grad[:, :NOPE].astype(BF)
            rope_ref[rows, :] = grad[:, KV_END:QK_END].astype(BF)
        if beside and t == 1:
            expand_ref[...] = mm_tn(cn[...], a_ref[:, NOPE:KV_END]).astype(BF)
    for t in range(n):
        for d in range(2):
            across(t, d).wait_send()
            if t < n - 1:
                for k in range(2):
                    onward(t, d, k).wait_send()
    for copy in swapped:
        copy.wait()


def ring_scatter(a, w, collective_id, swaps=(), beside=()):
    devices = lax.axis_size("seq")
    n = devices // 2
    rows = a.shape[0] // devices
    columns = w.shape[0]
    cut = columns // 256 * 128
    vmem = pl.BlockSpec(memory_space=pltpu.VMEM)
    anywhere = [pl.BlockSpec(memory_space=pl.ANY)] * len(swaps)
    grads, held = [], []
    if beside:
        width, rank = (x.shape[1] for x in beside)
        grads = [jax.ShapeDtypeStruct(shape, BF) for shape in ((width, NOPE), (width, ROPE), (rank, NOPE + V_DIM))]
        held = [pltpu.VMEM(x.shape, BF) for x in beside] + [pltpu.SemaphoreType.DMA((2,))]
    out, *taken = pl.pallas_call(
        functools.partial(scatter_kernel, n, cut, len(swaps), len(beside) > 0),
        out_shape=[jax.ShapeDtypeStruct((rows, columns), F32)] + swap_shapes(swaps) + grads,
        in_specs=[vmem, vmem] + anywhere + [pl.BlockSpec(memory_space=pl.ANY)] * len(beside),
        out_specs=[vmem] + anywhere + [vmem] * len(grads),
        scratch_shapes=[
            pltpu.VMEM((n, rows, columns), BF),
            pltpu.VMEM((n, rows, columns), BF),
            pltpu.VMEM((n - 1, rows, columns), BF),
            pltpu.VMEM((n - 1, rows, columns), BF),
        ]
        + [pltpu.SemaphoreType.DMA((n - 1, 2, 2))] * 2
        + [pltpu.SemaphoreType.DMA((n, 2))] * 2
        + [pltpu.SemaphoreType.DMA((max(1, len(swaps)), 2))]
        + held,
        compiler_params=pltpu.CompilerParams(
            collective_id=collective_id, has_side_effects=True, vmem_limit_bytes=VMEM_LIMIT
        ),
        cost_estimate=COST,
        name="ring_scatter",
    )(a, w, *swap_arrays(swaps), *beside)
    return (out, *taken[len(swaps) :], taken[: len(swaps)])


def fsdp_gather(x, other=None):
    count = lax.axis_size("fsdp")
    if count != 2:
        return lax.all_gather(x, "fsdp", axis=0, tiled=True)
    first = lax.axis_index("fsdp") == 0
    return jnp.concatenate([jnp.where(first, x, other), jnp.where(first, other, x)], axis=0)


def fsdp_pick(x, owner, other):
    count = lax.axis_size("fsdp")
    if count != 2:
        return lax.dynamic_index_in_dim(lax.all_gather(x, "fsdp", axis=0), owner, 0, keepdims=False)
    return jnp.where(lax.axis_index("fsdp") == owner, x, other)


def fsdp_scatter(x, taken=None):
    if taken is None:
        return lax.psum_scatter(x.astype(BF), "fsdp", scatter_dimension=0, tiled=True).astype(F32)
    half = x.shape[0] // 2
    kept = lax.dynamic_slice_in_dim(x, lax.axis_index("fsdp") * half, half, 0)
    return kept.astype(F32) + taken.astype(F32)


def fsdp_sum(x, taken=None):
    return lax.psum(x, "fsdp") if taken is None else x + taken


def turn(values, cosine, sine):
    half = values.shape[-1] // 2
    turned = jnp.concatenate([-values[:, half:], values[:, :half]], axis=-1)
    return values * cosine + turned * sine


def turn_back(gradient, cosine, sine):
    half = gradient.shape[-1] // 2
    scaled = gradient * sine
    return gradient * cosine + jnp.concatenate([scaled[:, half:], -scaled[:, :half]], axis=-1)


def spans_of(length):
    step = length // 8
    for i in range(8):
        start = i * step
        yield start, step, max(0, start - (3 * step if i % 2 == 0 else 2 * step))


def allowed_of(seg_col, seg_row, start, step, low):
    width = start + step - low
    query = start + lax.broadcasted_iota(jnp.int32, (step, width), 0)
    key = low + lax.broadcasted_iota(jnp.int32, (step, width), 1)
    return (key <= query) & (seg_col[start : start + step, :] == seg_row[:, low : start + step])


def attend_block(start, step, low, qh_ref, kh_ref, v_ref, segc_ref, segr_ref, heads_ref, lse_ref):
    end = start + step
    scores = mm_nt(qh_ref[start:end, :], kh_ref[low:end, :]) * SCALE
    scores = jnp.where(allowed_of(segc_ref, segr_ref, start, step, low), scores, NEG)
    peak = jnp.max(scores, axis=-1, keepdims=True)
    raised = jnp.exp(scores - peak)
    total = jnp.sum(raised, axis=-1, keepdims=True)
    prob = (raised * (1.0 / total)).astype(BF)
    heads_ref[start:end, :] = mm(prob, v_ref[low:end, :]).astype(BF)
    lse_ref[start:end, :] = peak + jnp.log(total)


def weights_back(wb_ref, wq, we):
    width = wq.shape[0]
    rank = we.shape[0]
    wb_ref[:, :] = jnp.zeros(wb_ref.shape, BF)
    wb_ref[:width, :NOPE] = wq[:, :NOPE]
    wb_ref[:width, KV_END:QK_END] = wq[:, NOPE:]
    wb_ref[width : width + rank, NOPE:KV_END] = we[...]
    shape = (ROPE, 2 * ROPE)
    eye = lax.broadcasted_iota(jnp.int32, shape, 0) + ROPE == lax.broadcasted_iota(jnp.int32, shape, 1)
    wb_ref[width + rank : width + rank + ROPE, KV_END:] = eye.astype(F32).astype(BF)


def front_kernel(count, swaps, chunks, *refs):
    wq_parts, wl_parts, we_parts = refs[:count], refs[count : 2 * count], refs[2 * count : 3 * count]
    x_ref, gain_ref, lgain_ref, cos_ref, sin_ref, segc_ref, segr_ref = refs[3 * count : 3 * count + 7]
    refs = refs[3 * count + 7 :]
    gives, refs = refs[:swaps], refs[swaps:]
    act_ref, cn_ref, qh_ref, kh_ref, v_ref, heads_ref, lse_ref, wb_ref = refs[:8]
    takes, refs = refs[8 : 8 + swaps], refs[8 + swaps :]
    wq, wl, we, sems, swap_sems = refs
    i = pl.program_id(0)
    length = qh_ref.shape[0]
    step = length // chunks
    swapped = swap_copies(gives, takes, swap_sems) if swaps else []
    copies = [fill(p, w, sems.at[j]) for j, (p, w) in enumerate(((wq_parts, wq), (wl_parts, wl), (we_parts, we)))]
    start_first(copies)

    @pl.when(i == 0)
    def _():
        if swaps:
            greet((), True)
            for copy in swapped:
                copy.start()

    wait_first(copies)

    @pl.when(i < chunks)
    def _():
        rows = pl.ds(pl.multiple_of(i * step, step), step)
        x = x_ref[...].astype(F32)
        act_ref[...] = (x * norm_scale(x) * gain_ref[...]).astype(BF)
        cosine, sine = cos_ref[...], sin_ref[...]
        query = mm(act_ref[...], wq[...])
        qh_ref[rows, :NOPE] = query[:, :NOPE].astype(BF)
        qh_ref[rows, NOPE:] = turn(query[:, NOPE:].astype(BF).astype(F32), cosine, sine).astype(BF)
        latent = mm(act_ref[...], wl[...])
        comp = latent[:, :KV_RANK]
        cn_ref[...] = (comp * norm_scale(comp) * lgain_ref[...]).astype(BF)
        kh_ref[rows, NOPE:] = turn(latent[:, KV_RANK:].astype(BF).astype(F32), cosine, sine).astype(BF)
        kv = mm(cn_ref[...], we[...])
        kh_ref[rows, :NOPE] = kv[:, :NOPE].astype(BF)
        v_ref[rows, :] = kv[:, NOPE:].astype(BF)

    @pl.when(i == chunks)
    def _():
        for start, size, low in spans_of(length):
            attend_block(start, size, low, qh_ref, kh_ref, v_ref, segc_ref, segr_ref, heads_ref, lse_ref)
        weights_back(wb_ref, wq, we)
        for copy in swapped:
            copy.wait()


def front(pieces, x, gain, lgain, cosine, sine, seg_col, seg_row, swaps, collective_id):
    length, width = x.shape
    chunks = 4
    step = length // chunks
    count = len(pieces[0])
    vmem = pl.BlockSpec(memory_space=pltpu.VMEM)
    anywhere = pl.BlockSpec(memory_space=pl.ANY)

    def tile(columns):
        return pl.BlockSpec((step, columns), lambda i: (jnp.minimum(i, chunks - 1), 0))

    def held(rows, columns):
        return pl.BlockSpec((rows, columns), lambda i: (0, 0))

    full = lambda group: (group[0].shape[0] * count, group[0].shape[1])
    backs = (width + KV_RANK + 2 * ROPE, QK_END + ROPE)
    outs = [
        (tile(width), (length, width), BF),
        (tile(KV_RANK), (length, KV_RANK), BF),
        (held(length, QD), (length, QD), BF),
        (held(length, QD), (length, QD), BF),
        (held(length, V_DIM), (length, V_DIM), BF),
        (held(length, V_DIM), (length, V_DIM), BF),
        (held(length, 1), (length, 1), F32),
        (held(*backs), backs, BF),
    ]
    return pl.pallas_call(
        functools.partial(front_kernel, count, len(swaps), chunks),
        grid=(chunks + 1,),
        out_shape=[jax.ShapeDtypeStruct(shape, dtype) for _, shape, dtype in outs]
        + [jax.ShapeDtypeStruct(w.shape, w.dtype) for w in swaps],
        in_specs=[anywhere] * (3 * count) + [tile(width), vmem, vmem, tile(ROPE), tile(ROPE), vmem, vmem]
        + [anywhere] * len(swaps),
        out_specs=[spec for spec, _, _ in outs] + [anywhere] * len(swaps),
        scratch_shapes=[pltpu.VMEM(full(group), BF) for group in pieces]
        + [pltpu.SemaphoreType.DMA((3, count)), pltpu.SemaphoreType.DMA((max(1, len(swaps)), 2))],
        compiler_params=pltpu.CompilerParams(
            vmem_limit_bytes=VMEM_LIMIT, collective_id=collective_id, has_side_effects=len(swaps) > 0
        ),
        cost_estimate=COST,
        name="front",
    )(*sum(pieces, ()), x, gain, lgain, cosine, sine, seg_col, seg_row, *swaps)


def attend_back_kernel(*refs):
    qh_ref, kh_ref, v_ref, lse_ref, heads_ref, da_ref, wo_ref, cos_ref, sin_ref, segc_ref, segr_ref = refs[:11]
    back_ref, gout_ref, dk_acc, dv_acc = refs[11:]
    dk_acc[...] = jnp.zeros_like(dk_acc)
    dv_acc[...] = jnp.zeros_like(dv_acc)
    for start, step, low in spans_of(qh_ref.shape[0]):
        end = start + step
        query = qh_ref[start:end, :]
        grad = mm_nt(da_ref[start:end, :], wo_ref[...]).astype(BF)
        keys = kh_ref[low:end, :]
        scores = mm_nt(query, keys) * SCALE
        allowed = allowed_of(segc_ref, segr_ref, start, step, low)
        prob = jnp.where(allowed, jnp.exp(scores - lse_ref[start:end, :]), 0.0)
        dv_acc[low:end, :] += mm_tn(prob.astype(BF), grad)
        dprob = mm_nt(grad, v_ref[low:end, :])
        delta = jnp.sum(prob * dprob, axis=-1, keepdims=True)
        dscore = (prob * (dprob - delta) * SCALE).astype(BF)
        dquery = mm(dscore, keys)
        back_ref[start:end, :NOPE] = dquery[:, :NOPE].astype(BF)
        turned = turn_back(dquery[:, NOPE:], cos_ref[start:end, :], sin_ref[start:end, :])
        back_ref[start:end, KV_END:QK_END] = turned.astype(BF)
        dk_acc[low:end, :] += mm_tn(dscore, query)
    back_ref[:, NOPE : 2 * NOPE] = dk_acc[:, :NOPE].astype(BF)
    back_ref[:, 2 * NOPE : KV_END] = dv_acc[...].astype(BF)
    back_ref[:, QK_END:] = turn_back(dk_acc[:, NOPE:], cos_ref[...], sin_ref[...]).astype(BF)
    gout_ref[...] = mm_tn(heads_ref[...], da_ref[...]).astype(BF)


def attend_back(*operands):
    length, width = operands[5].shape
    vmem = pl.BlockSpec(memory_space=pltpu.VMEM)
    return pl.pallas_call(
        attend_back_kernel,
        out_shape=[jax.ShapeDtypeStruct((length, QK_END + ROPE), BF), jax.ShapeDtypeStruct((V_DIM, width), BF)],
        in_specs=[vmem] * len(operands),
        out_specs=[vmem, vmem],
        scratch_shapes=[pltpu.VMEM((length, QD), F32), pltpu.VMEM((length, V_DIM), F32)],
        compiler_params=pltpu.CompilerParams(vmem_limit_bytes=VMEM_LIMIT),
        cost_estimate=COST,
        name="attend_back",
    )(*operands)


def fsdp_pieces(x, other):
    if lax.axis_size("fsdp") != 2:
        return (lax.all_gather(x, "fsdp", axis=0, tiled=True),)
    return (x, other)


def fill(pieces, dst, sems):
    if len(pieces) == 1:
        return [pltpu.make_async_copy(pieces[0], dst, sems.at[0])]
    part = lax.axis_index("fsdp")
    height = pieces[0].shape[0]
    starts = (part * height, (1 - part) * height)
    return [
        pltpu.make_async_copy(piece, dst.at[pl.ds(pl.multiple_of(start, height), height), :], sems.at[i])
        for i, (piece, start) in enumerate(zip(pieces, starts))
    ]


def picks(slot_ref, share_ref, b, most):
    slots = slot_ref[b]
    pick = slots == lax.broadcasted_iota(jnp.int32, (most, slots.shape[1]), 0)
    return pick.astype(BF), jnp.sum(jnp.where(pick, share_ref[b], 0.0), axis=-1, keepdims=True)


def hidden_spans(hidden):
    cut = -(-hidden // 256) * 128
    return ((0, cut), (cut, hidden))


def start_first(groups):
    @pl.when(pl.program_id(0) == 0)
    def _():
        for group in groups:
            for copy in group:
                copy.start()


def wait_first(groups):
    @pl.when(pl.program_id(0) == 0)
    def _():
        for group in groups:
            for copy in group:
                copy.wait()


def expert_in_kernel(count, most, swaps, *refs):
    wg_parts, wu_parts = refs[:count], refs[count : 2 * count]
    act_ref, slot_ref, share_ref, wsgu_ref, wsd_ref, g_ref = refs[2 * count : 2 * count + 6]
    gives, refs = refs[2 * count + 6 : 2 * count + 6 + swaps], refs[2 * count + 6 + swaps :]
    xe_ref, ge_ref, ue_ref, he_ref, sh_ref, dye_ref, dsgu_ref, ys_ref, ds_ref = refs[:9]
    takes, (wg, wu, sems, swap_sems) = refs[9 : 9 + swaps], refs[9 + swaps :]
    swapped = swap_copies(gives, takes, swap_sems) if swaps else []
    if swaps:

        @pl.when(pl.program_id(0) == 0)
        def _():
            greet((), True)
            for copy in swapped:
                copy.start()

    copies = [fill(wg_parts, wg, sems.at[0]), fill(wu_parts, wu, sems.at[1])]
    start_first(copies)
    blocks, rows = slot_ref.shape[0], slot_ref.shape[2]
    for b in range(blocks):
        pick, share = picks(slot_ref, share_ref, b, most)
        block, packed = slice(b * rows, (b + 1) * rows), slice(b * most, (b + 1) * most)
        xe_ref[packed, :] = mm(pick, act_ref[block, :]).astype(BF)
        dye_ref[packed, :] = (share * mm(pick, g_ref[block, :])).astype(BF)
    sgu = mm(act_ref[...], wsgu_ref[...])
    units = sh_ref.shape[1]
    sg, su = sgu[:, :units], sgu[:, units:]
    sig = jax.nn.sigmoid(sg)
    sh_ref[...] = (sg * sig * su).astype(BF)
    dsh = mm_nt(g_ref[...], wsd_ref[...])
    dsgu_ref[:, :units] = (dsh * su * sig * (1.0 + sg * (1.0 - sig))).astype(BF)
    dsgu_ref[:, units:] = (dsh * sg * sig).astype(BF)
    ys_ref[...] = mm(sh_ref[...], wsd_ref[...]).astype(BF)
    ds_ref[...] = mm_nt(dsgu_ref[...], wsgu_ref[...]).astype(BF)
    wait_first(copies)
    for low, high in hidden_spans(wg.shape[1]):
        ge = mm(xe_ref[...], wg[:, low:high])
        ue = mm(xe_ref[...], wu[:, low:high])
        ge_ref[:, low:high] = ge
        ue_ref[:, low:high] = ue
        he_ref[:, low:high] = (ge * jax.nn.sigmoid(ge) * ue).astype(BF)
    if swaps:

        @pl.when(pl.program_id(0) == pl.num_programs(0) - 1)
        def _():
            for copy in swapped:
                copy.wait()


def expert_out_kernel(count, most, swaps, *refs):
    wd_parts = refs[:count]
    he_ref, slot_ref, share_ref, ys_ref, y_ref, wd, sems, _ = refs[count:]
    copies = [fill(wd_parts, wd, sems.at[0])]
    start_first(copies)
    wait_first(copies)
    blocks, rows = slot_ref.shape[0], slot_ref.shape[2]
    z = mm(he_ref[...], wd[...]).astype(BF)
    for b in range(blocks):
        pick, share = picks(slot_ref, share_ref, b, most)
        ye = z[b * most : (b + 1) * most, :].astype(F32)
        ys = ys_ref[b * rows : (b + 1) * rows, :].astype(F32)
        y_ref[b * rows : (b + 1) * rows, :] = (ys + mm_tn(pick, (share * ye).astype(BF))).astype(BF)


def expert_back_kernel(n, cut, count, most, swaps, *refs):
    wg_parts, wu_parts, wd_parts = refs[:count], refs[count : 2 * count], refs[2 * count : 3 * count]
    dye_ref, slot_ref, share_ref, part_ref, ge_ref, ue_ref, ds_ref = refs[3 * count : 3 * count + 7]
    dact_ref, dge_ref, due_ref, y_ref = refs[3 * count + 7 : 3 * count + 11]
    wg, wu, wd, sems, _, *buffers = refs[3 * count + 11 :]
    copies = [fill(p, w, sems.at[i]) for i, (p, w) in enumerate(((wg_parts, wg), (wu_parts, wu), (wd_parts, wd)))]
    start_first(copies)
    middle, finish = scatter_in_grid(pl.program_id(0), n, cut, part_ref, y_ref, buffers)
    blocks, rows = slot_ref.shape[0], slot_ref.shape[2]
    wait_first(copies)
    for low, high in hidden_spans(wg.shape[1]):
        dhe = mm_nt(dye_ref[...], wd[low:high, :])
        ge, ue = ge_ref[:, low:high], ue_ref[:, low:high]
        sig = jax.nn.sigmoid(ge)
        dge_ref[:, low:high] = (dhe * ue * sig * (1.0 + ge * (1.0 - sig))).astype(BF)
        due_ref[:, low:high] = (dhe * ge * sig).astype(BF)
    middle()
    dxe = (mm_nt(dge_ref[...], wg[...]) + mm_nt(due_ref[...], wu[...])).astype(BF)
    for b in range(blocks):
        pick, _ = picks(slot_ref, share_ref, b, most)
        block = slice(b * rows, (b + 1) * rows)
        shared = ds_ref[block, :].astype(F32)
        dact_ref[block, :] = (shared + mm_tn(pick, dxe[b * most : (b + 1) * most, :])).astype(BF)
    finish()


def expert_call(kernel, name, pieces, most, steps, slot, share, whole, tiled, outs, swaps=(), collective_id=None, summed=None):
    devices, rows = slot.shape[0], slot.shape[2]
    per = devices // steps
    anywhere = pl.BlockSpec(memory_space=pl.ANY)
    vmem = pl.BlockSpec(memory_space=pltpu.VMEM)

    def tile(total, columns):
        return pl.BlockSpec((total // steps, columns), lambda i: (i, 0))

    cut = pl.BlockSpec((per, 1, rows), lambda i: (i, 0, 0))
    count = len(pieces[0])
    full = lambda group: (group[0].shape[0] * count, group[0].shape[1])
    buffers, kept = [], []
    if summed is not None:
        buffers = scatter_buffers(devices // 2, *summed)
        kept = [(pl.BlockSpec(summed, lambda i: (0, 0)), jax.ShapeDtypeStruct(summed, F32))]
    return pl.pallas_call(
        functools.partial(kernel, count, most, len(swaps)),
        grid=(steps,),
        out_shape=[jax.ShapeDtypeStruct((total, columns), dtype) for total, columns, dtype in outs]
        + [shape for _, shape in kept]
        + [jax.ShapeDtypeStruct(x.shape, x.dtype) for x in swaps],
        in_specs=[anywhere] * (len(pieces) * count) + [tile(*tiled[0].shape), cut, cut] + [vmem] * len(whole)
        + [tile(*t.shape) for t in tiled[1:]]
        + [anywhere] * len(swaps),
        out_specs=[tile(total, columns) for total, columns, _ in outs]
        + [spec for spec, _ in kept]
        + [anywhere] * len(swaps),
        scratch_shapes=[pltpu.VMEM(full(group), BF) for group in pieces]
        + [pltpu.SemaphoreType.DMA((len(pieces), count)), pltpu.SemaphoreType.DMA((max(1, len(swaps)), 2))]
        + buffers,
        compiler_params=pltpu.CompilerParams(
            vmem_limit_bytes=VMEM_LIMIT, collective_id=collective_id, has_side_effects=collective_id is not None
        ),
        cost_estimate=COST,
        name=name,
    )(*sum(pieces, ()), tiled[0], slot, share, *whole, *tiled[1:], *swaps)


def widen_query(nope, rope):
    devices, rows, _ = nope.shape
    steps = 8
    step = rows // steps

    def kernel(n_ref, r_ref, o_ref):
        def put(first):
            for d in range(devices):
                o_ref[:, d * QD : d * QD + NOPE] = n_ref[d].astype(F32)
                o_ref[:, d * QD + NOPE : (d + 1) * QD] = r_ref[d, :, first : first + ROPE].astype(F32)

        low = pl.program_id(0) < steps // 2
        pl.when(low)(lambda: put(0))
        pl.when(jnp.logical_not(low))(lambda: put(ROPE))

    return pl.pallas_call(
        kernel,
        grid=(steps,),
        out_shape=jax.ShapeDtypeStruct((rows, devices * QD), F32),
        in_specs=[
            pl.BlockSpec((devices, step, NOPE), lambda i: (0, i, 0)),
            pl.BlockSpec((devices, step, 2 * ROPE), lambda i: (0, i % (steps // 2), 0)),
        ],
        out_specs=pl.BlockSpec((step, devices * QD), lambda i: (i, 0)),
        compiler_params=pltpu.CompilerParams(vmem_limit_bytes=VMEM_LIMIT),
        cost_estimate=COST,
        name="wide_query",
    )(nope, rope)


def trim(stacks, share):
    devices, _, width = stacks[0].shape
    if share % 8:
        return jnp.concatenate(stacks, axis=1)[:, :share].reshape(-1, width).astype(F32)

    def kernel(*refs):
        *i_refs, o_ref = refs
        for d in range(i_refs[0].shape[0]):
            at = d * share
            for i_ref in i_refs:
                height = min(i_ref.shape[1], (d + 1) * share - at)
                o_ref[at : at + height, :] = i_ref[d, :height, :].astype(F32)
                at += height

    return pl.pallas_call(
        kernel,
        grid=(4,),
        out_shape=jax.ShapeDtypeStruct((devices * share, width), F32),
        in_specs=[pl.BlockSpec((devices // 4, x.shape[1], width), lambda i: (i, 0, 0)) for x in stacks],
        out_specs=pl.BlockSpec((devices // 4 * share, width), lambda i: (i, 0)),
        compiler_params=pltpu.CompilerParams(vmem_limit_bytes=VMEM_LIMIT),
        cost_estimate=COST,
        name="trim",
    )(*stacks)


def scatter_in_grid(t, n, cut, part_ref, o_ref, buffers):
    sibbuf, rbuf, sbuf, send, recv, fsend, frecv = buffers
    me, core, r, _ = ring_place()
    targets = (ring_seq((r + 1) % n, core, n), ring_seq((r + n - 1) % n, core, n))
    sibling = ring_seq(r, 1 - core, n)
    columns = o_ref.shape[1]
    spans = (pl.ds(0, cut), pl.ds(cut, columns - cut))

    def block(step, d, c):
        return ring_seq((r + (-step - 1 if d == 0 else step + 1) + n) % n, c, n)

    def across(step, d):
        source = part_ref.at[block(step, d, 1 - core), :, spans[d]]
        return remote(source, sibbuf.at[step, :, spans[d]], fsend.at[step, d], frecv.at[step, d], sibling)

    height = o_ref.shape[0] // 2

    def onward(step, d, k):
        at = (step, pl.ds(k * height, height), spans[d])
        return remote(sbuf.at[at], rbuf.at[at], send.at[step, d, k], recv.at[step, d, k], targets[d])

    @pl.when(t == 0)
    def _():
        greet((*targets, sibling))
        for step in range(2):
            for d in range(2):
                across(step, d).start()

    @pl.when(t < n - 2)
    def _():
        for d in range(2):
            across(t + 2, d).start()

    def advance(k):
        rows = pl.ds(k * height, height)
        for d in range(2):
            if k == 0:
                across(t, d).wait_recv()

            def both():
                return part_ref[block(t, d, core), rows, spans[d]].astype(F32) + sibbuf[t, rows, spans[d]].astype(F32)

            @pl.when(t == 0)
            def _():
                sbuf[0, rows, spans[d]] = both().astype(BF)
                onward(0, d, k).start()

            @pl.when((t > 0) & (t < n - 1))
            def _():
                onward(t - 1, d, k).wait_recv()
                sbuf[t, rows, spans[d]] = (both() + rbuf[t - 1, rows, spans[d]].astype(F32)).astype(BF)
                onward(t, d, k).start()

            @pl.when(t == n - 1)
            def _():
                onward(n - 2, d, k).wait_recv()
                o_ref[rows, spans[d]] = both() + rbuf[n - 2, rows, spans[d]].astype(F32)

    def finish():
        @pl.when(t == n - 1)
        def _():
            for step in range(n):
                for d in range(2):
                    across(step, d).wait_send()
                    if step < n - 1:
                        for k in range(2):
                            onward(step, d, k).wait_send()

    advance(0)
    return lambda: advance(1), finish


def scatter_buffers(n, rows, columns):
    return (
        [pltpu.VMEM((n, rows, columns), BF), pltpu.VMEM((n - 1, rows, columns), BF), pltpu.VMEM((n - 1, rows, columns), BF)]
        + [pltpu.SemaphoreType.DMA((n - 1, 2, 2))] * 2
        + [pltpu.SemaphoreType.DMA((n, 2))] * 2
    )


def weight_grads_kernel(n, cut, parts, *refs):
    xe_ref, dge_ref, due_ref, he_ref, dye_ref, act_ref, dsgu_ref, sh_ref, g_ref, part_ref = refs[:10]
    o_ref, gate_ref, up_ref, down_ref, sgu_ref, sdown_ref = refs[10:16]
    middle, finish = scatter_in_grid(pl.program_id(0), n, cut, part_ref, o_ref, refs[16:])
    gate_ref[...] = mm_tn(xe_ref[...], dge_ref[...]).astype(BF)
    sgu_ref[...] = mm_tn(act_ref[...], dsgu_ref[...]).astype(BF)
    middle()
    up_ref[...] = mm_tn(xe_ref[...], due_ref[...]).astype(BF)
    down_ref[...] = mm_tn(he_ref[...], dye_ref[...]).astype(BF)
    sdown = mm_tn(sh_ref[...], g_ref[...]).astype(BF)
    share = sdown.shape[0] // parts
    room = sdown_ref.shape[0] // parts
    for p in range(parts):
        sdown_ref[p * room : p * room + share, :] = sdown[p * share : (p + 1) * share, :]
        if room > share:
            sdown_ref[p * room + share : (p + 1) * room, :] = jnp.zeros((room - share, sdown.shape[1]), BF)

    finish()


def weight_grads(xe, dge, due, he, dye, act, dsgu, sh, g, part, parts, room, collective_id):
    devices = lax.axis_size("seq")
    n = devices // 2
    length, columns = part.shape
    rows = length // devices
    cut = columns // 256 * 128

    def tile(x):
        return pl.BlockSpec((x.shape[0], x.shape[1] // n), lambda i: (0, i))

    def held(x):
        return pl.BlockSpec(memory_space=pltpu.VMEM)

    ff, units = dge.shape[1], dsgu.shape[1]
    slab = columns // n
    down = lambda width: pl.BlockSpec((slab, width), lambda i: (i, 0))
    along = lambda height: pl.BlockSpec((height, slab), lambda i: (0, i))
    return pl.pallas_call(
        functools.partial(weight_grads_kernel, n, cut, parts),
        grid=(n,),
        out_shape=[jax.ShapeDtypeStruct((rows, columns), F32)]
        + [
            jax.ShapeDtypeStruct(shape, BF)
            for shape in ((columns, ff), (columns, ff), (ff, columns), (columns, units), (parts * room, columns))
        ],
        in_specs=[tile(xe), held(dge), held(due), held(he), tile(dye), tile(act), held(dsgu), held(sh), tile(g)]
        + [held(part)],
        out_specs=[pl.BlockSpec((rows, columns), lambda i: (0, 0)), down(ff), down(ff), along(ff)]
        + [down(units), along(parts * room)],
        scratch_shapes=scatter_buffers(n, rows, columns),
        compiler_params=pltpu.CompilerParams(
            collective_id=collective_id, has_side_effects=True, vmem_limit_bytes=VMEM_LIMIT
        ),
        cost_estimate=COST,
        name="weight_grads",
    )(xe, dge, due, he, dye, act, dsgu, sh, g, part.reshape(devices, rows, columns))


def widen(stacked, count, parts, name):
    devices, rows, columns = stacked.shape
    share = columns // parts // count
    width = devices * columns // count
    steps = 8

    def kernel(i_ref, *o_refs):
        for j, o_ref in enumerate(o_refs):
            for p in range(parts):
                for d in range(devices):
                    at, source = (p * devices + d) * share, (j * parts + p) * share
                    o_ref[:, at : at + share] = i_ref[d, :, source : source + share].astype(F32)

    return pl.pallas_call(
        kernel,
        grid=(steps,),
        out_shape=[jax.ShapeDtypeStruct((rows, width), F32)] * count,
        in_specs=[pl.BlockSpec((devices, rows // steps, columns), lambda i: (0, i, 0))],
        out_specs=[pl.BlockSpec((rows // steps, width), lambda i: (i, 0))] * count,
        compiler_params=pltpu.CompilerParams(vmem_limit_bytes=VMEM_LIMIT),
        cost_estimate=COST,
        name=name,
    )(stacked)


def columns_of(weight, at, width):
    return lax.dynamic_slice_in_dim(weight, at * width, width, 1).astype(BF)


def rows_of(weight, at, height):
    return lax.dynamic_slice_in_dim(weight, at * height, height, 0).astype(BF)


def per_device(
    tokens,
    segment_ids,
    routes,
    gate_weights,
    out_grad,
    attn_gain,
    q_weight,
    latent_weight,
    latent_gain,
    kv_weight,
    out_weight,
    ffn_gain,
    shared_gate,
    shared_up,
    shared_down,
    expert_gate,
    expert_up,
    expert_down,
):
    _, rows, width = tokens.shape
    devices = lax.axis_size("seq")
    at = lax.axis_index("seq")
    parts = lax.axis_size("fsdp")
    part = lax.axis_index("fsdp")
    length = rows * devices
    own_x = tokens[0]
    own_g = out_grad[0]

    per, per_latent = attn_gain.shape[0], latent_gain.shape[0]
    gains = jnp.concatenate([attn_gain, ffn_gain, latent_gain]).astype(BF)
    gains_size = gains.shape[0]
    gains_rows = -(-gains_size // 2048) * 16
    gains = jnp.pad(gains, (0, gains_rows * 128 - gains_size)).reshape(gains_rows, 128)
    out_rows = out_weight.shape[0]
    early_latent = 2
    share = shared_down.shape[0] // devices
    share_pad = -(-share // 32) * 32
    sdown = jnp.pad(rows_of(shared_down, at, share), ((0, share_pad - share), (0, 0)))
    early = (
        gains,
        columns_of(q_weight, at, QD),
        latent_weight.astype(BF),
        columns_of(kv_weight, at, NOPE + V_DIM),
        lax.dynamic_slice_in_dim(out_weight, at * V_DIM % out_rows, V_DIM, 0).astype(BF),
    )
    pair = parts == 2

    def crossing(*arrays):
        return arrays if pair else ()

    def crossed(taken, count):
        return taken if pair else [None] * count

    experts = jnp.arange(devices, dtype=jnp.int32)
    spread = jnp.sum(
        jnp.where(routes[0].T[None, :, :] == experts[:, None, None], gate_weights[0].T[None, :, :], 0.0), axis=1
    )
    x_all, spread_all, *others = ring_gather_many(
        [own_x, spread],
        8,
        None,
        crossing(*early),
        early_latent if pair else None,
        (expert_gate[0], expert_up[0], expert_down[0]),
    )
    others, (egate, eup, edown) = others[:-3], others[-3:]
    late_g, x_all = lax.optimization_barrier((own_g, x_all.reshape(length, width)))
    g_all = lax.all_gather(late_g, "seq", axis=0, tiled=True)
    share_of = lax.dynamic_index_in_dim(spread_all, at, 1, keepdims=False)
    others = crossed(others, len(early))
    gains = fsdp_gather(gains, others[0]).reshape(parts, -1)[:, :gains_size].astype(F32)
    gain_one = gains[:, :per].reshape(1, -1)
    gain_two = gains[:, per : 2 * per].reshape(1, -1)
    gain_lat = gains[:, 2 * per :].reshape(1, -1)
    w_latent = fsdp_gather(early[2], others[2])
    w_out = fsdp_pick(early[4], at * V_DIM // out_rows, others[4])

    hidden = shared_down.shape[0] * parts

    def shared_columns(weight):
        pieces = [
            lax.dynamic_slice_in_dim(weight, p * (hidden // parts) + at * share, share, 1) for p in range(parts)
        ]
        return pieces

    sgu = jnp.concatenate(shared_columns(shared_gate) + shared_columns(shared_up), axis=1).astype(BF)

    cosine, sine = rope_tables(length)
    seg_col, seg_row = segment_ids.reshape(length, 1), segment_ids
    act_one, cnorm, qh, kh, values, heads, lse, w_back, *taken = front(
        tuple(fsdp_pieces(early[i], others[i]) for i in (1, 2, 3)),
        x_all,
        gain_one,
        gain_lat,
        cosine,
        sine,
        seg_col,
        seg_row,
        crossing(sgu, sdown),
        11 if pair else None,
    )
    sgu_other, sdown_other = crossed(taken, 2)
    own_xf = own_x.astype(F32)
    attended, taken = ring_scatter(heads, w_out.T, 2, crossing(egate))
    (egate_other,) = crossed(taken, 1)
    x1 = own_xf + attended
    r3 = norm_scale(x1)
    act_two = (x1 * r3 * gain_two).astype(BF)
    act_all, taken = ring_gather(act_two, 9, crossing(eup))
    (eup_other,) = crossed(taken, 1)
    w_egate, w_eup = fsdp_pieces(egate, egate_other), fsdp_pieces(eup, eup_other)
    w_sgu = fsdp_gather(sgu, sgu_other)
    w_sdown = fsdp_gather(sdown[:share], sdown_other[:share] if pair else None)

    most = min(MOST, rows)
    named = share_of > 0.0
    rank = jnp.cumsum(named.astype(jnp.int32), axis=1) - 1
    slot = jnp.where(named, rank, -1)[:, None, :]
    share_of = share_of[:, None, :]
    packed = devices * most
    ff = expert_gate.shape[2]
    units = parts * share
    steps = 4
    xe, ge, ue, he, sh, dye, dsgu, ys, ds, *taken = expert_call(
        expert_in_kernel,
        "experts_in",
        (w_egate, w_eup),
        most,
        steps,
        slot,
        share_of,
        (w_sgu, w_sdown),
        (act_all, g_all),
        (
            (packed, width, BF),
            (packed, ff, F32),
            (packed, ff, F32),
            (packed, ff, BF),
            (length, units, BF),
            (packed, width, BF),
            (length, 2 * units, BF),
            (length, width, BF),
            (length, width, BF),
        ),
        crossing(edown),
        10 if pair else None,
    )
    (edown_other,) = crossed(taken, 1)
    w_edown = fsdp_pieces(edown, edown_other)
    (y_part,) = expert_call(
        expert_out_kernel,
        "experts_out",
        (w_edown,),
        most,
        steps,
        slot,
        share_of,
        (),
        (he, ys),
        ((length, width, BF),),
    )
    dact_part, dge, due, y_sum = expert_call(
        functools.partial(expert_back_kernel, devices // 2, width // 256 * 128),
        "experts_back",
        (w_egate, w_eup, w_edown),
        most,
        devices // 2,
        slot,
        share_of,
        (y_part.reshape(devices, rows, width),),
        (dye, ge, ue, ds),
        ((length, width, BF), (packed, ff, BF), (packed, ff, BF)),
        (),
        12,
        (rows, width),
    )
    dact_two, grad_egate, grad_eup, grad_edown, grad_sgu, grad_sdown = weight_grads(
        xe, dge, due, he, dye, act_all, dsgu, sh, g_all, dact_part, parts, share_pad, 3
    )
    own_gf = own_g.astype(F32)
    grad_gain_two = jnp.sum(dact_two * x1 * r3, axis=0)
    dx1 = own_gf + norm_back(x1, r3, dact_two * gain_two)
    dattn_all, taken = ring_gather(dx1.astype(BF), 1, (given(grad_sgu), given(grad_sdown)) if pair else ())
    sgu_taken, sdown_taken = crossed(taken, 2)
    grad_sgu = fsdp_scatter(grad_sgu, sgu_taken).astype(BF)
    grad_sdown = fsdp_scatter(grad_sdown, sdown_taken).astype(BF)
    output = (x1 + y_sum).astype(BF)

    back, grad_out = attend_back(qh, kh, values, lse, heads, dattn_all, w_out, cosine, sine, seg_col, seg_row)
    summed, grad_nope, grad_rope, grad_expand, taken = ring_scatter(
        back, w_back, 4, (given(grad_edown),) if pair else (), (act_one, cnorm)
    )
    grad_edown = fsdp_scatter(grad_edown, *taken)

    r1 = norm_scale(own_xf)
    own_act = (own_xf * r1 * gain_one).astype(BF)
    own_comp = mm(own_act, w_latent)[:, :KV_RANK]
    r2 = norm_scale(own_comp)
    dcn = summed[:, width : width + KV_RANK]
    grad_gain_lat = jnp.sum(dcn * own_comp * r2, axis=0)
    dcomp = norm_back(own_comp, r2, dcn * gain_lat)
    dlatent = jnp.concatenate([dcomp, summed[:, width + KV_RANK : width + KV_RANK + ROPE]], axis=-1).astype(BF)
    dact_one = summed[:, :width] + mm_nt(dlatent, w_latent)
    grad_gain_one = jnp.sum(dact_one * own_xf * r1, axis=0)
    input_grad = dx1 + norm_back(own_xf, r1, dact_one * gain_one)

    small = jnp.concatenate([grad_gain_one, grad_gain_two, grad_gain_lat])
    small = jnp.pad(small, (0, 64 * 128 - small.shape[0])).reshape(64, 128)

    def in_part(device):
        return device * V_DIM // out_rows == lax.axis_index("fsdp")

    sgu_all, dlatent_all, sdown_all, *taken = ring_gather_many(
        [grad_sgu, dlatent, grad_sdown],
        5,
        None,
        (given(grad_nope), given(grad_rope), given(grad_expand), grad_out, small, given(grad_egate)) if pair else (),
    )
    nope_taken, rope_taken, expand_taken, out_taken, small_taken, egate_taken = crossed(taken, 6)
    grad_nope = fsdp_scatter(grad_nope, nope_taken).astype(BF)
    grad_rope = fsdp_scatter(grad_rope, rope_taken).astype(BF)
    grad_rope = jnp.concatenate(jnp.split(grad_rope, 2, axis=0), axis=1)
    grad_expand = fsdp_scatter(grad_expand, expand_taken).astype(BF)
    grad_out = fsdp_sum(grad_out, out_taken)
    small = fsdp_sum(small, small_taken)
    grad_egate = fsdp_scatter(grad_egate, egate_taken)
    slab = width // parts // devices
    act_cols = jnp.concatenate(
        [lax.dynamic_slice_in_dim(act_one, p * (width // parts) + at * slab, slab, 1) for p in range(parts)], axis=1
    )
    grad_latent = mm_tn(act_cols, dlatent_all.reshape(length, -1)).astype(BF)
    latent_taken = None
    if pair:
        latent_taken = lax.ppermute(
            lax.dynamic_slice_in_dim(grad_latent, (1 - part) * slab, slab, 0), "fsdp", [(0, 1), (1, 0)]
        )
    grad_latent = fsdp_scatter(grad_latent, latent_taken).astype(BF)
    latent_pad = -(-slab // 32) * 32
    nope_all, rope_all, expand_all, out_all, latent_all, small_all, *taken = ring_gather_many(
        [grad_nope, grad_rope, grad_expand, grad_out, jnp.pad(grad_latent, ((0, latent_pad - slab), (0, 0))), small],
        7,
        [None, None, None, in_part, None, None],
        (given(grad_eup),) if pair else (),
    )
    (eup_taken,) = crossed(taken, 1)
    grad_eup = fsdp_scatter(grad_eup, eup_taken)
    latent_all = latent_all[:, :slab]
    out_grad_own = lax.dynamic_slice_in_dim(
        out_all.reshape(devices * V_DIM, width), part * out_rows, out_rows, 0
    ).astype(F32)
    small = jnp.sum(small_all, axis=0).reshape(-1)
    wide_gate, wide_up = widen(sgu_all, 2, parts, "wide_shared")
    gain_rows = width // parts
    own_gains = [
        lax.dynamic_slice_in_dim(small, part * gain_rows, gain_rows),
        lax.dynamic_slice_in_dim(small, width + part * gain_rows, gain_rows),
        lax.dynamic_slice_in_dim(small, 2 * width + part * (KV_RANK // parts), KV_RANK // parts),
    ]
    return (
        output[None],
        input_grad[None],
        own_gains[0],
        widen_query(nope_all, rope_all),
        latent_all.reshape(-1, grad_latent.shape[1]).astype(F32),
        own_gains[2],
        widen(expand_all, 1, 1, "wide_kv")[0],
        out_grad_own,
        own_gains[1],
        wide_gate,
        wide_up,
        trim([sdown_all], share),
        grad_egate[None],
        grad_eup[None],
        grad_edown[None],
    )


def solution(mesh):
    token_spec = P("fsdp", "seq", None)
    row_spec = P("fsdp", None)
    gain_spec = P("fsdp")
    expert_spec = P("seq", "fsdp", None)
    dense = (gain_spec, row_spec, row_spec, gain_spec, row_spec, row_spec, gain_spec, row_spec, row_spec, row_spec)
    weights = dense + (expert_spec,) * 3
    return jax.shard_map(
        per_device,
        mesh=mesh,
        in_specs=(token_spec, row_spec, token_spec, token_spec, token_spec) + weights,
        out_specs=(token_spec, token_spec) + weights,
        check_vma=False,
    )
```

```python
import functools
import math

import jax
import jax.numpy as jnp
import numpy as np
from jax import lax
from jax.experimental import pallas as pl
from jax.experimental.pallas import tpu as pltpu
from jax.sharding import PartitionSpec as P

HEADS = 16
NOPE = 128
ROPE = 64
QD = NOPE + ROPE
KV_RANK = 512
V_DIM = 128
TOP = 6
MOST = 96

EPS = 1e-06
NEG = -1e30
THETA = 10000.0
SCALE = 1.0 / math.sqrt(QD)
KV_END = 2 * NOPE + V_DIM
QK_END = KV_END + ROPE
MESH = pl.DeviceIdType.MESH
BF = jnp.bfloat16
F32 = jnp.float32
VMEM_LIMIT = 60 * 2**20
COST = pl.CostEstimate(flops=0, bytes_accessed=2**20, transcendentals=0)


def norm_scale(values):
    return lax.rsqrt(jnp.mean(values * values, axis=-1, keepdims=True) + EPS)


def norm_back(values, inverse, gradient):
    return inverse * gradient - values * inverse * inverse * inverse * jnp.mean(
        gradient * values, axis=-1, keepdims=True
    )


def mm(a, b):
    return jnp.dot(a, b, preferred_element_type=F32)


def mm_tn(a, b):
    return lax.dot_general(a, b, (((0,), (0,)), ((), ())), preferred_element_type=F32)


def mm_nt(a, b):
    return lax.dot_general(a, b, (((1,), (1,)), ((), ())), preferred_element_type=F32)


def rope_tables(length):
    places = np.arange(length, dtype=np.float32)
    frequency = np.power(np.float32(THETA), np.arange(ROPE // 2, dtype=np.float32) * np.float32(-2.0 / ROPE))
    angles = places[:, None] * frequency[None, :].astype(np.float32)
    angles = np.concatenate([angles, angles], axis=-1)
    return jnp.asarray(np.cos(angles), F32), jnp.asarray(np.sin(angles), F32)


def ring_place():
    me = lax.axis_index("seq")
    core, chip = me % 2, me // 2
    z, y = chip // 2, chip % 2
    half = lax.axis_size("seq") // 4
    return me, core, jnp.where(y == 0, z, 2 * half - 1 - z), 2 * half


def ring_seq(r, core, n):
    low = r < n // 2
    return (jnp.where(low, r, n - 1 - r) * 2 + jnp.where(low, 0, 1)) * 2 + core


def greet(devices, across=False):
    barrier = pltpu.get_barrier_semaphore()
    for device in devices:
        pl.semaphore_signal(barrier, inc=1, device_id={"seq": device}, device_id_type=MESH)
    if across:
        other = 1 - lax.axis_index("fsdp")
        pl.semaphore_signal(barrier, inc=1, device_id={"fsdp": other}, device_id_type=MESH)
    pl.semaphore_wait(barrier, len(devices) + across)


def given(x):
    return (x, True)


def swap_arrays(swaps):
    return [x[0] if isinstance(x, tuple) else x for x in swaps]


def swap_shapes(swaps):
    shapes = [(x[0].shape[0] // 2, x[0].shape[1]) if isinstance(x, tuple) else x.shape for x in swaps]
    return [jax.ShapeDtypeStruct(shape, x.dtype) for shape, x in zip(shapes, swap_arrays(swaps))]


def swap_copies(gives, takes, sems):
    other = 1 - lax.axis_index("fsdp")

    def source(give, take):
        height = take.shape[0]
        return give if give.shape[0] == height else give.at[pl.ds(pl.multiple_of(other * height, height), height), :]

    return [
        pltpu.make_async_remote_copy(
            source(give, take), take, sems.at[i, 0], sems.at[i, 1], device_id={"fsdp": other}, device_id_type=MESH
        )
        for i, (give, take) in enumerate(zip(gives, takes))
    ]


def remote(src, dst, send, recv, device):
    return pltpu.make_async_remote_copy(src, dst, send, recv, device_id={"seq": device}, device_id_type=MESH)


def cast_pieces(rows):
    return next(pieces for pieces in (8, 4, 2, 1) if rows % (16 * pieces) == 0 or pieces == 1)


def cast_scratch(casts):
    shapes = []
    for x in casts:
        height = x.shape[0] // cast_pieces(x.shape[0])
        shapes += [
            pltpu.VMEM((2, height, x.shape[1]), F32),
            pltpu.VMEM((2, height, x.shape[1]), BF),
            pltpu.SemaphoreType.DMA((2,)),
            pltpu.SemaphoreType.DMA((2,)),
        ]
    return shapes


def cast_steps(sources, targets, scratch):
    for i, (source, target) in enumerate(zip(sources, targets)):
        wide, narrow, in_sem, out_sem = scratch[4 * i : 4 * i + 4]
        pieces = cast_pieces(source.shape[0])
        height = source.shape[0] // pieces

        def load(c):
            return pltpu.make_async_copy(source.at[pl.ds(c * height, height), :], wide.at[c % 2], in_sem.at[c % 2])

        def save(c):
            return pltpu.make_async_copy(narrow.at[c % 2], target.at[pl.ds(c * height, height), :], out_sem.at[c % 2])

        load(0).start()
        for c in range(pieces):
            if c + 1 < pieces:
                load(c + 1).start()
            load(c).wait()
            if c >= 2:
                save(c - 2).wait()
            narrow[c % 2] = wide[c % 2].astype(BF)
            save(c).start()
            yield
        for c in range(max(0, pieces - 2), pieces):
            save(c).wait()


def neighbours(n):
    _, core, r, _ = ring_place()
    return ring_seq((r + 1) % n, core, n), ring_seq((r + n - 1) % n, core, n), ring_seq(r, 1 - core, n)


def gather_steps(n, cuts, actives, x_refs, o_refs, own_sem, local_sem, sems):
    count = len(cuts)
    me, core, r, _ = ring_place()
    *targets, sibling = neighbours(n)

    def block(t, d, c):
        return ring_seq((r + (-t if d == 0 else t) + n) % n, c, n)

    def guarded(i, source, action):
        if actives[i] is None:
            action()
        else:
            pl.when(actives[i](source))(action)

    def parts_of(i):
        height = x_refs[i].shape[0] // (2 * cuts[i])
        for k in range(cuts[i]):
            for d in range(2):
                yield k, d, pl.ds((d * cuts[i] + k) * height, height)

    def onward(i, t, d, k, rows):
        at = o_refs[i].at[block(t, d, core), rows]
        source = x_refs[i].at[rows] if t == 0 else at
        return remote(source, at, sems[4 * i].at[t, d, k], sems[4 * i + 1].at[t, d, k], targets[d])

    def across(i, t, d, k, rows, c):
        at = o_refs[i].at[block(t, d, c), rows]
        return remote(at, at, sems[4 * i + 2].at[t - 1, d, k], sems[4 * i + 3].at[t - 1, d, k], sibling)

    def local(i):
        return pltpu.make_async_copy(x_refs[i], o_refs[i].at[me], local_sem.at[i])

    def own(i):
        return remote(x_refs[i], o_refs[i].at[me], own_sem.at[i, 0], own_sem.at[i, 1], sibling)

    for i in range(count):
        local(i).start()
        for k, d, rows in parts_of(i):
            guarded(i, me, lambda: onward(i, 0, d, k, rows).start())
        guarded(i, me, lambda: own(i).start())
    yield
    for t in range(n - 1):
        for i in range(count):
            for k, d, rows in parts_of(i):

                def step():
                    onward(i, t, d, k, rows).wait_recv()
                    if t < n - 2:
                        onward(i, t + 1, d, k, rows).start()
                    across(i, t + 1, d, k, rows, core).start()

                guarded(i, block(t + 1, d, core), step)
        yield
    for i in range(count):
        local(i).wait()
        guarded(i, me, lambda: own(i).wait_send())
        guarded(i, sibling, lambda: own(i).wait_recv())
        for t in range(n - 1):
            for k, d, rows in parts_of(i):
                guarded(i, block(t, d, core), lambda: onward(i, t, d, k, rows).wait_send())
                guarded(i, block(t + 1, d, core), lambda: across(i, t + 1, d, k, rows, core).wait_send())
                guarded(i, block(t + 1, d, 1 - core), lambda: across(i, t + 1, d, k, rows, 1 - core).wait_recv())


def gather_cut(height):
    return 2 if height % 64 == 0 else 1


def gather_sems(n, cuts):
    return [pltpu.SemaphoreType.DMA((n - 1, 2, cut)) for cut in cuts for _ in range(4)]


def gather_kernel(n, cuts, actives, swaps, shared, casts, *refs):
    count = len(cuts)
    total = count + swaps
    x_refs, give_refs, wide_refs = refs[:count], refs[count:total], refs[total : total + casts]
    refs = refs[total + casts :]
    o_refs, take_refs, narrow_refs = refs[:count], refs[count:total], refs[total : total + casts]
    own_sem, local_sem, swap_sems, hand_sem = refs[total + casts : total + casts + 4]
    sems = refs[total + casts + 4 :]
    casting = cast_steps(wide_refs, narrow_refs, sems[4 * count :])
    _, core, _, _ = ring_place()
    greet(neighbours(n), swaps > 0)
    sibling = neighbours(n)[2]

    def half_of(ref, c):
        height = ref.shape[0] // 2
        return ref.at[pl.ds(pl.multiple_of(c * height, height), height), :]

    gives, takes = list(give_refs), list(take_refs)
    if shared is not None:
        gives[shared], takes[shared] = half_of(gives[shared], core), half_of(takes[shared], core)
    swapped = swap_copies(gives, takes, swap_sems)
    for copy in swapped:
        copy.start()

    def handed(c):
        half = half_of(take_refs[shared], c)
        return remote(half, half, hand_sem.at[0], hand_sem.at[1], sibling)

    steps = gather_steps(n, cuts, actives, x_refs, o_refs, own_sem, local_sem, sems)
    next(steps)
    for _ in range(n - 1):
        next(steps)
        for _ in range(4):
            next(casting, None)
    for _ in casting:
        pass
    for _ in steps:
        pass
    if shared is not None:
        swapped[shared].wait_recv()
        handed(core).start()
    for i, copy in enumerate(swapped):
        copy.wait_send()
        if i != shared:
            copy.wait_recv()
    if shared is not None:
        handed(core).wait_send()
        handed(1 - core).wait_recv()


def ring_gather_many(operands, collective_id, actives=None, swaps=(), shared=None, casts=()):
    devices = lax.axis_size("seq")
    n = devices // 2
    cuts = [gather_cut(x.shape[0]) for x in operands]
    anywhere = pl.BlockSpec(memory_space=pl.ANY)
    sems = gather_sems(n, cuts)
    return pl.pallas_call(
        functools.partial(gather_kernel, n, cuts, actives or [None] * len(operands), len(swaps), shared, len(casts)),
        out_shape=[jax.ShapeDtypeStruct((devices, *x.shape), x.dtype) for x in operands]
        + swap_shapes(swaps)
        + [jax.ShapeDtypeStruct(x.shape, BF) for x in casts],
        in_specs=[anywhere] * (len(operands) + len(swaps) + len(casts)),
        out_specs=[anywhere] * (len(operands) + len(swaps) + len(casts)),
        scratch_shapes=[
            pltpu.SemaphoreType.DMA((len(operands), 2)),
            pltpu.SemaphoreType.DMA((len(operands),)),
            pltpu.SemaphoreType.DMA((max(1, len(swaps)), 2)),
            pltpu.SemaphoreType.DMA((2,)),
        ]
        + sems
        + cast_scratch(casts),
        compiler_params=pltpu.CompilerParams(
            collective_id=collective_id, has_side_effects=True, **({"vmem_limit_bytes": VMEM_LIMIT} if casts else {})
        ),
        cost_estimate=COST,
        name="ring_gather",
    )(*operands, *swap_arrays(swaps), *casts)


def ring_gather(x, collective_id, swaps=()):
    out, *taken = ring_gather_many([x], collective_id, None, swaps)
    return out.reshape(-1, x.shape[1]), taken


def scatter_kernel(n, cut, swaps, beside, *refs):
    a_ref, w_ref = refs[:2]
    gives, refs = refs[2 : 2 + swaps], refs[2 + swaps :]
    if beside:
        act_hbm, cn_hbm, *refs = refs
    o_ref, takes, refs = refs[0], refs[1 : 1 + swaps], refs[1 + swaps :]
    if beside:
        nope_ref, rope_ref, expand_ref, *refs = refs
    stage, sibbuf, rbuf, sbuf, send, recv, fsend, frecv, swap_sems, *refs = refs
    if beside:
        act, cn, sems = refs
        loads = [pltpu.make_async_copy(act_hbm, act, sems.at[0]), pltpu.make_async_copy(cn_hbm, cn, sems.at[1])]
        for load in loads:
            load.start()
    me, core, r, _ = ring_place()
    targets = (ring_seq((r + 1) % n, core, n), ring_seq((r + n - 1) % n, core, n))
    sibling = ring_seq(r, 1 - core, n)
    greet((*targets, sibling), swaps > 0)
    swapped = swap_copies(gives, takes, swap_sems)
    for copy in swapped:
        copy.start()
    height, columns = o_ref.shape
    spans = (pl.ds(0, cut), pl.ds(cut, columns - cut))

    def chip(t, d):
        return (r + (-t - 1 if d == 0 else t + 1) + n) % n

    def part(t, d, c):
        block = ring_seq(chip(t, d), c, n)
        rows = a_ref[pl.ds(block * height, height), :]
        return mm_nt(rows, w_ref[spans[d], :])

    def across(t, d):
        return remote(stage.at[t, :, spans[d]], sibbuf.at[t, :, spans[d]], fsend.at[t, d], frecv.at[t, d], sibling)

    half = height // 2

    def onward(t, d, k):
        at = (t, pl.ds(k * half, half), spans[d])
        return remote(sbuf.at[at], rbuf.at[at], send.at[t, d, k], recv.at[t, d, k], targets[d])

    def give(t, d):
        stage[t, :, spans[d]] = part(t, d, 1 - core).astype(BF)
        across(t, d).start()

    for d in range(2):
        give(0, d)
    for t in range(n):
        values = []
        for d in range(2):
            if t < n - 1:
                give(t + 1, d)
            values.append(part(t, d, core))
        for k in range(2):
            for d in range(2):
                if k == 0:
                    across(t, d).wait_recv()
                rows = slice(k * half, (k + 1) * half)
                value = values[d][rows] + sibbuf[t, rows, spans[d]].astype(F32)
                if t > 0:
                    onward(t - 1, d, k).wait_recv()
                    value = value + rbuf[t - 1, rows, spans[d]].astype(F32)
                if t < n - 1:
                    sbuf[t, rows, spans[d]] = value.astype(BF)
                    onward(t, d, k).start()
                else:
                    o_ref[rows, spans[d]] = value
        if beside and t == 0:
            for load in loads:
                load.wait()
        if beside:
            slab = act.shape[1] // n
            rows = slice(t * slab, (t + 1) * slab)
            grad = mm_tn(act[:, rows], a_ref[...])
            nope_ref[rows, :] = grad[:, :NOPE].astype(BF)
            rope_ref[rows, :] = grad[:, KV_END:QK_END].astype(BF)
        if beside and t == 1:
            expand_ref[...] = mm_tn(cn[...], a_ref[:, NOPE:KV_END]).astype(BF)
    for t in range(n):
        for d in range(2):
            across(t, d).wait_send()
            if t < n - 1:
                for k in range(2):
                    onward(t, d, k).wait_send()
    for copy in swapped:
        copy.wait()


def ring_scatter(a, w, collective_id, swaps=(), beside=()):
    devices = lax.axis_size("seq")
    n = devices // 2
    rows = a.shape[0] // devices
    columns = w.shape[0]
    cut = columns // 256 * 128
    vmem = pl.BlockSpec(memory_space=pltpu.VMEM)
    anywhere = [pl.BlockSpec(memory_space=pl.ANY)] * len(swaps)
    grads, held = [], []
    if beside:
        width, rank = (x.shape[1] for x in beside)
        grads = [jax.ShapeDtypeStruct(shape, BF) for shape in ((width, NOPE), (width, ROPE), (rank, NOPE + V_DIM))]
        held = [pltpu.VMEM(x.shape, BF) for x in beside] + [pltpu.SemaphoreType.DMA((2,))]
    out, *taken = pl.pallas_call(
        functools.partial(scatter_kernel, n, cut, len(swaps), len(beside) > 0),
        out_shape=[jax.ShapeDtypeStruct((rows, columns), F32)] + swap_shapes(swaps) + grads,
        in_specs=[vmem, vmem] + anywhere + [pl.BlockSpec(memory_space=pl.ANY)] * len(beside),
        out_specs=[vmem] + anywhere + [vmem] * len(grads),
        scratch_shapes=[
            pltpu.VMEM((n, rows, columns), BF),
            pltpu.VMEM((n, rows, columns), BF),
            pltpu.VMEM((n - 1, rows, columns), BF),
            pltpu.VMEM((n - 1, rows, columns), BF),
        ]
        + [pltpu.SemaphoreType.DMA((n - 1, 2, 2))] * 2
        + [pltpu.SemaphoreType.DMA((n, 2))] * 2
        + [pltpu.SemaphoreType.DMA((max(1, len(swaps)), 2))]
        + held,
        compiler_params=pltpu.CompilerParams(
            collective_id=collective_id, has_side_effects=True, vmem_limit_bytes=VMEM_LIMIT
        ),
        cost_estimate=COST,
        name="ring_scatter",
    )(a, w, *swap_arrays(swaps), *beside)
    return (out, *taken[len(swaps) :], taken[: len(swaps)])


def fsdp_gather(x, other=None):
    count = lax.axis_size("fsdp")
    if count != 2:
        return lax.all_gather(x, "fsdp", axis=0, tiled=True)
    first = lax.axis_index("fsdp") == 0
    return jnp.concatenate([jnp.where(first, x, other), jnp.where(first, other, x)], axis=0)


def fsdp_pick(x, owner, other):
    count = lax.axis_size("fsdp")
    if count != 2:
        return lax.dynamic_index_in_dim(lax.all_gather(x, "fsdp", axis=0), owner, 0, keepdims=False)
    return jnp.where(lax.axis_index("fsdp") == owner, x, other)


def fsdp_scatter(x, taken=None):
    if taken is None:
        return lax.psum_scatter(x.astype(BF), "fsdp", scatter_dimension=0, tiled=True).astype(F32)
    half = x.shape[0] // 2
    kept = lax.dynamic_slice_in_dim(x, lax.axis_index("fsdp") * half, half, 0)
    return kept.astype(F32) + taken.astype(F32)


def fsdp_sum(x, taken=None):
    return lax.psum(x, "fsdp") if taken is None else x + taken


def turn(values, cosine, sine):
    half = values.shape[-1] // 2
    turned = jnp.concatenate([-values[:, half:], values[:, :half]], axis=-1)
    return values * cosine + turned * sine


def turn_back(gradient, cosine, sine):
    half = gradient.shape[-1] // 2
    scaled = gradient * sine
    return gradient * cosine + jnp.concatenate([scaled[:, half:], -scaled[:, :half]], axis=-1)


def spans_of(length):
    step = length // 8
    for i in range(8):
        start = i * step
        yield start, step, max(0, start - (3 * step if i % 2 == 0 else 2 * step))


def allowed_of(seg_col, seg_row, start, step, low):
    width = start + step - low
    query = start + lax.broadcasted_iota(jnp.int32, (step, width), 0)
    key = low + lax.broadcasted_iota(jnp.int32, (step, width), 1)
    return (key <= query) & (seg_col[start : start + step, :] == seg_row[:, low : start + step])


def attend_block(start, step, low, qh_ref, kh_ref, v_ref, segc_ref, segr_ref, heads_ref, lse_ref):
    end = start + step
    scores = mm_nt(qh_ref[start:end, :], kh_ref[low:end, :]) * SCALE
    scores = jnp.where(allowed_of(segc_ref, segr_ref, start, step, low), scores, NEG)
    peak = jnp.max(scores, axis=-1, keepdims=True)
    raised = jnp.exp(scores - peak)
    total = jnp.sum(raised, axis=-1, keepdims=True)
    prob = (raised * (1.0 / total)).astype(BF)
    heads_ref[start:end, :] = mm(prob, v_ref[low:end, :]).astype(BF)
    lse_ref[start:end, :] = peak + jnp.log(total)


def weights_back(wb_ref, wq, we):
    width = wq.shape[0]
    rank = we.shape[0]
    wb_ref[:, :] = jnp.zeros(wb_ref.shape, BF)
    wb_ref[:width, :NOPE] = wq[:, :NOPE]
    wb_ref[:width, KV_END:QK_END] = wq[:, NOPE:]
    wb_ref[width : width + rank, NOPE:KV_END] = we[...]
    shape = (ROPE, 2 * ROPE)
    eye = lax.broadcasted_iota(jnp.int32, shape, 0) + ROPE == lax.broadcasted_iota(jnp.int32, shape, 1)
    wb_ref[width + rank : width + rank + ROPE, KV_END:] = eye.astype(F32).astype(BF)


def front_kernel(count, swaps, chunks, *refs):
    wq_parts, wl_parts, we_parts = refs[:count], refs[count : 2 * count], refs[2 * count : 3 * count]
    x_ref, gain_ref, lgain_ref, cos_ref, sin_ref, segc_ref, segr_ref = refs[3 * count : 3 * count + 7]
    refs = refs[3 * count + 7 :]
    gives, refs = refs[:swaps], refs[swaps:]
    act_ref, cn_ref, qh_ref, kh_ref, v_ref, heads_ref, lse_ref, wb_ref = refs[:8]
    takes, refs = refs[8 : 8 + swaps], refs[8 + swaps :]
    wq, wl, we, sems, swap_sems = refs
    i = pl.program_id(0)
    length = qh_ref.shape[0]
    step = length // chunks
    swapped = swap_copies(gives, takes, swap_sems) if swaps else []
    copies = [fill(p, w, sems.at[j]) for j, (p, w) in enumerate(((wq_parts, wq), (wl_parts, wl), (we_parts, we)))]
    start_first(copies)

    @pl.when(i == 0)
    def _():
        if swaps:
            greet((), True)
            for copy in swapped:
                copy.start()

    wait_first(copies)

    @pl.when(i < chunks)
    def _():
        rows = pl.ds(pl.multiple_of(i * step, step), step)
        x = x_ref[...].astype(F32)
        act_ref[...] = (x * norm_scale(x) * gain_ref[...]).astype(BF)
        cosine, sine = cos_ref[...], sin_ref[...]
        query = mm(act_ref[...], wq[...])
        qh_ref[rows, :NOPE] = query[:, :NOPE].astype(BF)
        qh_ref[rows, NOPE:] = turn(query[:, NOPE:].astype(BF).astype(F32), cosine, sine).astype(BF)
        latent = mm(act_ref[...], wl[...])
        comp = latent[:, :KV_RANK]
        cn_ref[...] = (comp * norm_scale(comp) * lgain_ref[...]).astype(BF)
        kh_ref[rows, NOPE:] = turn(latent[:, KV_RANK:].astype(BF).astype(F32), cosine, sine).astype(BF)
        kv = mm(cn_ref[...], we[...])
        kh_ref[rows, :NOPE] = kv[:, :NOPE].astype(BF)
        v_ref[rows, :] = kv[:, NOPE:].astype(BF)

    @pl.when(i == chunks)
    def _():
        for start, size, low in spans_of(length):
            attend_block(start, size, low, qh_ref, kh_ref, v_ref, segc_ref, segr_ref, heads_ref, lse_ref)
        weights_back(wb_ref, wq, we)
        for copy in swapped:
            copy.wait()


def front(pieces, x, gain, lgain, cosine, sine, seg_col, seg_row, swaps, collective_id):
    length, width = x.shape
    chunks = 4
    step = length // chunks
    count = len(pieces[0])
    vmem = pl.BlockSpec(memory_space=pltpu.VMEM)
    anywhere = pl.BlockSpec(memory_space=pl.ANY)

    def tile(columns):
        return pl.BlockSpec((step, columns), lambda i: (jnp.minimum(i, chunks - 1), 0))

    def held(rows, columns):
        return pl.BlockSpec((rows, columns), lambda i: (0, 0))

    full = lambda group: (group[0].shape[0] * count, group[0].shape[1])
    backs = (width + KV_RANK + 2 * ROPE, QK_END + ROPE)
    outs = [
        (tile(width), (length, width), BF),
        (tile(KV_RANK), (length, KV_RANK), BF),
        (held(length, QD), (length, QD), BF),
        (held(length, QD), (length, QD), BF),
        (held(length, V_DIM), (length, V_DIM), BF),
        (held(length, V_DIM), (length, V_DIM), BF),
        (held(length, 1), (length, 1), F32),
        (held(*backs), backs, BF),
    ]
    return pl.pallas_call(
        functools.partial(front_kernel, count, len(swaps), chunks),
        grid=(chunks + 1,),
        out_shape=[jax.ShapeDtypeStruct(shape, dtype) for _, shape, dtype in outs]
        + [jax.ShapeDtypeStruct(w.shape, w.dtype) for w in swaps],
        in_specs=[anywhere] * (3 * count) + [tile(width), vmem, vmem, tile(ROPE), tile(ROPE), vmem, vmem]
        + [anywhere] * len(swaps),
        out_specs=[spec for spec, _, _ in outs] + [anywhere] * len(swaps),
        scratch_shapes=[pltpu.VMEM(full(group), BF) for group in pieces]
        + [pltpu.SemaphoreType.DMA((3, count)), pltpu.SemaphoreType.DMA((max(1, len(swaps)), 2))],
        compiler_params=pltpu.CompilerParams(
            vmem_limit_bytes=VMEM_LIMIT, collective_id=collective_id, has_side_effects=len(swaps) > 0
        ),
        cost_estimate=COST,
        name="front",
    )(*sum(pieces, ()), x, gain, lgain, cosine, sine, seg_col, seg_row, *swaps)


def attend_back_kernel(*refs):
    qh_ref, kh_ref, v_ref, lse_ref, heads_ref, da_ref, wo_ref, cos_ref, sin_ref, segc_ref, segr_ref = refs[:11]
    back_ref, gout_ref, dk_acc, dv_acc = refs[11:]
    dk_acc[...] = jnp.zeros_like(dk_acc)
    dv_acc[...] = jnp.zeros_like(dv_acc)
    for start, step, low in spans_of(qh_ref.shape[0]):
        end = start + step
        query = qh_ref[start:end, :]
        grad = mm_nt(da_ref[start:end, :], wo_ref[...]).astype(BF)
        keys = kh_ref[low:end, :]
        scores = mm_nt(query, keys) * SCALE
        allowed = allowed_of(segc_ref, segr_ref, start, step, low)
        prob = jnp.where(allowed, jnp.exp(scores - lse_ref[start:end, :]), 0.0)
        dv_acc[low:end, :] += mm_tn(prob.astype(BF), grad)
        dprob = mm_nt(grad, v_ref[low:end, :])
        delta = jnp.sum(prob * dprob, axis=-1, keepdims=True)
        dscore = (prob * (dprob - delta) * SCALE).astype(BF)
        dquery = mm(dscore, keys)
        back_ref[start:end, :NOPE] = dquery[:, :NOPE].astype(BF)
        turned = turn_back(dquery[:, NOPE:], cos_ref[start:end, :], sin_ref[start:end, :])
        back_ref[start:end, KV_END:QK_END] = turned.astype(BF)
        dk_acc[low:end, :] += mm_tn(dscore, query)
    back_ref[:, NOPE : 2 * NOPE] = dk_acc[:, :NOPE].astype(BF)
    back_ref[:, 2 * NOPE : KV_END] = dv_acc[...].astype(BF)
    back_ref[:, QK_END:] = turn_back(dk_acc[:, NOPE:], cos_ref[...], sin_ref[...]).astype(BF)
    gout_ref[...] = mm_tn(heads_ref[...], da_ref[...]).astype(BF)


def attend_back(*operands):
    length, width = operands[5].shape
    vmem = pl.BlockSpec(memory_space=pltpu.VMEM)
    return pl.pallas_call(
        attend_back_kernel,
        out_shape=[jax.ShapeDtypeStruct((length, QK_END + ROPE), BF), jax.ShapeDtypeStruct((V_DIM, width), BF)],
        in_specs=[vmem] * len(operands),
        out_specs=[vmem, vmem],
        scratch_shapes=[pltpu.VMEM((length, QD), F32), pltpu.VMEM((length, V_DIM), F32)],
        compiler_params=pltpu.CompilerParams(vmem_limit_bytes=VMEM_LIMIT),
        cost_estimate=COST,
        name="attend_back",
    )(*operands)


def fsdp_pieces(x, other):
    if lax.axis_size("fsdp") != 2:
        return (lax.all_gather(x, "fsdp", axis=0, tiled=True),)
    return (x, other)


def fill(pieces, dst, sems):
    if len(pieces) == 1:
        return [pltpu.make_async_copy(pieces[0], dst, sems.at[0])]
    part = lax.axis_index("fsdp")
    height = pieces[0].shape[0]
    starts = (part * height, (1 - part) * height)
    return [
        pltpu.make_async_copy(piece, dst.at[pl.ds(pl.multiple_of(start, height), height), :], sems.at[i])
        for i, (piece, start) in enumerate(zip(pieces, starts))
    ]


def picks(slot_ref, share_ref, b, most):
    slots = slot_ref[b]
    pick = slots == lax.broadcasted_iota(jnp.int32, (most, slots.shape[1]), 0)
    return pick.astype(BF), jnp.sum(jnp.where(pick, share_ref[b], 0.0), axis=-1, keepdims=True)


def hidden_spans(hidden):
    cut = -(-hidden // 256) * 128
    return ((0, cut), (cut, hidden))


def start_first(groups):
    @pl.when(pl.program_id(0) == 0)
    def _():
        for group in groups:
            for copy in group:
                copy.start()


def wait_first(groups):
    @pl.when(pl.program_id(0) == 0)
    def _():
        for group in groups:
            for copy in group:
                copy.wait()


def expert_in_kernel(count, most, swaps, *refs):
    wg_parts, wu_parts = refs[:count], refs[count : 2 * count]
    act_ref, slot_ref, share_ref, wsgu_ref, wsd_ref, g_ref = refs[2 * count : 2 * count + 6]
    gives, refs = refs[2 * count + 6 : 2 * count + 6 + swaps], refs[2 * count + 6 + swaps :]
    xe_ref, ge_ref, ue_ref, he_ref, sh_ref, dye_ref, dsgu_ref, ys_ref, ds_ref = refs[:9]
    takes, (wg, wu, sems, swap_sems) = refs[9 : 9 + swaps], refs[9 + swaps :]
    swapped = swap_copies(gives, takes, swap_sems) if swaps else []
    if swaps:

        @pl.when(pl.program_id(0) == 0)
        def _():
            greet((), True)
            for copy in swapped:
                copy.start()

    copies = [fill(wg_parts, wg, sems.at[0]), fill(wu_parts, wu, sems.at[1])]
    start_first(copies)
    blocks, rows = slot_ref.shape[0], slot_ref.shape[2]
    for b in range(blocks):
        pick, share = picks(slot_ref, share_ref, b, most)
        block, packed = slice(b * rows, (b + 1) * rows), slice(b * most, (b + 1) * most)
        xe_ref[packed, :] = mm(pick, act_ref[block, :]).astype(BF)
        dye_ref[packed, :] = (share * mm(pick, g_ref[block, :])).astype(BF)
    sgu = mm(act_ref[...], wsgu_ref[...])
    units = sh_ref.shape[1]
    sg, su = sgu[:, :units], sgu[:, units:]
    sig = jax.nn.sigmoid(sg)
    sh_ref[...] = (sg * sig * su).astype(BF)
    dsh = mm_nt(g_ref[...], wsd_ref[...])
    dsgu_ref[:, :units] = (dsh * su * sig * (1.0 + sg * (1.0 - sig))).astype(BF)
    dsgu_ref[:, units:] = (dsh * sg * sig).astype(BF)
    ys_ref[...] = mm(sh_ref[...], wsd_ref[...]).astype(BF)
    ds_ref[...] = mm_nt(dsgu_ref[...], wsgu_ref[...]).astype(BF)
    wait_first(copies)
    for low, high in hidden_spans(wg.shape[1]):
        ge = mm(xe_ref[...], wg[:, low:high])
        ue = mm(xe_ref[...], wu[:, low:high])
        ge_ref[:, low:high] = ge
        ue_ref[:, low:high] = ue
        he_ref[:, low:high] = (ge * jax.nn.sigmoid(ge) * ue).astype(BF)
    if swaps:

        @pl.when(pl.program_id(0) == pl.num_programs(0) - 1)
        def _():
            for copy in swapped:
                copy.wait()


def expert_out_kernel(count, most, swaps, *refs):
    wd_parts = refs[:count]
    he_ref, slot_ref, share_ref, ys_ref, y_ref, wd, sems, _ = refs[count:]
    copies = [fill(wd_parts, wd, sems.at[0])]
    start_first(copies)
    wait_first(copies)
    blocks, rows = slot_ref.shape[0], slot_ref.shape[2]
    z = mm(he_ref[...], wd[...]).astype(BF)
    for b in range(blocks):
        pick, share = picks(slot_ref, share_ref, b, most)
        ye = z[b * most : (b + 1) * most, :].astype(F32)
        ys = ys_ref[b * rows : (b + 1) * rows, :].astype(F32)
        y_ref[b * rows : (b + 1) * rows, :] = (ys + mm_tn(pick, (share * ye).astype(BF))).astype(BF)


def expert_back_kernel(n, cut, count, most, swaps, *refs):
    wg_parts, wu_parts, wd_parts = refs[:count], refs[count : 2 * count], refs[2 * count : 3 * count]
    dye_ref, slot_ref, share_ref, part_ref, ge_ref, ue_ref, ds_ref = refs[3 * count : 3 * count + 7]
    dact_ref, dge_ref, due_ref, y_ref = refs[3 * count + 7 : 3 * count + 11]
    wg, wu, wd, sems, _, *buffers = refs[3 * count + 11 :]
    copies = [fill(p, w, sems.at[i]) for i, (p, w) in enumerate(((wg_parts, wg), (wu_parts, wu), (wd_parts, wd)))]
    start_first(copies)
    middle, finish = scatter_in_grid(pl.program_id(0), n, cut, part_ref, y_ref, buffers)
    middle()
    blocks, rows = slot_ref.shape[0], slot_ref.shape[2]
    wait_first(copies)
    for low, high in hidden_spans(wg.shape[1]):
        dhe = mm_nt(dye_ref[...], wd[low:high, :])
        ge, ue = ge_ref[:, low:high], ue_ref[:, low:high]
        sig = jax.nn.sigmoid(ge)
        dge_ref[:, low:high] = (dhe * ue * sig * (1.0 + ge * (1.0 - sig))).astype(BF)
        due_ref[:, low:high] = (dhe * ge * sig).astype(BF)
    dxe = (mm_nt(dge_ref[...], wg[...]) + mm_nt(due_ref[...], wu[...])).astype(BF)
    for b in range(blocks):
        pick, _ = picks(slot_ref, share_ref, b, most)
        block = slice(b * rows, (b + 1) * rows)
        shared = ds_ref[block, :].astype(F32)
        dact_ref[block, :] = (shared + mm_tn(pick, dxe[b * most : (b + 1) * most, :])).astype(BF)
    finish()


def expert_call(kernel, name, pieces, most, steps, slot, share, whole, tiled, outs, swaps=(), collective_id=None, summed=None):
    devices, rows = slot.shape[0], slot.shape[2]
    per = devices // steps
    anywhere = pl.BlockSpec(memory_space=pl.ANY)
    vmem = pl.BlockSpec(memory_space=pltpu.VMEM)

    def tile(total, columns):
        return pl.BlockSpec((total // steps, columns), lambda i: (i, 0))

    cut = pl.BlockSpec((per, 1, rows), lambda i: (i, 0, 0))
    count = len(pieces[0])
    full = lambda group: (group[0].shape[0] * count, group[0].shape[1])
    buffers, kept = [], []
    if summed is not None:
        buffers = scatter_buffers(devices // 2, *summed)
        kept = [(pl.BlockSpec(summed, lambda i: (0, 0)), jax.ShapeDtypeStruct(summed, F32))]
    return pl.pallas_call(
        functools.partial(kernel, count, most, len(swaps)),
        grid=(steps,),
        out_shape=[jax.ShapeDtypeStruct((total, columns), dtype) for total, columns, dtype in outs]
        + [shape for _, shape in kept]
        + [jax.ShapeDtypeStruct(x.shape, x.dtype) for x in swaps],
        in_specs=[anywhere] * (len(pieces) * count) + [tile(*tiled[0].shape), cut, cut] + [vmem] * len(whole)
        + [tile(*t.shape) for t in tiled[1:]]
        + [anywhere] * len(swaps),
        out_specs=[tile(total, columns) for total, columns, _ in outs]
        + [spec for spec, _ in kept]
        + [anywhere] * len(swaps),
        scratch_shapes=[pltpu.VMEM(full(group), BF) for group in pieces]
        + [pltpu.SemaphoreType.DMA((len(pieces), count)), pltpu.SemaphoreType.DMA((max(1, len(swaps)), 2))]
        + buffers,
        compiler_params=pltpu.CompilerParams(
            vmem_limit_bytes=VMEM_LIMIT, collective_id=collective_id, has_side_effects=collective_id is not None
        ),
        cost_estimate=COST,
        name=name,
    )(*sum(pieces, ()), tiled[0], slot, share, *whole, *tiled[1:], *swaps)


def widen_query(nope, rope):
    devices, rows, _ = nope.shape
    steps = 8
    step = rows // steps

    def kernel(n_ref, r_ref, o_ref):
        def put(first):
            for d in range(devices):
                o_ref[:, d * QD : d * QD + NOPE] = n_ref[d].astype(F32)
                o_ref[:, d * QD + NOPE : (d + 1) * QD] = r_ref[d, :, first : first + ROPE].astype(F32)

        low = pl.program_id(0) < steps // 2
        pl.when(low)(lambda: put(0))
        pl.when(jnp.logical_not(low))(lambda: put(ROPE))

    return pl.pallas_call(
        kernel,
        grid=(steps,),
        out_shape=jax.ShapeDtypeStruct((rows, devices * QD), F32),
        in_specs=[
            pl.BlockSpec((devices, step, NOPE), lambda i: (0, i, 0)),
            pl.BlockSpec((devices, step, 2 * ROPE), lambda i: (0, i % (steps // 2), 0)),
        ],
        out_specs=pl.BlockSpec((step, devices * QD), lambda i: (i, 0)),
        compiler_params=pltpu.CompilerParams(vmem_limit_bytes=VMEM_LIMIT),
        cost_estimate=COST,
        name="wide_query",
    )(nope, rope)


def trim(stacks, share):
    devices, _, width = stacks[0].shape
    if share % 8:
        return jnp.concatenate(stacks, axis=1)[:, :share].reshape(-1, width).astype(F32)

    def kernel(*refs):
        *i_refs, o_ref = refs
        for d in range(i_refs[0].shape[0]):
            at = d * share
            for i_ref in i_refs:
                height = min(i_ref.shape[1], (d + 1) * share - at)
                o_ref[at : at + height, :] = i_ref[d, :height, :].astype(F32)
                at += height

    return pl.pallas_call(
        kernel,
        grid=(4,),
        out_shape=jax.ShapeDtypeStruct((devices * share, width), F32),
        in_specs=[pl.BlockSpec((devices // 4, x.shape[1], width), lambda i: (i, 0, 0)) for x in stacks],
        out_specs=pl.BlockSpec((devices // 4 * share, width), lambda i: (i, 0)),
        compiler_params=pltpu.CompilerParams(vmem_limit_bytes=VMEM_LIMIT),
        cost_estimate=COST,
        name="trim",
    )(*stacks)


def scatter_in_grid(t, n, cut, part_ref, o_ref, buffers):
    sibbuf, rbuf, sbuf, send, recv, fsend, frecv = buffers
    me, core, r, _ = ring_place()
    targets = (ring_seq((r + 1) % n, core, n), ring_seq((r + n - 1) % n, core, n))
    sibling = ring_seq(r, 1 - core, n)
    columns = o_ref.shape[1]
    spans = (pl.ds(0, cut), pl.ds(cut, columns - cut))

    def block(step, d, c):
        return ring_seq((r + (-step - 1 if d == 0 else step + 1) + n) % n, c, n)

    def across(step, d):
        source = part_ref.at[block(step, d, 1 - core), :, spans[d]]
        return remote(source, sibbuf.at[step, :, spans[d]], fsend.at[step, d], frecv.at[step, d], sibling)

    height = o_ref.shape[0] // 2

    def onward(step, d, k):
        at = (step, pl.ds(k * height, height), spans[d])
        return remote(sbuf.at[at], rbuf.at[at], send.at[step, d, k], recv.at[step, d, k], targets[d])

    @pl.when(t == 0)
    def _():
        greet((*targets, sibling))
        for step in range(2):
            for d in range(2):
                across(step, d).start()

    @pl.when(t < n - 2)
    def _():
        for d in range(2):
            across(t + 2, d).start()

    def advance(k):
        rows = pl.ds(k * height, height)
        for d in range(2):
            if k == 0:
                across(t, d).wait_recv()

            def both():
                return part_ref[block(t, d, core), rows, spans[d]].astype(F32) + sibbuf[t, rows, spans[d]].astype(F32)

            @pl.when(t == 0)
            def _():
                sbuf[0, rows, spans[d]] = both().astype(BF)
                onward(0, d, k).start()

            @pl.when((t > 0) & (t < n - 1))
            def _():
                onward(t - 1, d, k).wait_recv()
                sbuf[t, rows, spans[d]] = (both() + rbuf[t - 1, rows, spans[d]].astype(F32)).astype(BF)
                onward(t, d, k).start()

            @pl.when(t == n - 1)
            def _():
                onward(n - 2, d, k).wait_recv()
                o_ref[rows, spans[d]] = both() + rbuf[n - 2, rows, spans[d]].astype(F32)

    def finish():
        @pl.when(t == n - 1)
        def _():
            for step in range(n):
                for d in range(2):
                    across(step, d).wait_send()
                    if step < n - 1:
                        for k in range(2):
                            onward(step, d, k).wait_send()

    advance(0)
    return lambda: advance(1), finish


def scatter_buffers(n, rows, columns):
    return (
        [pltpu.VMEM((n, rows, columns), BF), pltpu.VMEM((n - 1, rows, columns), BF), pltpu.VMEM((n - 1, rows, columns), BF)]
        + [pltpu.SemaphoreType.DMA((n - 1, 2, 2))] * 2
        + [pltpu.SemaphoreType.DMA((n, 2))] * 2
    )


def weight_grads_kernel(n, cut, parts, *refs):
    xe_ref, dge_ref, due_ref, he_ref, dye_ref, act_ref, dsgu_ref, sh_ref, g_ref, part_ref = refs[:10]
    o_ref, gate_ref, up_ref, down_ref, sgu_ref, sdown_ref = refs[10:16]
    middle, finish = scatter_in_grid(pl.program_id(0), n, cut, part_ref, o_ref, refs[16:])
    gate_ref[...] = mm_tn(xe_ref[...], dge_ref[...]).astype(BF)
    sgu_ref[...] = mm_tn(act_ref[...], dsgu_ref[...]).astype(BF)
    middle()
    up_ref[...] = mm_tn(xe_ref[...], due_ref[...]).astype(BF)
    down_ref[...] = mm_tn(he_ref[...], dye_ref[...]).astype(BF)
    sdown = mm_tn(sh_ref[...], g_ref[...]).astype(BF)
    share = sdown.shape[0] // parts
    room = sdown_ref.shape[0] // parts
    for p in range(parts):
        sdown_ref[p * room : p * room + share, :] = sdown[p * share : (p + 1) * share, :]
        if room > share:
            sdown_ref[p * room + share : (p + 1) * room, :] = jnp.zeros((room - share, sdown.shape[1]), BF)

    finish()


def weight_grads(xe, dge, due, he, dye, act, dsgu, sh, g, part, parts, room, collective_id):
    devices = lax.axis_size("seq")
    n = devices // 2
    length, columns = part.shape
    rows = length // devices
    cut = columns // 256 * 128

    def tile(x):
        return pl.BlockSpec((x.shape[0], x.shape[1] // n), lambda i: (0, i))

    def held(x):
        return pl.BlockSpec(memory_space=pltpu.VMEM)

    ff, units = dge.shape[1], dsgu.shape[1]
    slab = columns // n
    down = lambda width: pl.BlockSpec((slab, width), lambda i: (i, 0))
    along = lambda height: pl.BlockSpec((height, slab), lambda i: (0, i))
    return pl.pallas_call(
        functools.partial(weight_grads_kernel, n, cut, parts),
        grid=(n,),
        out_shape=[jax.ShapeDtypeStruct((rows, columns), F32)]
        + [
            jax.ShapeDtypeStruct(shape, BF)
            for shape in ((columns, ff), (columns, ff), (ff, columns), (columns, units), (parts * room, columns))
        ],
        in_specs=[tile(xe), held(dge), held(due), held(he), tile(dye), tile(act), held(dsgu), held(sh), tile(g)]
        + [held(part)],
        out_specs=[pl.BlockSpec((rows, columns), lambda i: (0, 0)), down(ff), down(ff), along(ff)]
        + [down(units), along(parts * room)],
        scratch_shapes=scatter_buffers(n, rows, columns),
        compiler_params=pltpu.CompilerParams(
            collective_id=collective_id, has_side_effects=True, vmem_limit_bytes=VMEM_LIMIT
        ),
        cost_estimate=COST,
        name="weight_grads",
    )(xe, dge, due, he, dye, act, dsgu, sh, g, part.reshape(devices, rows, columns))


def widen(stacked, count, parts, name):
    devices, rows, columns = stacked.shape
    share = columns // parts // count
    width = devices * columns // count
    steps = 8

    def kernel(i_ref, *o_refs):
        for j, o_ref in enumerate(o_refs):
            for p in range(parts):
                for d in range(devices):
                    at, source = (p * devices + d) * share, (j * parts + p) * share
                    o_ref[:, at : at + share] = i_ref[d, :, source : source + share].astype(F32)

    return pl.pallas_call(
        kernel,
        grid=(steps,),
        out_shape=[jax.ShapeDtypeStruct((rows, width), F32)] * count,
        in_specs=[pl.BlockSpec((devices, rows // steps, columns), lambda i: (0, i, 0))],
        out_specs=[pl.BlockSpec((rows // steps, width), lambda i: (i, 0))] * count,
        compiler_params=pltpu.CompilerParams(vmem_limit_bytes=VMEM_LIMIT),
        cost_estimate=COST,
        name=name,
    )(stacked)


def columns_of(weight, at, width):
    return lax.dynamic_slice_in_dim(weight, at * width, width, 1).astype(BF)


def rows_of(weight, at, height):
    return lax.dynamic_slice_in_dim(weight, at * height, height, 0).astype(BF)


def per_device(
    tokens,
    segment_ids,
    routes,
    gate_weights,
    out_grad,
    attn_gain,
    q_weight,
    latent_weight,
    latent_gain,
    kv_weight,
    out_weight,
    ffn_gain,
    shared_gate,
    shared_up,
    shared_down,
    expert_gate,
    expert_up,
    expert_down,
):
    _, rows, width = tokens.shape
    devices = lax.axis_size("seq")
    at = lax.axis_index("seq")
    parts = lax.axis_size("fsdp")
    part = lax.axis_index("fsdp")
    length = rows * devices
    own_x = tokens[0]
    own_g = out_grad[0]

    per, per_latent = attn_gain.shape[0], latent_gain.shape[0]
    gains = jnp.concatenate([attn_gain, ffn_gain, latent_gain]).astype(BF)
    gains_size = gains.shape[0]
    gains_rows = -(-gains_size // 2048) * 16
    gains = jnp.pad(gains, (0, gains_rows * 128 - gains_size)).reshape(gains_rows, 128)
    out_rows = out_weight.shape[0]
    early_latent = 2
    share = shared_down.shape[0] // devices
    share_pad = -(-share // 32) * 32
    sdown = jnp.pad(rows_of(shared_down, at, share), ((0, share_pad - share), (0, 0)))
    early = (
        gains,
        columns_of(q_weight, at, QD),
        latent_weight.astype(BF),
        columns_of(kv_weight, at, NOPE + V_DIM),
        lax.dynamic_slice_in_dim(out_weight, at * V_DIM % out_rows, V_DIM, 0).astype(BF),
    )
    pair = parts == 2

    def crossing(*arrays):
        return arrays if pair else ()

    def crossed(taken, count):
        return taken if pair else [None] * count

    experts = jnp.arange(devices, dtype=jnp.int32)
    spread = jnp.sum(
        jnp.where(routes[0].T[None, :, :] == experts[:, None, None], gate_weights[0].T[None, :, :], 0.0), axis=1
    )
    x_all, spread_all, *others = ring_gather_many(
        [own_x, spread],
        8,
        None,
        crossing(*early),
        early_latent if pair else None,
        (expert_gate[0], expert_up[0], expert_down[0]),
    )
    others, (egate, eup, edown) = others[:-3], others[-3:]
    late_g, x_all = lax.optimization_barrier((own_g, x_all.reshape(length, width)))
    g_all = lax.all_gather(late_g, "seq", axis=0, tiled=True)
    share_of = lax.dynamic_index_in_dim(spread_all, at, 1, keepdims=False)
    others = crossed(others, len(early))
    gains = fsdp_gather(gains, others[0]).reshape(parts, -1)[:, :gains_size].astype(F32)
    gain_one = gains[:, :per].reshape(1, -1)
    gain_two = gains[:, per : 2 * per].reshape(1, -1)
    gain_lat = gains[:, 2 * per :].reshape(1, -1)
    w_latent = fsdp_gather(early[2], others[2])
    w_out = fsdp_pick(early[4], at * V_DIM // out_rows, others[4])

    hidden = shared_down.shape[0] * parts

    def shared_columns(weight):
        pieces = [
            lax.dynamic_slice_in_dim(weight, p * (hidden // parts) + at * share, share, 1) for p in range(parts)
        ]
        return pieces

    sgu = jnp.concatenate(shared_columns(shared_gate) + shared_columns(shared_up), axis=1).astype(BF)

    cosine, sine = rope_tables(length)
    seg_col, seg_row = segment_ids.reshape(length, 1), segment_ids
    act_one, cnorm, qh, kh, values, heads, lse, w_back, *taken = front(
        tuple(fsdp_pieces(early[i], others[i]) for i in (1, 2, 3)),
        x_all,
        gain_one,
        gain_lat,
        cosine,
        sine,
        seg_col,
        seg_row,
        crossing(sgu, sdown),
        11 if pair else None,
    )
    sgu_other, sdown_other = crossed(taken, 2)
    own_xf = own_x.astype(F32)
    attended, taken = ring_scatter(heads, w_out.T, 2, crossing(egate))
    (egate_other,) = crossed(taken, 1)
    x1 = own_xf + attended
    r3 = norm_scale(x1)
    act_two = (x1 * r3 * gain_two).astype(BF)
    act_all, taken = ring_gather(act_two, 9, crossing(eup))
    (eup_other,) = crossed(taken, 1)
    w_egate, w_eup = fsdp_pieces(egate, egate_other), fsdp_pieces(eup, eup_other)
    w_sgu = fsdp_gather(sgu, sgu_other)
    w_sdown = fsdp_gather(sdown[:share], sdown_other[:share] if pair else None)

    most = min(MOST, rows)
    named = share_of > 0.0
    rank = jnp.cumsum(named.astype(jnp.int32), axis=1) - 1
    slot = jnp.where(named, rank, -1)[:, None, :]
    share_of = share_of[:, None, :]
    packed = devices * most
    ff = expert_gate.shape[2]
    units = parts * share
    steps = 4
    xe, ge, ue, he, sh, dye, dsgu, ys, ds, *taken = expert_call(
        expert_in_kernel,
        "experts_in",
        (w_egate, w_eup),
        most,
        steps,
        slot,
        share_of,
        (w_sgu, w_sdown),
        (act_all, g_all),
        (
            (packed, width, BF),
            (packed, ff, F32),
            (packed, ff, F32),
            (packed, ff, BF),
            (length, units, BF),
            (packed, width, BF),
            (length, 2 * units, BF),
            (length, width, BF),
            (length, width, BF),
        ),
        crossing(edown),
        10 if pair else None,
    )
    (edown_other,) = crossed(taken, 1)
    w_edown = fsdp_pieces(edown, edown_other)
    (y_part,) = expert_call(
        expert_out_kernel,
        "experts_out",
        (w_edown,),
        most,
        steps,
        slot,
        share_of,
        (),
        (he, ys),
        ((length, width, BF),),
    )
    dact_part, dge, due, y_sum = expert_call(
        functools.partial(expert_back_kernel, devices // 2, width // 256 * 128),
        "experts_back",
        (w_egate, w_eup, w_edown),
        most,
        devices // 2,
        slot,
        share_of,
        (y_part.reshape(devices, rows, width),),
        (dye, ge, ue, ds),
        ((length, width, BF), (packed, ff, BF), (packed, ff, BF)),
        (),
        12,
        (rows, width),
    )
    dact_two, grad_egate, grad_eup, grad_edown, grad_sgu, grad_sdown = weight_grads(
        xe, dge, due, he, dye, act_all, dsgu, sh, g_all, dact_part, parts, share_pad, 3
    )
    own_gf = own_g.astype(F32)
    grad_gain_two = jnp.sum(dact_two * x1 * r3, axis=0)
    dx1 = own_gf + norm_back(x1, r3, dact_two * gain_two)
    dattn_all, taken = ring_gather(dx1.astype(BF), 1, (given(grad_sgu), given(grad_sdown)) if pair else ())
    sgu_taken, sdown_taken = crossed(taken, 2)
    grad_sgu = fsdp_scatter(grad_sgu, sgu_taken).astype(BF)
    grad_sdown = fsdp_scatter(grad_sdown, sdown_taken).astype(BF)
    output = (x1 + y_sum).astype(BF)

    back, grad_out = attend_back(qh, kh, values, lse, heads, dattn_all, w_out, cosine, sine, seg_col, seg_row)
    summed, grad_nope, grad_rope, grad_expand, taken = ring_scatter(
        back, w_back, 4, (given(grad_edown),) if pair else (), (act_one, cnorm)
    )
    grad_edown = fsdp_scatter(grad_edown, *taken)

    r1 = norm_scale(own_xf)
    own_act = (own_xf * r1 * gain_one).astype(BF)
    own_comp = mm(own_act, w_latent)[:, :KV_RANK]
    r2 = norm_scale(own_comp)
    dcn = summed[:, width : width + KV_RANK]
    grad_gain_lat = jnp.sum(dcn * own_comp * r2, axis=0)
    dcomp = norm_back(own_comp, r2, dcn * gain_lat)
    dlatent = jnp.concatenate([dcomp, summed[:, width + KV_RANK : width + KV_RANK + ROPE]], axis=-1).astype(BF)
    dact_one = summed[:, :width] + mm_nt(dlatent, w_latent)
    grad_gain_one = jnp.sum(dact_one * own_xf * r1, axis=0)
    input_grad = dx1 + norm_back(own_xf, r1, dact_one * gain_one)

    small = jnp.concatenate([grad_gain_one, grad_gain_two, grad_gain_lat])
    small = jnp.pad(small, (0, 64 * 128 - small.shape[0])).reshape(64, 128)

    def in_part(device):
        return device * V_DIM // out_rows == lax.axis_index("fsdp")

    sgu_all, dlatent_all, sdown_all, *taken = ring_gather_many(
        [grad_sgu, dlatent, grad_sdown],
        5,
        None,
        (given(grad_nope), given(grad_rope), given(grad_expand), grad_out, small, given(grad_egate)) if pair else (),
    )
    nope_taken, rope_taken, expand_taken, out_taken, small_taken, egate_taken = crossed(taken, 6)
    grad_nope = fsdp_scatter(grad_nope, nope_taken).astype(BF)
    grad_rope = fsdp_scatter(grad_rope, rope_taken).astype(BF)
    grad_rope = jnp.concatenate(jnp.split(grad_rope, 2, axis=0), axis=1)
    grad_expand = fsdp_scatter(grad_expand, expand_taken).astype(BF)
    grad_out = fsdp_sum(grad_out, out_taken)
    small = fsdp_sum(small, small_taken)
    grad_egate = fsdp_scatter(grad_egate, egate_taken)
    slab = width // parts // devices
    act_cols = jnp.concatenate(
        [lax.dynamic_slice_in_dim(act_one, p * (width // parts) + at * slab, slab, 1) for p in range(parts)], axis=1
    )
    grad_latent = mm_tn(act_cols, dlatent_all.reshape(length, -1)).astype(BF)
    latent_taken = None
    if pair:
        latent_taken = lax.ppermute(
            lax.dynamic_slice_in_dim(grad_latent, (1 - part) * slab, slab, 0), "fsdp", [(0, 1), (1, 0)]
        )
    grad_latent = fsdp_scatter(grad_latent, latent_taken).astype(BF)
    latent_pad = -(-slab // 32) * 32
    nope_all, rope_all, expand_all, out_all, latent_all, small_all, *taken = ring_gather_many(
        [grad_nope, grad_rope, grad_expand, grad_out, jnp.pad(grad_latent, ((0, latent_pad - slab), (0, 0))), small],
        7,
        [None, None, None, in_part, None, None],
        (given(grad_eup),) if pair else (),
    )
    (eup_taken,) = crossed(taken, 1)
    grad_eup = fsdp_scatter(grad_eup, eup_taken)
    latent_all = latent_all[:, :slab]
    out_grad_own = lax.dynamic_slice_in_dim(
        out_all.reshape(devices * V_DIM, width), part * out_rows, out_rows, 0
    ).astype(F32)
    small = jnp.sum(small_all, axis=0).reshape(-1)
    wide_gate, wide_up = widen(sgu_all, 2, parts, "wide_shared")
    gain_rows = width // parts
    own_gains = [
        lax.dynamic_slice_in_dim(small, part * gain_rows, gain_rows),
        lax.dynamic_slice_in_dim(small, width + part * gain_rows, gain_rows),
        lax.dynamic_slice_in_dim(small, 2 * width + part * (KV_RANK // parts), KV_RANK // parts),
    ]
    return (
        output[None],
        input_grad[None],
        own_gains[0],
        widen_query(nope_all, rope_all),
        latent_all.reshape(-1, grad_latent.shape[1]).astype(F32),
        own_gains[2],
        widen(expand_all, 1, 1, "wide_kv")[0],
        out_grad_own,
        own_gains[1],
        wide_gate,
        wide_up,
        trim([sdown_all], share),
        grad_egate[None],
        grad_eup[None],
        grad_edown[None],
    )


def solution(mesh):
    token_spec = P("fsdp", "seq", None)
    row_spec = P("fsdp", None)
    gain_spec = P("fsdp")
    expert_spec = P("seq", "fsdp", None)
    dense = (gain_spec, row_spec, row_spec, gain_spec, row_spec, row_spec, gain_spec, row_spec, row_spec, row_spec)
    weights = dense + (expert_spec,) * 3
    return jax.shard_map(
        per_device,
        mesh=mesh,
        in_specs=(token_spec, row_spec, token_spec, token_spec, token_spec) + weights,
        out_specs=(token_spec, token_spec) + weights,
        check_vma=False,
    )
```
